32 devices in a mesh: tmpl: 8 (over y, x, core), stn: 4 (over z).
Axes of the slice: x: 2, y: 2, z: 4, core: 2. Of those that a mesh axis runs over, the one named last changes fastest.
Arguments:
- data: bfloat16 [2, 24, 3, 1024], P(None, 'stn', None, 'tmpl'), may hold values from -6 to 6
- waves: bfloat16 [24, 128, 3, 300], P('stn', 'tmpl'), may hold values from -6 to 6
- slot_group: int32 [24, 128, 1], P('stn', 'tmpl'), may hold values from 0 to 7; in each aligned block of 16 rows (0 to 15, 16 to 31, ..., all dimensions but the last counted through in order) at most 4 rows name the same one
- slot_local: int32 [24, 128], P('stn', 'tmpl'), may hold values from 0 to 63
- moveout: int32 [24, 128], P('stn', 'tmpl'), may hold values from 0 to 469
- chan_mask: int32 [24, 3], P('stn'), may hold values 0 or 1
Outputs:
- scores: float32 [2, 512, 256], P(None, ('tmpl', 'stn'))
The draws below stay inside these ranges and needn't reach their ends.
Inputs may be any that keep to these rules, and one draw needn't show every extreme that they name: `slot_group`: among the 16 slots k*16 to (k+1)*16 - 1 of one station, no template group is named more than 4 times.
All inputs are finite; a program needn't handle non-finite values. No bound on the sum of `chan_mask` on one device may be relied on, other than what follows from the above.
Results may differ from the reference program's by a relative error of at most 0.0029.
Values may be sent and summed in bfloat16 or wider, within the bound.
No kernel may reach another device: no remote copies, remote signals or barrier semaphores. Data moves between devices by JAX's collectives and lax.ppermute only.
A program may use at most 128 MiB of HBM per device.

```python
import math
import jax
import jax.numpy as jnp
import numpy as np
from jax import lax

TAPS = 300
COMP = 3
W = 1024
NK = 256
BLOCKS = 2
SLOT_DEV = 16
TPD = 16
MAXSHIFT = 469
MOST = 4
TG = 64
TEMPLATES = 512
STATIONS = 24
SLOTS = 128
N_TMPL = 8
N_STN = 4


def plant(drawn, key, smallest, largest):
    dims = drawn.shape
    spot = [jax.random.randint(jax.random.fold_in(key, axis), (), 0, dims[axis]) for axis in range(len(dims))]
    drawn = drawn.at[tuple(spot)].set(smallest)
    longest = dims.index(max(dims))
    spot[longest] = (spot[longest] + 1) % dims[longest]
    return drawn.at[tuple(spot)].set(largest)


def block_levels(own_key, extent, split, least, high):
    level, own = 1.0, jax.random.fold_in(own_key, 6)
    for position, shards_of in split:
        steps = jnp.exp(jax.random.uniform(jax.random.fold_in(own, position), (shards_of,), jnp.float32, least / len(split), high / len(split)))
        level = level * jnp.repeat(steps, extent[position] // shards_of).reshape([-1 if axis == position else 1 for axis in range(len(extent))])
    return level


def cumulative_ranks(amount, skew):
    portions = [(1 << 20) // math.isqrt(standing ** skew) + 1 for standing in range(1, amount + 1)]
    scale = 1 + sum(portions) // (1 << 30)
    return np.cumsum(np.array([max(1, weight // scale) for weight in portions]))


def skewed_ids(own_key, extent, number_of, slope):
    table = cumulative_ranks(number_of, slope)
    pick = jax.random.randint(jax.random.fold_in(own_key, 1), extent, 0, int(table[number_of - 1]))
    rank = jnp.searchsorted(jnp.asarray(table, jnp.int32), pick, side="right")
    return jax.random.permutation(jax.random.fold_in(own_key, 2), number_of)[rank].astype(jnp.int32)


def assign_block(stream_key, own, number, rows, amount, top, most, slope):
    sequence = jax.random.permutation(stream_key, amount)
    packed, ordinary = portions_of(amount, rows * top, most, slope, True), portions_of(amount, rows * top, most, slope, False)
    places = jnp.arange(amount)

    def named(sizes, offset_by):
        used = int((sizes > 0).sum())
        fixed = max(1, used // 4)
        passed = fixed + (places - fixed + offset_by * (used - fixed)) % max(1, amount - fixed)
        return jnp.zeros((amount,), jnp.int32).at[sequence[jnp.where(places < fixed, places, passed)]].set(jnp.asarray(sizes, jnp.int32))

    sizes = jnp.where(number % 4 == 0, named(packed, number // 4), named(ordinary, number - number // 4 - 1))
    mixed = jax.random.permutation(jax.random.fold_in(own, 3), amount)
    donor, sink = mixed[0:amount // 2 * 2:2], mixed[1:amount // 2 * 2:2]
    room = jnp.minimum(sizes[donor] - 1, most - sizes[sink]) // 2
    room = jnp.where((donor == sequence[0]) | (sink == sequence[0]) | (sizes[sink] == 0), 0, jnp.maximum(room, 0))
    passed = jax.random.randint(jax.random.fold_in(own, 4), (amount // 2,), 0, 1 << 20) % (room + 1)
    sizes = sizes.at[donor].add(-passed).at[sink].add(passed)
    items = jnp.searchsorted(jnp.cumsum(sizes), jnp.arange(rows * top), side="right").astype(jnp.int32)
    table = items.reshape(top, rows).T
    table = table[jax.random.permutation(jax.random.fold_in(own, 1), rows)]
    offset_by = jax.random.randint(jax.random.fold_in(own, 2), (rows, 1), 0, top)
    return jnp.take_along_axis(table, (jnp.arange(top)[None, :] + offset_by) % top, axis=1)


def portions_of(number_of, total, bound, slope, full):
    portions = [(1 << 20) // math.isqrt(rank ** slope) + 1 for rank in range(1, number_of + 1)]
    largest = bound if full else min(bound, max(-(-total // number_of), total * portions[0] // sum(portions)))
    least = 1 if total - largest >= number_of - 1 else 0
    given, rest = [largest] + [least] * (number_of - 1), total - largest - least * (number_of - 1)
    while rest > 0:
        free = [i for i in range(1, number_of) if given[i] < largest] or [i for i in range(1, number_of) if given[i] < bound]
        whole, left = sum([portions[i] for i in free]), rest
        for i in free:
            extra = min(bound - given[i], max(1, left * portions[i] // whole), rest)
            given[i] = given[i] + extra
            rest = rest - extra
    return np.array(given)


def noise(key, shape, deviation, limit, shards=(), held_as=jnp.bfloat16):
    entries = jax.random.normal(key, shape, jnp.float32) * deviation
    if len(shards) > 0:
        entries = block_levels(key, shape, shards, -0.22, 0.18) * entries
    return jnp.clip(entries, min=-limit, max=limit).astype(held_as)


def setup_inputs(seed: int = 0) -> dict:
    splits = jax.random.split(jax.random.key(seed), 7)
    data = noise(splits[0], (BLOCKS, STATIONS, COMP, W), 1.0, 6.0, ((1, 4), (3, 8)))
    waves = noise(splits[1], (STATIONS, SLOTS, COMP, TAPS), 1.0, 6.0, ((0, 4), (1, 8)))
    slot_group_keys = jax.random.split(jax.random.fold_in(splits[2], 1), STATIONS * SLOTS // SLOT_DEV)
    slot_group_turns = jax.random.permutation(jax.random.fold_in(splits[2], 3), STATIONS * SLOTS // SLOT_DEV)
    slot_group = jax.vmap(lambda own, number: assign_block(jax.random.fold_in(splits[2], 2), own, number, SLOT_DEV, N_TMPL, 1, MOST, 2))(slot_group_keys, slot_group_turns).reshape((STATIONS, SLOTS, 1))
    slot_local = plant(skewed_ids(splits[3], (STATIONS, SLOTS), TG, 2), jax.random.fold_in(splits[3], 3), 0, TG - 1).astype(jnp.int32)
    moveout = plant(jax.random.randint(splits[4], (STATIONS, SLOTS), 0, MAXSHIFT + 1), jax.random.fold_in(splits[4], 1), 0, MAXSHIFT).astype(jnp.int32)
    chan_mask = plant((jax.random.randint(splits[5], (STATIONS, COMP), 0, 4) < 3).astype(jnp.int32), jax.random.fold_in(splits[5], 1), 0, 1)
    return {"data": data, "waves": waves, "slot_group": slot_group, "slot_local": slot_local, "moveout": moveout, "chan_mask": chan_mask}


epsilon = 1e-06

def window_rows(series, tap_count, lag_count):
    index_grid = jnp.arange(tap_count)[:, None] + jnp.arange(lag_count)[None, :]
    return series[..., index_grid]

def reference(data, waves, slot_group, slot_local, moveout, chan_mask):
    per_group = TPD * N_STN
    lag_count = W - TAPS + 1

    def station_step(running, inputs):
        stack_sums, counts = running
        station_data, station_waves, group_ids, local_ids, shift_by, station_mask = inputs
        hankel_rows = window_rows(station_data.astype(jnp.float32), TAPS, lag_count)
        data_power = lax.optimization_barrier(jnp.sum(hankel_rows * hankel_rows, axis=2)) / TAPS
        wave_float = station_waves.astype(jnp.float32)
        wave_power = lax.optimization_barrier(jnp.sum(wave_float * wave_float, axis=2)) / TAPS
        numerator = jnp.einsum('pcj,bcjk->pbck', wave_float, hankel_rows)
        denominator = TAPS * jnp.sqrt(wave_power + epsilon)[:, None, :, None] * jnp.sqrt(data_power + epsilon)[None]
        mask_float = station_mask.astype(jnp.float32)
        channel_sum = lax.optimization_barrier(jnp.sum(numerator / denominator * mask_float[None, None, :, None], axis=2))
        correlation = (channel_sum / jnp.maximum(jnp.sum(mask_float), 1.0)).astype(jnp.bfloat16)
        lag_index = shift_by[:, None, None] + jnp.arange(NK)[None, None, :]
        lag_index = jnp.broadcast_to(lag_index, (SLOTS, BLOCKS, NK))
        shifted = jnp.take_along_axis(correlation, lag_index, axis=2).astype(jnp.float32)
        template_ids = group_ids[:, 0] * per_group + local_ids
        stack_sums = stack_sums.at[template_ids].add(shifted)
        counts = counts.at[template_ids].add(jnp.ones((SLOTS,), jnp.float32))
        return ((stack_sums, counts), None)
    initial = (jnp.zeros((TEMPLATES, BLOCKS, NK), jnp.float32), jnp.zeros((TEMPLATES,), jnp.float32))
    (stack_sums, counts), ignored = lax.scan(station_step, initial, (jnp.moveaxis(data, 1, 0), waves, slot_group, slot_local, moveout, chan_mask))
    scores = jnp.sqrt(jnp.float32(TAPS)) * stack_sums / jnp.sqrt(jnp.maximum(counts, 1.0))[:, None, None]
    return jnp.moveaxis(scores, 0, 1)
```

```python
import functools

import jax
import jax.numpy as jnp
from jax import lax
from jax.experimental import pallas as pl
from jax.experimental.pallas import tpu as pltpu
from jax.sharding import PartitionSpec as P

NK = 256
TPD = 16
LANES = 128
SHIFTS = 16

epsilon = 1e-06


def ceil_to(value, multiple):
    return -(-value // multiple) * multiple


def column_of(row):
    n = row.shape[1]
    eye = lax.broadcasted_iota(jnp.int32, (n, n), 0) == lax.broadcasted_iota(jnp.int32, (n, n), 1)
    return jnp.sum(jnp.where(eye, jnp.broadcast_to(row, (n, n)), 0), axis=1, keepdims=True)


def chunk_plan(taps, components):
    whole = taps // LANES
    tail = taps - whole * LANES
    per_tail = (LANES - 3) // tail
    return whole, tail, per_tail, ceil_to(components, per_tail) // per_tail


def pack_kernel(dims, with_data, *refs):
    ins = refs[: 5 if with_data else 4]
    send_ref = refs[len(ins)]
    held = refs[len(ins) + 1 : 2 * len(ins) + 1]
    sems = refs[-1]
    copies = [pltpu.make_async_copy(ins[i], held[i], sems.at[i]) for i in range(len(ins))]
    for copy in copies:
        copy.start()
    waves_ref, group_ref, local_ref, moveout_ref = held[-4:]
    n, stations, slots, components, taps, most, rows = dims
    count = stations * slots
    whole, tail, per_tail, tails = chunk_plan(taps, components)

    def flat(ref, three):
        pieces = [ref[s] if three else ref[s : s + 1, :] for s in range(stations)]
        return jnp.concatenate(pieces, axis=1)

    for copy in copies[-3:]:
        copy.wait()
    group = flat(group_ref, True)
    local = flat(local_ref, False)
    moveout = flat(moveout_ref, False)
    group_col = column_of(group)
    upper = lax.broadcasted_iota(jnp.int32, (count, count), 0)
    lower = lax.broadcasted_iota(jnp.int32, (count, count), 1)
    same = (upper // slots == lower // slots) & (upper < lower)
    rank = jnp.sum(jnp.where(same & (group_col == group), 1, 0), axis=0, keepdims=True)
    station = lax.broadcasted_iota(jnp.int32, (1, count), 1) // slots
    position = group * rows + station * most + rank
    place = lax.broadcasted_iota(jnp.int32, (n * rows, count), 0) == position
    place = jnp.where(place, 1.0, 0.0).astype(jnp.bfloat16)

    lane = lax.broadcasted_iota(jnp.int32, (count, LANES), 1)
    meta = jnp.where(lane == LANES - 1, column_of(local) + 1, 0)
    meta = jnp.where(lane == LANES - 2, column_of(moveout // LANES), meta)
    meta = jnp.where(lane == LANES - 3, column_of(moveout % LANES), meta)
    meta = meta.astype(jnp.float32).astype(jnp.bfloat16)

    for copy in copies[:-3]:
        copy.wait()
    waves = [
        jnp.concatenate([waves_ref[s * components + c] for s in range(stations)], axis=0)
        for c in range(components)
    ]
    placed = [
        jnp.dot(place, waves[c][:, : whole * LANES], preferred_element_type=jnp.float32)
        for c in range(components)
    ]
    ends = []
    for e in range(tails):
        pieces = [waves[c][:, whole * LANES :] for c in range(e * per_tail, min((e + 1) * per_tail, components))]
        used = tail * len(pieces)
        pieces.append(
            meta[:, used:] if e == 0 else jnp.zeros((count, LANES - used), jnp.bfloat16)
        )
        ends.append(jnp.concatenate(pieces, axis=1))
    ends = jnp.dot(place, jnp.concatenate(ends, axis=1), preferred_element_type=jnp.float32)
    if with_data:
        samples = held[0][...].astype(jnp.float32)
        samples = samples.reshape(samples.shape[0] * samples.shape[1], LANES)
        extra = send_ref.shape[1] - (components * whole + tails) * rows - samples.shape[0]
        samples = jnp.concatenate([samples, jnp.zeros((extra, LANES), jnp.float32)], axis=0)
    for g in range(n):
        mine = slice(g * rows, (g + 1) * rows)
        pieces = [
            placed[c][mine, a * LANES : (a + 1) * LANES] for c in range(components) for a in range(whole)
        ]
        pieces += [ends[mine, e * LANES : (e + 1) * LANES] for e in range(tails)]
        if with_data:
            pieces.append(samples)
        send_ref[g] = jnp.concatenate(pieces, axis=0).astype(jnp.bfloat16)


def correlate_kernel(dims, with_data, *refs):
    if with_data:
        recv_ref, mask_ref, *refs = refs
    else:
        recv_ref, data_ref, mask_ref, *refs = refs
    *out_refs, dsh_ref, rd_ref, ws_ref, rw_ref, meta_ref, sh_ref, stack_ref = refs
    n, stations, blocks, components, taps, most, rows, width, per_group = dims
    whole, tail, per_tail, tails = chunk_plan(taps, components)
    chunks = whole + 1
    sent = components * whole + tails
    total = n * rows
    here = n * most
    lag_tiles = ceil_to(width - taps + 1, LANES) // LANES
    lag_width = lag_tiles * LANES
    series = stations * components * blocks
    series_rows = ceil_to(series, 8)

    if with_data:
        first = sent * rows
        x = [recv_ref[i, first:, :].astype(jnp.float32)[:series_rows] for i in range(n)]
        x = jnp.concatenate(x, axis=1)
    else:
        x = data_ref[...].astype(jnp.float32)
        x = jnp.concatenate([x, jnp.zeros((series_rows - series, width), jnp.float32)], axis=0)
    for r in range(SHIFTS):
        moved = pltpu.roll(x, width - r, 1) if r else x
        for t in range(width // LANES):
            dsh_ref[t, r * series_rows : (r + 1) * series_rows, :] = moved[:, t * LANES : (t + 1) * LANES]

    def ahead(values, by):
        return pltpu.roll(values, width - by, 1)

    sums = {1: x * x}
    size = 1
    while 2 * size <= taps:
        sums[2 * size] = sums[size] + ahead(sums[size], size)
        size = 2 * size
    power = sums[size]
    start = size
    while start < taps:
        size = size // 2
        if taps - start >= size:
            power = power + ahead(sums[size], start)
            start += size
    scale = lax.rsqrt(power / taps + epsilon)
    row = lax.broadcasted_iota(jnp.int32, (series_rows, LANES), 0)
    factor = jnp.zeros((series_rows, LANES), jnp.float32)
    for s in range(stations):
        used = [mask_ref[s, c] for c in range(components)]
        total_used = jnp.maximum(functools.reduce(lambda p, q: p + q, used), 1)
        for c in range(components):
            at = (s * components + c) * blocks
            mine = (row >= at) & (row < at + blocks)
            value = jnp.full((series_rows, LANES), used[c]).astype(jnp.float32)
            value = value / jnp.full((series_rows, LANES), total_used).astype(jnp.float32)
            factor = jnp.where(mine, value, factor)
    for t in range(lag_tiles):
        rd_ref[:, t * LANES : (t + 1) * LANES] = scale[:, t * LANES : (t + 1) * LANES] * factor

    target = lax.broadcasted_iota(jnp.int32, (stations * here, total), 0)
    source = lax.broadcasted_iota(jnp.int32, (stations * here, total), 1)
    wanted = (target % here // most) * rows + (target // here) * most + target % most
    order = jnp.where(source == wanted, 1.0, 0.0).astype(jnp.bfloat16)
    lane = lax.broadcasted_iota(jnp.int32, (stations * here, LANES), 1)
    blocks_in = [recv_ref[i, : ceil_to(sent * rows, 16), :].astype(jnp.float32) for i in range(n)]

    def received(k):
        piece = jnp.concatenate([blocks_in[i][k * rows : (k + 1) * rows] for i in range(n)], axis=0)
        return jnp.dot(order, piece.astype(jnp.bfloat16), preferred_element_type=jnp.float32)

    ends = [received(components * whole + e) for e in range(tails)]
    meta_ref[...] = ends[0]
    for c in range(components):
        pieces = [received(c * whole + a) for a in range(whole)]
        end, before = ends[c // per_tail], (c % per_tail) * tail
        end = pltpu.roll(end, LANES - before, 1) if before else end
        pieces.append(jnp.where(lane < tail, end, 0.0))
        squares = functools.reduce(lambda p, q: p + q, [piece * piece for piece in pieces])
        for a in range(chunks):
            at = (c * chunks + a) * LANES
            ws_ref[:, at : at + LANES] = pieces[a].astype(jnp.bfloat16)
        wave_power = jnp.sum(squares, axis=1, keepdims=True) / taps
        rw_ref[:, c * LANES : (c + 1) * LANES] = jnp.broadcast_to(
            lax.rsqrt(wave_power + epsilon) / taps, (stations * here, LANES)
        )

    depth = (chunks - 1) * LANES + ceil_to(tail, 16)
    lane_here = lax.broadcasted_iota(jnp.int32, (here, LANES), 1)

    @pl.loop(0, stations)
    def _(s):
        rows_here = pl.ds(pl.multiple_of(s * here, here), here)
        meta = meta_ref[rows_here, :]
        tiles_over = meta[:, LANES - 2 : LANES - 1].astype(jnp.int32)
        lanes_over = meta[:, LANES - 3 : LANES - 2].astype(jnp.int32)
        index = lane_here + lanes_over
        within = index < LANES
        index = jnp.bitwise_and(index, LANES - 1)
        for b in range(blocks):
            total_corr = [jnp.zeros((here, LANES), jnp.float32) for _ in range(lag_tiles)]
            for c in range(components):
                at = (s * components + c) * blocks + b
                low = [
                    dsh_ref[t, pl.ds(at, SHIFTS, stride=series_rows), :] for t in range(width // LANES)
                ]
                low = jnp.concatenate(low, axis=1).astype(jnp.bfloat16)
                pieces = [low] + [pltpu.roll(low, width - q, 1) for q in range(SHIFTS, LANES, SHIFTS)]
                shifted = jnp.concatenate(pieces, axis=0)
                hankel = jnp.concatenate(
                    [
                        shifted[: min(LANES, depth - a * LANES), a * LANES : a * LANES + lag_width]
                        for a in range(chunks)
                    ],
                    axis=0,
                )
                w = ws_ref[rows_here, c * chunks * LANES : c * chunks * LANES + depth]
                numerator = jnp.dot(w, hankel, preferred_element_type=jnp.float32)
                over_wave = rw_ref[rows_here, c * LANES : (c + 1) * LANES]
                over_data = rd_ref[pl.ds(at, 1), :]
                for t in range(lag_tiles):
                    cut = slice(t * LANES, (t + 1) * LANES)
                    total_corr[t] = total_corr[t] + numerator[:, cut] * over_wave * over_data[:, cut]
            windows = []
            for t in range(NK // LANES + 1):
                window = total_corr[t]
                for h in range(1, lag_tiles - NK // LANES):
                    if t + h < lag_tiles:
                        window = jnp.where(tiles_over == h, total_corr[t + h], window)
                windows.append(jnp.take_along_axis(window, index, axis=1))
            for t in range(NK // LANES):
                aligned = jnp.where(within, windows[t], windows[t + 1])
                at = b * NK + t * LANES
                sh_ref[rows_here, at : at + LANES] = aligned.astype(jnp.bfloat16)

    slot = lax.broadcasted_iota(jnp.int32, (stations * here, LANES), 0)
    half = (slot < stations * here // 2) == (lane < LANES // 2)
    sh_ref[:, blocks * NK :] = jnp.where(half, 1.0, 0.0).astype(jnp.bfloat16)
    local = meta_ref[:, LANES - 1 :].astype(jnp.int32) - 1
    template = lax.broadcasted_iota(jnp.int32, (stations * here, per_group), 1)
    onehot = jnp.where(local == template, 1.0, 0.0).astype(jnp.bfloat16)
    stack_ref[...] = lax.dot_general(
        onehot, sh_ref[...], (((0,), (0,)), ((), ())), preferred_element_type=jnp.float32
    )
    me = lax.axis_index("stn")
    for d, out_ref in enumerate(out_refs):
        owner = lax.rem(me + d, len(out_refs))
        theirs = pl.ds(pl.multiple_of(owner * TPD, TPD), TPD)
        out_ref[...] = stack_ref[theirs, :].astype(jnp.bfloat16)


def finish_kernel(taps, blocks, *refs):
    *parts_refs, out_ref = refs
    total = functools.reduce(lambda p, q: p + q, [ref[...].astype(jnp.float32) for ref in parts_refs])
    first, middle = blocks * NK, blocks * NK + LANES // 2
    count = total[:, first : first + 1] + total[:, middle : middle + 1]
    scale = jnp.sqrt(jnp.float32(taps)) / jnp.sqrt(jnp.maximum(count, 1.0))
    for b in range(blocks):
        out_ref[b] = total[:, b * NK : (b + 1) * NK] * scale


def body(data, waves, slot_group, slot_local, moveout, chan_mask):
    blocks, stations, components, width_here = data.shape
    slots, taps = waves.shape[1], waves.shape[3]
    n = lax.axis_size("tmpl")
    owners = lax.axis_size("stn")
    per_group = TPD * owners
    width = width_here * n
    most = max(2, 2 * slots // n)
    rows = ceil_to(stations * most, 8)
    whole, tail, per_tail, tails = chunk_plan(taps, components)
    series = stations * components * blocks
    series_rows = ceil_to(series, 8)
    with_data = width_here == LANES
    here = n * most

    waves = jnp.transpose(waves, (0, 2, 1, 3)).reshape(stations * components, slots, taps)
    groups = jnp.transpose(slot_group, (0, 2, 1))
    samples = jnp.transpose(data, (1, 2, 0, 3)).reshape(stations * components, blocks, width_here)
    block_rows = (components * whole + tails) * rows + (series_rows if with_data else 0)
    block_rows = ceil_to(block_rows, 16)
    ins = ([samples] if with_data else []) + [waves, groups, slot_local, moveout]
    send = pl.pallas_call(
        functools.partial(
            pack_kernel, (n, stations, slots, components, taps, most, rows), with_data
        ),
        out_shape=jax.ShapeDtypeStruct((n, block_rows, LANES), jnp.bfloat16),
        in_specs=[pl.BlockSpec(memory_space=pltpu.HBM)] * len(ins),
        scratch_shapes=[pltpu.VMEM(x.shape, x.dtype) for x in ins]
        + [pltpu.SemaphoreType.DMA((len(ins),))],
        compiler_params=pltpu.CompilerParams(vmem_limit_bytes=60 << 20),
        name="pack",
    )(*ins)
    received = lax.all_to_all(send, "tmpl", split_axis=0, concat_axis=0, tiled=True)
    if not with_data:
        samples = lax.all_gather(samples.reshape(series, width_here), "tmpl", axis=1, tiled=True)
    vmem = pl.BlockSpec(memory_space=pltpu.VMEM)
    partial_stacks = pl.pallas_call(
        functools.partial(
            correlate_kernel,
            (n, stations, blocks, components, taps, most, rows, width, per_group),
            with_data,
        ),
        out_shape=[jax.ShapeDtypeStruct((TPD, blocks * NK + LANES), jnp.bfloat16)] * owners,
        in_specs=[vmem] * (1 if with_data else 2) + [pl.BlockSpec(memory_space=pltpu.SMEM)],
        scratch_shapes=[
            pltpu.VMEM((width // LANES, SHIFTS * series_rows, LANES), jnp.float32),
            pltpu.VMEM((series_rows, ceil_to(width - taps + 1, LANES)), jnp.float32),
            pltpu.VMEM((stations * here, components * (whole + 1) * LANES), jnp.bfloat16),
            pltpu.VMEM((stations * here, components * LANES), jnp.float32),
            pltpu.VMEM((stations * here, LANES), jnp.float32),
            pltpu.VMEM((stations * here, blocks * NK + LANES), jnp.bfloat16),
            pltpu.VMEM((per_group, blocks * NK + LANES), jnp.float32),
        ],
        compiler_params=pltpu.CompilerParams(vmem_limit_bytes=40 << 20),
        name="correlate",
    )(received, *([] if with_data else [samples]), chan_mask)
    parts = [partial_stacks[0]]
    for d in range(1, owners):
        step = [(i, (i + d) % owners) for i in range(owners)]
        parts.append(lax.ppermute(partial_stacks[d], "stn", step))
    return pl.pallas_call(
        functools.partial(finish_kernel, taps, blocks),
        out_shape=jax.ShapeDtypeStruct((blocks, TPD, NK), jnp.float32),
        name="finish",
    )(*parts)


def solution(mesh):
    in_specs = (
        P(None, "stn", None, "tmpl"),
        P("stn", "tmpl", None, None),
        P("stn", "tmpl", None),
        P("stn", "tmpl"),
        P("stn", "tmpl"),
        P("stn", None),
    )
    out_specs = P(None, ("tmpl", "stn"), None)
    return jax.shard_map(body, mesh=mesh, in_specs=in_specs, out_specs=out_specs, check_vma=False)
```

```python
import functools

import jax
import jax.numpy as jnp
from jax import lax
from jax.experimental import pallas as pl
from jax.experimental.pallas import tpu as pltpu
from jax.sharding import PartitionSpec as P

NK = 256
TPD = 16
LANES = 128
SHIFTS = 16

epsilon = 1e-06


def ceil_to(value, multiple):
    return -(-value // multiple) * multiple


def column_of(row):
    n = row.shape[1]
    eye = lax.broadcasted_iota(jnp.int32, (n, n), 0) == lax.broadcasted_iota(jnp.int32, (n, n), 1)
    return jnp.sum(jnp.where(eye, jnp.broadcast_to(row, (n, n)), 0), axis=1, keepdims=True)


def chunk_plan(taps, components):
    whole = taps // LANES
    tail = taps - whole * LANES
    per_tail = (LANES - 3) // tail
    return whole, tail, per_tail, ceil_to(components, per_tail) // per_tail


def pack_kernel(dims, with_data, *refs):
    n, stations, slots, components, taps, most, rows = dims
    ins = refs[: 5 if with_data else 4]
    send_refs = refs[len(ins) : len(ins) + n]
    held = refs[len(ins) + n : -1]
    sems = refs[-1]
    copies = [pltpu.make_async_copy(ins[i], held[i], sems.at[i]) for i in range(len(ins))]
    for copy in copies:
        copy.start()
    waves_ref, group_ref, local_ref, moveout_ref = held[-4:]
    count = stations * slots
    whole, tail, per_tail, tails = chunk_plan(taps, components)

    def flat(ref, three):
        pieces = [ref[s] if three else ref[s : s + 1, :] for s in range(stations)]
        return jnp.concatenate(pieces, axis=1)

    for copy in copies[-3:]:
        copy.wait()
    group = flat(group_ref, True)
    local = flat(local_ref, False)
    moveout = flat(moveout_ref, False)
    group_col = column_of(group)
    upper = lax.broadcasted_iota(jnp.int32, (count, count), 0)
    lower = lax.broadcasted_iota(jnp.int32, (count, count), 1)
    same = (upper // slots == lower // slots) & (upper < lower)
    rank = jnp.sum(jnp.where(same & (group_col == group), 1, 0), axis=0, keepdims=True)
    station = lax.broadcasted_iota(jnp.int32, (1, count), 1) // slots
    partner = group ^ lax.axis_index("tmpl")
    position = partner * rows + station * most + rank
    place = lax.broadcasted_iota(jnp.int32, (n * rows, count), 0) == position
    place = jnp.where(place, 1.0, 0.0).astype(jnp.bfloat16)

    lane = lax.broadcasted_iota(jnp.int32, (count, LANES), 1)
    meta = jnp.where(lane == LANES - 1, column_of(local) + 1, 0)
    meta = jnp.where(lane == LANES - 2, column_of(moveout // LANES), meta)
    meta = jnp.where(lane == LANES - 3, column_of(moveout % LANES), meta)
    meta = meta.astype(jnp.float32).astype(jnp.bfloat16)

    for copy in copies[:-3]:
        copy.wait()
    waves = [
        jnp.concatenate([waves_ref[s * components + c] for s in range(stations)], axis=0)
        for c in range(components)
    ]
    placed = [
        jnp.dot(place, waves[c][:, : whole * LANES], preferred_element_type=jnp.float32)
        for c in range(components)
    ]
    ends = []
    for e in range(tails):
        pieces = [waves[c][:, whole * LANES :] for c in range(e * per_tail, min((e + 1) * per_tail, components))]
        used = tail * len(pieces)
        pieces.append(
            meta[:, used:] if e == 0 else jnp.zeros((count, LANES - used), jnp.bfloat16)
        )
        ends.append(jnp.concatenate(pieces, axis=1))
    ends = jnp.dot(place, jnp.concatenate(ends, axis=1), preferred_element_type=jnp.float32)
    if with_data:
        samples = held[0][...].astype(jnp.float32)
        samples = samples.reshape(samples.shape[0] * samples.shape[1], LANES)
        extra = send_refs[0].shape[0] - (components * whole + tails) * rows - samples.shape[0]
        samples = jnp.concatenate([samples, jnp.zeros((extra, LANES), jnp.float32)], axis=0)
    for g in range(n):
        mine = slice(g * rows, (g + 1) * rows)
        pieces = [
            placed[c][mine, a * LANES : (a + 1) * LANES] for c in range(components) for a in range(whole)
        ]
        pieces += [ends[mine, e * LANES : (e + 1) * LANES] for e in range(tails)]
        if with_data:
            pieces.append(samples)
        send_refs[g][...] = jnp.concatenate(pieces, axis=0).astype(jnp.bfloat16)


def correlate_kernel(dims, with_data, *refs):
    if with_data:
        mask_ref, *refs = refs
    else:
        data_ref, mask_ref, *refs = refs
    n, stations, blocks, components, taps, most, rows, width, per_group = dims
    recv_refs, refs = refs[:n], refs[n:]
    *out_refs, x_ref, dsh_ref, rd_ref, ws_ref, rw_ref, meta_ref, sh_ref, stack_ref = refs
    whole, tail, per_tail, tails = chunk_plan(taps, components)
    chunks = whole + 1
    sent = components * whole + tails
    total = n * rows
    here = n * most
    lag_tiles = ceil_to(width - taps + 1, LANES) // LANES
    series = stations * components * blocks
    series_rows = ceil_to(series, 8)

    if with_data:
        first = sent * rows
        for i in range(n):
            x_ref[lax.axis_index("tmpl") ^ i] = recv_refs[i][first:, :].astype(jnp.float32)[:series_rows]
        x = jnp.concatenate([x_ref[i] for i in range(n)], axis=1)
    else:
        x = data_ref[...].astype(jnp.float32)
        x = jnp.concatenate([x, jnp.zeros((series_rows - series, width), jnp.float32)], axis=0)
    for r in range(SHIFTS):
        moved = pltpu.roll(x, width - r, 1) if r else x
        for t in range(width // LANES):
            dsh_ref[t, r * series_rows : (r + 1) * series_rows, :] = moved[:, t * LANES : (t + 1) * LANES]

    def ahead(values, by):
        return pltpu.roll(values, width - by, 1)

    sums = {1: x * x}
    size = 1
    while 2 * size <= taps:
        sums[2 * size] = sums[size] + ahead(sums[size], size)
        size = 2 * size
    power = sums[size]
    start = size
    while start < taps:
        size = size // 2
        if taps - start >= size:
            power = power + ahead(sums[size], start)
            start += size
    scale = lax.rsqrt(power / taps + epsilon)
    row = lax.broadcasted_iota(jnp.int32, (series_rows, LANES), 0)
    factor = jnp.zeros((series_rows, LANES), jnp.float32)
    for s in range(stations):
        used = [mask_ref[s, c] for c in range(components)]
        total_used = jnp.maximum(functools.reduce(lambda p, q: p + q, used), 1)
        for c in range(components):
            at = (s * components + c) * blocks
            mine = (row >= at) & (row < at + blocks)
            value = jnp.full((series_rows, LANES), used[c]).astype(jnp.float32)
            value = value / jnp.full((series_rows, LANES), total_used).astype(jnp.float32)
            factor = jnp.where(mine, value, factor)
    for t in range(lag_tiles):
        rd_ref[:, t * LANES : (t + 1) * LANES] = scale[:, t * LANES : (t + 1) * LANES] * factor

    target = lax.broadcasted_iota(jnp.int32, (stations * here, total), 0)
    source = lax.broadcasted_iota(jnp.int32, (stations * here, total), 1)
    wanted = (target % here // most) * rows + (target // here) * most + target % most
    order = jnp.where(source == wanted, 1.0, 0.0).astype(jnp.bfloat16)
    lane = lax.broadcasted_iota(jnp.int32, (stations * here, LANES), 1)
    blocks_in = [ref[: ceil_to(sent * rows, 16), :].astype(jnp.float32) for ref in recv_refs]

    def received(k):
        piece = jnp.concatenate([blocks_in[i][k * rows : (k + 1) * rows] for i in range(n)], axis=0)
        return jnp.dot(order, piece.astype(jnp.bfloat16), preferred_element_type=jnp.float32)

    ends = [received(components * whole + e) for e in range(tails)]
    meta_ref[...] = ends[0]
    for c in range(components):
        pieces = [received(c * whole + a) for a in range(whole)]
        end, before = ends[c // per_tail], (c % per_tail) * tail
        end = pltpu.roll(end, LANES - before, 1) if before else end
        pieces.append(jnp.where(lane < tail, end, 0.0))
        squares = functools.reduce(lambda p, q: p + q, [piece * piece for piece in pieces])
        for a in range(chunks):
            for s in range(stations):
                at = ((s * components + c) * chunks + a) * here
                ws_ref[at : at + here, :] = pieces[a][s * here : (s + 1) * here].astype(jnp.bfloat16)
        wave_power = jnp.sum(squares, axis=1, keepdims=True) / taps
        rw_ref[:, c * LANES : (c + 1) * LANES] = jnp.broadcast_to(
            lax.rsqrt(wave_power + epsilon) / taps, (stations * here, LANES)
        )

    lane_here = lax.broadcasted_iota(jnp.int32, (here, LANES), 1)

    for s in range(stations):
        rows_here = slice(s * here, (s + 1) * here)
        meta = meta_ref[rows_here, :]
        tiles_over = meta[:, LANES - 2 : LANES - 1].astype(jnp.int32)
        lanes_over = meta[:, LANES - 3 : LANES - 2].astype(jnp.int32)
        index = lane_here + lanes_over
        within = index < LANES
        index = jnp.bitwise_and(index, LANES - 1)
        for b in range(blocks):
            total_corr = [jnp.zeros((here, LANES), jnp.float32) for _ in range(lag_tiles)]
            for c in range(components):
                at = (s * components + c) * blocks + b
                low = [
                    dsh_ref[t, pl.ds(at, SHIFTS, stride=series_rows), :] for t in range(width // LANES)
                ]
                low = jnp.concatenate(low, axis=1).astype(jnp.bfloat16)
                pieces = [low] + [pltpu.roll(low, width - q, 1) for q in range(SHIFTS, LANES, SHIFTS)]
                shifted = jnp.concatenate(pieces, axis=0)
                first = (s * components + c) * chunks * here
                w = ws_ref[first : first + chunks * here, :]
                numerator = jnp.dot(w, shifted, preferred_element_type=jnp.float32)
                over_wave = rw_ref[rows_here, c * LANES : (c + 1) * LANES]
                over_data = rd_ref[at : at + 1, :]
                for t in range(lag_tiles):
                    pieces = [
                        numerator[a * here : (a + 1) * here, (t + a) * LANES : (t + a + 1) * LANES]
                        for a in range(chunks)
                    ]
                    summed = functools.reduce(lambda p, q: p + q, pieces)
                    over = over_data[:, t * LANES : (t + 1) * LANES]
                    total_corr[t] = total_corr[t] + summed * over_wave * over
            windows = []
            for t in range(NK // LANES + 1):
                window = total_corr[t]
                for h in range(1, lag_tiles - NK // LANES):
                    if t + h < lag_tiles:
                        window = jnp.where(tiles_over == h, total_corr[t + h], window)
                windows.append(jnp.take_along_axis(window, index, axis=1))
            for t in range(NK // LANES):
                aligned = jnp.where(within, windows[t], windows[t + 1])
                at = b * NK + t * LANES
                sh_ref[rows_here, at : at + LANES] = aligned.astype(jnp.bfloat16)

    slot = lax.broadcasted_iota(jnp.int32, (stations * here, LANES), 0)
    half = (slot < stations * here // 2) == (lane < LANES // 2)
    sh_ref[:, blocks * NK :] = jnp.where(half, 1.0, 0.0).astype(jnp.bfloat16)
    local = meta_ref[:, LANES - 1 :].astype(jnp.int32) - 1
    template = lax.broadcasted_iota(jnp.int32, (stations * here, per_group), 1)
    onehot = jnp.where(local == template, 1.0, 0.0).astype(jnp.bfloat16)
    stack_ref[...] = lax.dot_general(
        onehot, sh_ref[...], (((0,), (0,)), ((), ())), preferred_element_type=jnp.float32
    )
    me = lax.axis_index("stn")
    for d, out_ref in enumerate(out_refs):
        owner = lax.rem(me + d, len(out_refs))
        theirs = pl.ds(pl.multiple_of(owner * TPD, TPD), TPD)
        out_ref[...] = stack_ref[theirs, :].astype(jnp.bfloat16)


def finish_kernel(taps, blocks, *refs):
    *parts_refs, out_ref = refs
    total = functools.reduce(lambda p, q: p + q, [ref[...].astype(jnp.float32) for ref in parts_refs])
    first, middle = blocks * NK, blocks * NK + LANES // 2
    count = total[:, first : first + 1] + total[:, middle : middle + 1]
    scale = jnp.sqrt(jnp.float32(taps)) / jnp.sqrt(jnp.maximum(count, 1.0))
    for b in range(blocks):
        out_ref[b] = total[:, b * NK : (b + 1) * NK] * scale


def body(data, waves, slot_group, slot_local, moveout, chan_mask):
    blocks, stations, components, width_here = data.shape
    slots, taps = waves.shape[1], waves.shape[3]
    n = lax.axis_size("tmpl")
    owners = lax.axis_size("stn")
    per_group = TPD * owners
    width = width_here * n
    most = max(2, 2 * slots // n)
    rows = ceil_to(stations * most, 8)
    whole, tail, per_tail, tails = chunk_plan(taps, components)
    series = stations * components * blocks
    series_rows = ceil_to(series, 8)
    with_data = width_here == LANES
    here = n * most

    waves = jnp.transpose(waves, (0, 2, 1, 3)).reshape(stations * components, slots, taps)
    groups = jnp.transpose(slot_group, (0, 2, 1))
    samples = jnp.transpose(data, (1, 2, 0, 3)).reshape(stations * components, blocks, width_here)
    block_rows = (components * whole + tails) * rows + (series_rows if with_data else 0)
    block_rows = ceil_to(block_rows, 16)
    ins = ([samples] if with_data else []) + [waves, groups, slot_local, moveout]
    send = pl.pallas_call(
        functools.partial(
            pack_kernel, (n, stations, slots, components, taps, most, rows), with_data
        ),
        out_shape=[jax.ShapeDtypeStruct((block_rows, LANES), jnp.bfloat16)] * n,
        in_specs=[pl.BlockSpec(memory_space=pltpu.HBM)] * len(ins),
        scratch_shapes=[pltpu.VMEM(x.shape, x.dtype) for x in ins]
        + [pltpu.SemaphoreType.DMA((len(ins),))],
        compiler_params=pltpu.CompilerParams(vmem_limit_bytes=60 << 20),
        name="pack",
    )(*ins)
    received = [send[0]] + [None] * (n - 1)
    for d in range(n - 1, 0, -1):
        received[d] = lax.ppermute(send[d], "tmpl", [(i, i ^ d) for i in range(n)])
    if not with_data:
        samples = lax.all_gather(samples.reshape(series, width_here), "tmpl", axis=1, tiled=True)
    vmem = pl.BlockSpec(memory_space=pltpu.VMEM)
    partial_stacks = pl.pallas_call(
        functools.partial(
            correlate_kernel,
            (n, stations, blocks, components, taps, most, rows, width, per_group),
            with_data,
        ),
        out_shape=[jax.ShapeDtypeStruct((TPD, blocks * NK + LANES), jnp.bfloat16)] * owners,
        in_specs=[vmem] * (0 if with_data else 1) + [pl.BlockSpec(memory_space=pltpu.SMEM)] + [vmem] * n,
        scratch_shapes=[
            pltpu.VMEM((width // LANES, series_rows, LANES), jnp.float32),
            pltpu.VMEM((width // LANES, SHIFTS * series_rows, LANES), jnp.float32),
            pltpu.VMEM((series_rows, ceil_to(width - taps + 1, LANES)), jnp.float32),
            pltpu.VMEM((stations * components * (whole + 1) * here, LANES), jnp.bfloat16),
            pltpu.VMEM((stations * here, components * LANES), jnp.float32),
            pltpu.VMEM((stations * here, LANES), jnp.float32),
            pltpu.VMEM((stations * here, blocks * NK + LANES), jnp.bfloat16),
            pltpu.VMEM((per_group, blocks * NK + LANES), jnp.float32),
        ],
        compiler_params=pltpu.CompilerParams(vmem_limit_bytes=40 << 20),
        name="correlate",
    )(*([] if with_data else [samples]), chan_mask, *received)
    parts = [partial_stacks[0]]
    for d in range(1, owners):
        step = [(i, (i + d) % owners) for i in range(owners)]
        parts.append(lax.ppermute(partial_stacks[d], "stn", step))
    return pl.pallas_call(
        functools.partial(finish_kernel, taps, blocks),
        out_shape=jax.ShapeDtypeStruct((blocks, TPD, NK), jnp.float32),
        compiler_params=pltpu.CompilerParams(vmem_limit_bytes=4 << 20),
        name="finish",
    )(*parts)


def solution(mesh):
    in_specs = (
        P(None, "stn", None, "tmpl"),
        P("stn", "tmpl", None, None),
        P("stn", "tmpl", None),
        P("stn", "tmpl"),
        P("stn", "tmpl"),
        P("stn", None),
    )
    out_specs = P(None, ("tmpl", "stn"), None)
    return jax.shard_map(body, mesh=mesh, in_specs=in_specs, out_specs=out_specs, check_vma=False)
```

```python
import functools

import jax
import jax.numpy as jnp
from jax import lax
from jax.experimental import pallas as pl
from jax.experimental.pallas import tpu as pltpu
from jax.sharding import PartitionSpec as P

NK = 256
TPD = 16
LANES = 128
SHIFTS = 16

epsilon = 1e-06


def ceil_to(value, multiple):
    return -(-value // multiple) * multiple


def quotient(values, divisor):
    if divisor & (divisor - 1):
        return values // divisor
    return lax.shift_right_logical(values, divisor.bit_length() - 1)


def remainder(values, divisor):
    if divisor & (divisor - 1):
        return values % divisor
    return values & (divisor - 1)


def partners(n):
    return [0] + list(range(n - 1, 0, -1))


def column_of(row):
    n = row.shape[1]
    eye = lax.broadcasted_iota(jnp.int32, (n, n), 0) == lax.broadcasted_iota(jnp.int32, (n, n), 1)
    return jnp.sum(jnp.where(eye, jnp.broadcast_to(row, (n, n)), 0), axis=1, keepdims=True)


def chunk_plan(taps, components):
    whole = taps // LANES
    tail = taps - whole * LANES
    per_tail = (LANES - 3) // tail
    return whole, tail, per_tail, ceil_to(components, per_tail) // per_tail


def pack_kernel(dims, with_data, *refs):
    n, stations, slots, components, taps, most, rows = dims
    ins = refs[: 5 if with_data else 4]
    send_refs = refs[len(ins) : len(ins) + n]
    held = refs[len(ins) + n : -1]
    sems = refs[-1]
    copies = [pltpu.make_async_copy(ins[i], held[i], sems.at[i]) for i in range(len(ins))]
    for copy in copies:
        copy.start()
    waves_ref, group_ref, local_ref, moveout_ref = held[-4:]
    count = stations * slots
    whole, tail, per_tail, tails = chunk_plan(taps, components)

    def flat(ref, three):
        pieces = [ref[s] if three else ref[s : s + 1, :] for s in range(stations)]
        return jnp.concatenate(pieces, axis=1)

    for copy in copies[-3:]:
        copy.wait()
    group = flat(group_ref, True)
    local = flat(local_ref, False)
    moveout = flat(moveout_ref, False)
    group_col = column_of(group)
    upper = lax.broadcasted_iota(jnp.int32, (count, count), 0)
    lower = lax.broadcasted_iota(jnp.int32, (count, count), 1)
    same = (quotient(upper, slots) == quotient(lower, slots)) & (upper < lower)
    rank = jnp.sum(jnp.where(same & (group_col == group), 1, 0), axis=0, keepdims=True)
    station = quotient(lax.broadcasted_iota(jnp.int32, (1, count), 1), slots)
    partner = group ^ lax.axis_index("tmpl")
    position = partner * rows + station * most + rank
    place = lax.broadcasted_iota(jnp.int32, (n * rows, count), 0) == position
    place = jnp.where(place, 1.0, 0.0).astype(jnp.bfloat16)

    lane = lax.broadcasted_iota(jnp.int32, (count, LANES), 1)
    meta = jnp.where(lane == LANES - 1, column_of(local) + 1, 0)
    meta = jnp.where(lane == LANES - 2, column_of(quotient(moveout, LANES)), meta)
    meta = jnp.where(lane == LANES - 3, column_of(remainder(moveout, LANES)), meta)
    meta = meta.astype(jnp.float32).astype(jnp.bfloat16)

    for copy in copies[:-3]:
        copy.wait()
    waves = [
        jnp.concatenate([waves_ref[s * components + c] for s in range(stations)], axis=0)
        for c in range(components)
    ]
    placed = [
        jnp.dot(place, waves[c][:, : whole * LANES], preferred_element_type=jnp.float32)
        for c in range(components)
    ]
    ends = []
    for e in range(tails):
        pieces = [waves[c][:, whole * LANES :] for c in range(e * per_tail, min((e + 1) * per_tail, components))]
        used = tail * len(pieces)
        pieces.append(
            meta[:, used:] if e == 0 else jnp.zeros((count, LANES - used), jnp.bfloat16)
        )
        ends.append(jnp.concatenate(pieces, axis=1))
    ends = jnp.dot(place, jnp.concatenate(ends, axis=1), preferred_element_type=jnp.float32)
    if with_data:
        samples = held[0][...].astype(jnp.float32)
        samples = samples.reshape(samples.shape[0] * samples.shape[1], LANES)
        extra = send_refs[0].shape[0] - (components * whole + tails) * rows - samples.shape[0]
        samples = jnp.concatenate([samples, jnp.zeros((extra, LANES), jnp.float32)], axis=0)
    for g, send_ref in zip(partners(n), send_refs):
        mine = slice(g * rows, (g + 1) * rows)
        pieces = [
            placed[c][mine, a * LANES : (a + 1) * LANES] for c in range(components) for a in range(whole)
        ]
        pieces += [ends[mine, e * LANES : (e + 1) * LANES] for e in range(tails)]
        if with_data:
            pieces.append(samples)
        send_ref[...] = jnp.concatenate(pieces, axis=0).astype(jnp.bfloat16)


def correlate_kernel(dims, with_data, *refs):
    if with_data:
        mask_ref, *refs = refs
    else:
        data_ref, mask_ref, *refs = refs
    n, stations, blocks, components, taps, most, rows, width, per_group = dims
    recv_refs, refs = refs[:n], refs[n:]
    *out_refs, x_ref, dsh_ref, rd_ref, ws_ref, rw_ref, meta_ref, sh_ref, stack_ref = refs
    whole, tail, per_tail, tails = chunk_plan(taps, components)
    chunks = whole + 1
    sent = components * whole + tails
    total = n * rows
    here = n * most
    lag_tiles = ceil_to(width - taps + 1, LANES) // LANES
    lag_width = lag_tiles * LANES
    series = stations * components * blocks
    series_rows = ceil_to(series, 8)

    if with_data:
        first = sent * rows
        for d, recv_ref in zip(partners(n), recv_refs):
            x_ref[lax.axis_index("tmpl") ^ d] = recv_ref[first:, :].astype(jnp.float32)[:series_rows]
        x = jnp.concatenate([x_ref[i] for i in range(n)], axis=1)
    else:
        x = data_ref[...].astype(jnp.float32)
        x = jnp.concatenate([x, jnp.zeros((series_rows - series, width), jnp.float32)], axis=0)
    for r in range(SHIFTS):
        moved = pltpu.roll(x, width - r, 1) if r else x
        for t in range(width // LANES):
            dsh_ref[t, r * series_rows : (r + 1) * series_rows, :] = moved[:, t * LANES : (t + 1) * LANES]

    def ahead(values, by):
        return pltpu.roll(values, width - by, 1)

    sums = {1: x * x}
    size = 1
    while 2 * size <= taps:
        sums[2 * size] = sums[size] + ahead(sums[size], size)
        size = 2 * size
    power = sums[size]
    start = size
    while start < taps:
        size = size // 2
        if taps - start >= size:
            power = power + ahead(sums[size], start)
            start += size
    scale = lax.rsqrt(power / taps + epsilon)
    row = lax.broadcasted_iota(jnp.int32, (series_rows, LANES), 0)
    factor = jnp.zeros((series_rows, LANES), jnp.float32)
    for s in range(stations):
        used = [mask_ref[s, c] for c in range(components)]
        total_used = jnp.maximum(functools.reduce(lambda p, q: p + q, used), 1)
        for c in range(components):
            at = (s * components + c) * blocks
            mine = (row >= at) & (row < at + blocks)
            value = jnp.full((series_rows, LANES), used[c]).astype(jnp.float32)
            value = value / jnp.full((series_rows, LANES), total_used).astype(jnp.float32)
            factor = jnp.where(mine, value, factor)
    for t in range(lag_tiles):
        rd_ref[:, t * LANES : (t + 1) * LANES] = scale[:, t * LANES : (t + 1) * LANES] * factor

    target = lax.broadcasted_iota(jnp.int32, (stations * here, total), 0)
    source = lax.broadcasted_iota(jnp.int32, (stations * here, total), 1)
    wanted = (
        quotient(remainder(target, here), most) * rows
        + quotient(target, here) * most
        + remainder(target, most)
    )
    order = jnp.where(source == wanted, 1.0, 0.0).astype(jnp.bfloat16)
    lane = lax.broadcasted_iota(jnp.int32, (stations * here, LANES), 1)
    blocks_in = [ref[: ceil_to(sent * rows, 16), :].astype(jnp.float32) for ref in recv_refs]

    def received(k):
        piece = jnp.concatenate([blocks_in[i][k * rows : (k + 1) * rows] for i in range(n)], axis=0)
        return jnp.dot(order, piece.astype(jnp.bfloat16), preferred_element_type=jnp.float32)

    ends = [received(components * whole + e) for e in range(tails)]
    meta_ref[...] = ends[0]
    for c in range(components):
        pieces = [received(c * whole + a) for a in range(whole)]
        end, before = ends[c // per_tail], (c % per_tail) * tail
        end = pltpu.roll(end, LANES - before, 1) if before else end
        pieces.append(jnp.where(lane < tail, end, 0.0))
        squares = functools.reduce(lambda p, q: p + q, [piece * piece for piece in pieces])
        for a in range(chunks):
            at = (c * chunks + a) * LANES
            ws_ref[:, at : at + LANES] = pieces[a].astype(jnp.bfloat16)
        wave_power = jnp.sum(squares, axis=1, keepdims=True) / taps
        rw_ref[:, c * LANES : (c + 1) * LANES] = jnp.broadcast_to(
            lax.rsqrt(wave_power + epsilon) / taps, (stations * here, LANES)
        )

    depth = (chunks - 1) * LANES + ceil_to(tail, 16)
    lane_here = lax.broadcasted_iota(jnp.int32, (here, LANES), 1)

    for s in range(stations):
        rows_here = slice(s * here, (s + 1) * here)
        meta = meta_ref[rows_here, :]
        tiles_over = meta[:, LANES - 2 : LANES - 1].astype(jnp.int32)
        lanes_over = meta[:, LANES - 3 : LANES - 2].astype(jnp.int32)
        index = lane_here + lanes_over
        within = index < LANES
        index = jnp.bitwise_and(index, LANES - 1)
        for b in range(blocks):
            total_corr = [jnp.zeros((here, LANES), jnp.float32) for _ in range(lag_tiles)]
            for c in range(components):
                at = (s * components + c) * blocks + b
                low = [
                    dsh_ref[t, pl.ds(at, SHIFTS, stride=series_rows), :] for t in range(width // LANES)
                ]
                low = jnp.concatenate(low, axis=1).astype(jnp.bfloat16)
                pieces = [low] + [pltpu.roll(low, width - q, 1) for q in range(SHIFTS, LANES, SHIFTS)]
                shifted = jnp.concatenate(pieces, axis=0)
                hankel = jnp.concatenate(
                    [
                        shifted[: min(LANES, depth - a * LANES), a * LANES : a * LANES + lag_width]
                        for a in range(chunks)
                    ],
                    axis=0,
                )
                w = ws_ref[rows_here, c * chunks * LANES : c * chunks * LANES + depth]
                numerator = jnp.dot(w, hankel, preferred_element_type=jnp.float32)
                over_wave = rw_ref[rows_here, c * LANES : (c + 1) * LANES]
                over_data = rd_ref[at : at + 1, :]
                for t in range(lag_tiles):
                    cut = slice(t * LANES, (t + 1) * LANES)
                    total_corr[t] = total_corr[t] + numerator[:, cut] * over_wave * over_data[:, cut]
            windows = []
            for t in range(NK // LANES + 1):
                window = total_corr[t]
                for h in range(1, lag_tiles - NK // LANES):
                    if t + h < lag_tiles:
                        window = jnp.where(tiles_over == h, total_corr[t + h], window)
                windows.append(jnp.take_along_axis(window, index, axis=1))
            for t in range(NK // LANES):
                aligned = jnp.where(within, windows[t], windows[t + 1])
                at = b * NK + t * LANES
                sh_ref[rows_here, at : at + LANES] = aligned.astype(jnp.bfloat16)

    slot = lax.broadcasted_iota(jnp.int32, (stations * here, LANES), 0)
    half = (slot < stations * here // 2) == (lane < LANES // 2)
    sh_ref[:, blocks * NK :] = jnp.where(half, 1.0, 0.0).astype(jnp.bfloat16)
    local = meta_ref[:, LANES - 1 :].astype(jnp.int32) - 1
    template = lax.broadcasted_iota(jnp.int32, (stations * here, per_group), 1)
    onehot = jnp.where(local == template, 1.0, 0.0).astype(jnp.bfloat16)
    stack_ref[...] = lax.dot_general(
        onehot, sh_ref[...], (((0,), (0,)), ((), ())), preferred_element_type=jnp.float32
    )
    me = lax.axis_index("stn")
    for d, out_ref in zip(partners(len(out_refs)), out_refs):
        owner = me ^ d
        theirs = pl.ds(pl.multiple_of(owner * TPD, TPD), TPD)
        out_ref[...] = stack_ref[theirs, :].astype(jnp.bfloat16)


def finish_kernel(taps, blocks, *refs):
    *parts_refs, out_ref = refs
    total = functools.reduce(lambda p, q: p + q, [ref[...].astype(jnp.float32) for ref in parts_refs])
    first, middle = blocks * NK, blocks * NK + LANES // 2
    count = total[:, first : first + 1] + total[:, middle : middle + 1]
    scale = jnp.sqrt(jnp.float32(taps)) / jnp.sqrt(jnp.maximum(count, 1.0))
    for b in range(blocks):
        out_ref[b] = total[:, b * NK : (b + 1) * NK] * scale


def body(data, waves, slot_group, slot_local, moveout, chan_mask):
    blocks, stations, components, width_here = data.shape
    slots, taps = waves.shape[1], waves.shape[3]
    n = lax.axis_size("tmpl")
    owners = lax.axis_size("stn")
    per_group = TPD * owners
    width = width_here * n
    most = max(2, 2 * slots // n)
    rows = ceil_to(stations * most, 8)
    whole, tail, per_tail, tails = chunk_plan(taps, components)
    series = stations * components * blocks
    series_rows = ceil_to(series, 8)
    with_data = width_here == LANES
    here = n * most

    waves = jnp.transpose(waves, (0, 2, 1, 3)).reshape(stations * components, slots, taps)
    groups = jnp.transpose(slot_group, (0, 2, 1))
    samples = jnp.transpose(data, (1, 2, 0, 3)).reshape(stations * components, blocks, width_here)
    block_rows = (components * whole + tails) * rows + (series_rows if with_data else 0)
    block_rows = ceil_to(block_rows, 16)
    ins = ([samples] if with_data else []) + [waves, groups, slot_local, moveout]
    ins = [pltpu.with_memory_space_constraint(x, pltpu.HBM) for x in ins]
    send = pl.pallas_call(
        functools.partial(
            pack_kernel, (n, stations, slots, components, taps, most, rows), with_data
        ),
        out_shape=[jax.ShapeDtypeStruct((block_rows, LANES), jnp.bfloat16)] * n,
        in_specs=[pl.BlockSpec(memory_space=pltpu.HBM)] * len(ins),
        scratch_shapes=[pltpu.VMEM(x.shape, x.dtype) for x in ins]
        + [pltpu.SemaphoreType.DMA((len(ins),))],
        compiler_params=pltpu.CompilerParams(vmem_limit_bytes=24 << 20),
        name="pack",
    )(*ins)
    received = [
        lax.ppermute(block, "tmpl", [(i, i ^ d) for i in range(n)]) if d else block
        for d, block in zip(partners(n), send)
    ]
    if not with_data:
        samples = lax.all_gather(samples.reshape(series, width_here), "tmpl", axis=1, tiled=True)
    vmem = pl.BlockSpec(memory_space=pltpu.VMEM)
    partial_stacks = pl.pallas_call(
        functools.partial(
            correlate_kernel,
            (n, stations, blocks, components, taps, most, rows, width, per_group),
            with_data,
        ),
        out_shape=[jax.ShapeDtypeStruct((TPD, blocks * NK + LANES), jnp.bfloat16)] * owners,
        in_specs=[vmem] * (0 if with_data else 1) + [pl.BlockSpec(memory_space=pltpu.SMEM)] + [vmem] * n,
        scratch_shapes=[
            pltpu.VMEM((width // LANES, series_rows, LANES), jnp.float32),
            pltpu.VMEM((width // LANES, SHIFTS * series_rows, LANES), jnp.float32),
            pltpu.VMEM((series_rows, ceil_to(width - taps + 1, LANES)), jnp.float32),
            pltpu.VMEM((stations * here, components * (whole + 1) * LANES), jnp.bfloat16),
            pltpu.VMEM((stations * here, components * LANES), jnp.float32),
            pltpu.VMEM((stations * here, LANES), jnp.float32),
            pltpu.VMEM((stations * here, blocks * NK + LANES), jnp.bfloat16),
            pltpu.VMEM((per_group, blocks * NK + LANES), jnp.float32),
        ],
        compiler_params=pltpu.CompilerParams(vmem_limit_bytes=40 << 20),
        name="correlate",
    )(*([] if with_data else [samples]), chan_mask, *received)
    parts = [
        lax.ppermute(part, "stn", [(i, i ^ d) for i in range(owners)]) if d else part
        for d, part in zip(partners(owners), partial_stacks)
    ]
    return pl.pallas_call(
        functools.partial(finish_kernel, taps, blocks),
        out_shape=jax.ShapeDtypeStruct((blocks, TPD, NK), jnp.float32),
        compiler_params=pltpu.CompilerParams(vmem_limit_bytes=4 << 20),
        name="finish",
    )(*parts)


def solution(mesh):
    in_specs = (
        P(None, "stn", None, "tmpl"),
        P("stn", "tmpl", None, None),
        P("stn", "tmpl", None),
        P("stn", "tmpl"),
        P("stn", "tmpl"),
        P("stn", None),
    )
    out_specs = P(None, ("tmpl", "stn"), None)
    return jax.shard_map(body, mesh=mesh, in_specs=in_specs, out_specs=out_specs, check_vma=False)
```

```python
import functools

import jax
import jax.numpy as jnp
from jax import lax
from jax.experimental import pallas as pl
from jax.experimental.pallas import tpu as pltpu
from jax.sharding import PartitionSpec as P

NK = 256
TPD = 16
LANES = 128
PHASES = 8

epsilon = 1e-06


def ceil_to(value, multiple):
    return -(-value // multiple) * multiple


def quotient(values, divisor):
    if divisor & (divisor - 1):
        return values // divisor
    return lax.shift_right_logical(values, divisor.bit_length() - 1)


def remainder(values, divisor):
    if divisor & (divisor - 1):
        return values % divisor
    return values & (divisor - 1)


def partners(n):
    return [0] + list(range(n - 1, 0, -1))


def by_phase(samples):
    old = lax.broadcasted_iota(jnp.int32, (LANES, LANES), 0)
    new = lax.broadcasted_iota(jnp.int32, (LANES, LANES), 1)
    each = LANES // PHASES
    order = jnp.where(old == PHASES * remainder(new, each) + quotient(new, each), 1.0, 0.0)
    return jnp.dot(samples, order.astype(jnp.bfloat16), preferred_element_type=jnp.float32)


def column_of(row):
    n = row.shape[1]
    eye = lax.broadcasted_iota(jnp.int32, (n, n), 0) == lax.broadcasted_iota(jnp.int32, (n, n), 1)
    return jnp.sum(jnp.where(eye, jnp.broadcast_to(row, (n, n)), 0), axis=1, keepdims=True)


def chunk_plan(taps, components):
    whole = taps // LANES
    tail = taps - whole * LANES
    per_tail = (LANES - 3) // tail
    return whole, tail, per_tail, ceil_to(components, per_tail) // per_tail


def pack_kernel(dims, with_data, *refs):
    n, stations, slots, components, taps, most, rows = dims
    ins = refs[: 5 if with_data else 4]
    send_refs = refs[len(ins) : len(ins) + n]
    held = refs[len(ins) + n : -1]
    sems = refs[-1]
    copies = [pltpu.make_async_copy(ins[i], held[i], sems.at[i]) for i in range(len(ins))]
    for copy in copies:
        copy.start()
    waves_ref, group_ref, local_ref, moveout_ref = held[-4:]
    count = stations * slots
    whole, tail, per_tail, tails = chunk_plan(taps, components)

    def flat(ref, three):
        pieces = [ref[s] if three else ref[s : s + 1, :] for s in range(stations)]
        return jnp.concatenate(pieces, axis=1)

    for copy in copies[-3:]:
        copy.wait()
    group = flat(group_ref, True)
    local = flat(local_ref, False)
    moveout = flat(moveout_ref, False)
    group_col = column_of(group)
    upper = lax.broadcasted_iota(jnp.int32, (count, count), 0)
    lower = lax.broadcasted_iota(jnp.int32, (count, count), 1)
    same = (quotient(upper, slots) == quotient(lower, slots)) & (upper < lower)
    rank = jnp.sum(jnp.where(same & (group_col == group), 1, 0), axis=0, keepdims=True)
    station = quotient(lax.broadcasted_iota(jnp.int32, (1, count), 1), slots)
    partner = group ^ lax.axis_index("tmpl")
    position = partner * rows + station * most + rank
    place = lax.broadcasted_iota(jnp.int32, (n * rows, count), 0) == position
    place = jnp.where(place, 1.0, 0.0).astype(jnp.bfloat16)

    lane = lax.broadcasted_iota(jnp.int32, (count, LANES), 1)
    meta = jnp.where(lane == LANES - 1, column_of(local) + 1, 0)
    meta = jnp.where(lane == LANES - 2, column_of(quotient(moveout, LANES)), meta)
    meta = jnp.where(lane == LANES - 3, column_of(remainder(moveout, LANES)), meta)
    meta = meta.astype(jnp.float32).astype(jnp.bfloat16)

    for copy in copies[:-3]:
        copy.wait()
    waves = [
        jnp.concatenate([waves_ref[s * components + c] for s in range(stations)], axis=0)
        for c in range(components)
    ]
    placed = [
        jnp.dot(place, waves[c][:, : whole * LANES], preferred_element_type=jnp.float32)
        for c in range(components)
    ]
    ends = []
    for e in range(tails):
        pieces = [waves[c][:, whole * LANES :] for c in range(e * per_tail, min((e + 1) * per_tail, components))]
        used = tail * len(pieces)
        pieces.append(
            meta[:, used:] if e == 0 else jnp.zeros((count, LANES - used), jnp.bfloat16)
        )
        ends.append(jnp.concatenate(pieces, axis=1))
    ends = jnp.dot(place, jnp.concatenate(ends, axis=1), preferred_element_type=jnp.float32)
    if with_data:
        samples = held[0][...].astype(jnp.float32)
        samples = samples.reshape(samples.shape[0] * samples.shape[1], LANES)
        samples = by_phase(samples.astype(jnp.bfloat16))
        extra = send_refs[0].shape[0] - (components * whole + tails) * rows - samples.shape[0]
        samples = jnp.concatenate([samples, jnp.zeros((extra, LANES), jnp.float32)], axis=0)
    for g, send_ref in zip(partners(n), send_refs):
        mine = slice(g * rows, (g + 1) * rows)
        pieces = [
            placed[c][mine, a * LANES : (a + 1) * LANES] for c in range(components) for a in range(whole)
        ]
        pieces += [ends[mine, e * LANES : (e + 1) * LANES] for e in range(tails)]
        if with_data:
            pieces.append(samples)
        send_ref[...] = jnp.concatenate(pieces, axis=0).astype(jnp.bfloat16)


def correlate_kernel(dims, with_data, *refs):
    if with_data:
        mask_ref, *refs = refs
    else:
        data_ref, mask_ref, *refs = refs
    n, stations, blocks, components, taps, most, rows, width, per_group = dims
    recv_refs, refs = refs[:n], refs[n:]
    *out_refs, x_ref, phase_ref, rd_ref, wave_ref, rw_ref, meta_ref, sh_ref, stack_ref = refs
    whole, tail, per_tail, tails = chunk_plan(taps, components)
    sent = components * whole + tails
    total = n * rows
    here = n * most
    series = stations * components * blocks
    series_rows = ceil_to(series, 8)
    tiles = width // LANES
    assert tiles == PHASES and taps % PHASES

    if with_data:
        first = sent * rows
        for d, recv_ref in zip(partners(n), recv_refs):
            x_ref[lax.axis_index("tmpl") ^ d] = recv_ref[first:, :].astype(jnp.float32)[:series_rows]
    else:
        for i in range(tiles):
            x_ref[i, :series, :] = by_phase(data_ref[:, i * LANES : (i + 1) * LANES])
            x_ref[i, series:, :] = jnp.zeros((series_rows - series, LANES), jnp.float32)
    each = LANES // PHASES
    piece = quotient(lax.broadcasted_iota(jnp.int32, (series_rows, LANES), 1), each)
    for r in range(PHASES):
        phase = jnp.zeros((series_rows, LANES), jnp.float32)
        for i in range(tiles):
            by = each * ((i - r) % PHASES)
            moved = pltpu.roll(x_ref[i], by, 1) if by else x_ref[i]
            phase = jnp.where(piece == i, moved, phase)
        phase_ref[pl.ds(r, series_rows, stride=PHASES), :] = phase

    def ahead(values, by):
        return pltpu.roll(values, LANES - by, 1)

    phase_rows = series_rows * PHASES
    squares = phase_ref[...]
    squares = squares * squares
    r = remainder(lax.broadcasted_iota(jnp.int32, (phase_rows, LANES), 0), PHASES)
    until, since = squares, squares
    for step in (1, 2, 4):
        until = until + jnp.where(r >= step, pltpu.roll(until, step, 0), 0.0)
        since = since + jnp.where(r < PHASES - step, pltpu.roll(since, phase_rows - step, 0), 0.0)
    block = until + since - squares
    full, over = taps // PHASES, taps % PHASES - 1
    sums = {1: block}
    size = 1
    while 2 * size <= full - 1:
        sums[2 * size] = sums[size] + ahead(sums[size], size)
        size = 2 * size
    power, start = since, 1
    while start < full:
        if start + size <= full:
            power = power + ahead(sums[size], start)
            start += size
        size = size // 2
    last = until
    if over:
        up, down = pltpu.roll(until, phase_rows - over, 0), pltpu.roll(until, PHASES - over, 0)
        last = jnp.where(r < PHASES - over, up, down)
    power = power + jnp.where(
        r < PHASES - over, ahead(last, full), ahead(block, full) + ahead(last, full + 1)
    )
    scale = lax.rsqrt(power / taps + epsilon)
    for s in range(stations):
        used = [mask_ref[s, c] for c in range(components)]
        total_used = jnp.maximum(functools.reduce(lambda p, q: p + q, used), 1)
        for c in range(components):
            mine = slice((s * components + c) * blocks * PHASES, (s * components + c + 1) * blocks * PHASES)
            factor = jnp.full((blocks * PHASES, LANES), used[c]).astype(jnp.float32)
            factor = factor / jnp.full((blocks * PHASES, LANES), total_used).astype(jnp.float32)
            rd_ref[mine, :] = scale[mine, :] * factor

    target = lax.broadcasted_iota(jnp.int32, (stations * here, total), 0)
    source = lax.broadcasted_iota(jnp.int32, (stations * here, total), 1)
    wanted = (
        quotient(remainder(target, here), most) * rows
        + quotient(target, here) * most
        + remainder(target, most)
    )
    order = jnp.where(source == wanted, 1.0, 0.0).astype(jnp.bfloat16)
    lane = lax.broadcasted_iota(jnp.int32, (stations * here, LANES), 1)
    blocks_in = [ref[: ceil_to(sent * rows, 16), :].astype(jnp.float32) for ref in recv_refs]

    def received(k):
        piece = jnp.concatenate([blocks_in[i][k * rows : (k + 1) * rows] for i in range(n)], axis=0)
        return jnp.dot(order, piece.astype(jnp.bfloat16), preferred_element_type=jnp.float32)

    ends = [received(components * whole + e) for e in range(tails)]
    meta_ref[...] = ends[0]
    for c in range(components):
        pieces = [received(c * whole + a) for a in range(whole)]
        end, before = ends[c // per_tail], (c % per_tail) * tail
        end = pltpu.roll(end, LANES - before, 1) if before else end
        pieces.append(jnp.where(lane < tail, end, 0.0))
        squares = functools.reduce(lambda p, q: p + q, [piece * piece for piece in pieces])
        wave = jnp.concatenate([piece.astype(jnp.bfloat16) for piece in pieces], axis=1)
        for p in range(PHASES):
            moved = pltpu.roll(wave, p, 1) if p else wave
            for s in range(stations):
                at = ((s * components + c) * PHASES + p) * here
                wave_ref[at : at + here, :] = moved[s * here : (s + 1) * here, :]
        wave_power = jnp.sum(squares, axis=1, keepdims=True) / taps
        rw_ref[:, c * LANES : (c + 1) * LANES] = jnp.broadcast_to(
            lax.rsqrt(wave_power + epsilon) / taps, (stations * here, LANES)
        )

    depth = ceil_to(taps + PHASES - 1, 2 * PHASES)
    span = NK // PHASES
    fit = LANES // span
    lane_here = lax.broadcasted_iota(jnp.int32, (here, LANES), 1)
    column = quotient(lane_here, span)

    for s in range(stations):
        rows_here = slice(s * here, (s + 1) * here)
        meta = meta_ref[rows_here, :]
        moved_by = meta[:, LANES - 2 : LANES - 1] * LANES + meta[:, LANES - 3 : LANES - 2]
        moved_by = moved_by.astype(jnp.int32)
        corr = [[None] * blocks for _ in range(PHASES)]
        for c in range(components):
            at = (s * components + c) * PHASES
            shifted = []
            for b in range(blocks):
                low = phase_ref[at * blocks + b * PHASES : at * blocks + (b + 1) * PHASES, :]
                low = jnp.concatenate([low, ahead(low, 1)], axis=0).astype(jnp.bfloat16)
                low = [low] + [ahead(low, i) for i in range(2, depth // PHASES, 2)]
                shifted.append(jnp.concatenate(low, axis=0))
            shifted = jnp.concatenate(shifted, axis=1)
            w = wave_ref[at * here : (at + PHASES) * here, :depth]
            numerator = jnp.dot(w, shifted, preferred_element_type=jnp.float32)
            over_wave = rw_ref[rows_here, c * LANES : (c + 1) * LANES]
            for p in range(PHASES):
                for b in range(blocks):
                    term = numerator[p * here : (p + 1) * here, b * LANES : (b + 1) * LANES]
                    row = at * blocks + b * PHASES + p
                    term = term * over_wave * rd_ref[row : row + 1, :]
                    corr[p][b] = term if c == 0 else corr[p][b] + term
        step = PHASES // 2
        while step:
            chosen = (moved_by & step) != 0
            ahead_of = [
                corr[p + step] if p + step < PHASES else [ahead(v, 1) for v in corr[p + step - PHASES]]
                for p in range(PHASES)
            ]
            corr = [
                [jnp.where(chosen, ahead_of[p][b], corr[p][b]) for b in range(blocks)]
                for p in range(PHASES)
            ]
            step = step // 2
        index = remainder(lane_here, span) + quotient(moved_by, PHASES)
        for b in range(blocks):
            for h in range(PHASES // fit):
                packed = jnp.take_along_axis(corr[h * fit][b], index, axis=1)
                for q in range(1, fit):
                    taken = jnp.take_along_axis(corr[h * fit + q][b], index, axis=1)
                    packed = jnp.where(column == q, taken, packed)
                at = b * NK + h * LANES
                sh_ref[rows_here, at : at + LANES] = packed.astype(jnp.bfloat16)

    slot = lax.broadcasted_iota(jnp.int32, (stations * here, LANES), 0)
    half = (slot < stations * here // 2) == (lane < LANES // 2)
    sh_ref[:, blocks * NK :] = jnp.where(half, 1.0, 0.0).astype(jnp.bfloat16)
    local = meta_ref[:, LANES - 1 :].astype(jnp.int32) - 1
    template = lax.broadcasted_iota(jnp.int32, (stations * here, per_group), 1)
    onehot = jnp.where(local == template, 1.0, 0.0).astype(jnp.bfloat16)
    stacks = lax.dot_general(
        onehot, sh_ref[...], (((0,), (0,)), ((), ())), preferred_element_type=jnp.float32
    )
    old = lax.broadcasted_iota(jnp.int32, (NK, NK), 0)
    new = lax.broadcasted_iota(jnp.int32, (NK, NK), 1)
    in_order = jnp.where(old == span * remainder(new, PHASES) + quotient(new, PHASES), 1.0, 0.0)
    for b in range(blocks):
        lags = slice(b * NK, (b + 1) * NK)
        stack_ref[:, lags] = jnp.dot(
            stacks[:, lags].astype(jnp.bfloat16),
            in_order.astype(jnp.bfloat16),
            preferred_element_type=jnp.float32,
        )
    stack_ref[:, blocks * NK :] = stacks[:, blocks * NK :]
    me = lax.axis_index("stn")
    for d, out_ref in zip(partners(len(out_refs)), out_refs):
        owner = me ^ d
        theirs = pl.ds(pl.multiple_of(owner * TPD, TPD), TPD)
        out_ref[...] = stack_ref[theirs, :].astype(jnp.bfloat16)


def finish_kernel(taps, blocks, *refs):
    *parts_refs, out_ref = refs
    total = functools.reduce(lambda p, q: p + q, [ref[...].astype(jnp.float32) for ref in parts_refs])
    first, middle = blocks * NK, blocks * NK + LANES // 2
    count = total[:, first : first + 1] + total[:, middle : middle + 1]
    scale = jnp.sqrt(jnp.float32(taps)) / jnp.sqrt(jnp.maximum(count, 1.0))
    for b in range(blocks):
        out_ref[b] = total[:, b * NK : (b + 1) * NK] * scale


def body(data, waves, slot_group, slot_local, moveout, chan_mask):
    blocks, stations, components, width_here = data.shape
    slots, taps = waves.shape[1], waves.shape[3]
    n = lax.axis_size("tmpl")
    owners = lax.axis_size("stn")
    per_group = TPD * owners
    width = width_here * n
    most = max(2, 2 * slots // n)
    rows = ceil_to(stations * most, 8)
    whole, tail, per_tail, tails = chunk_plan(taps, components)
    series = stations * components * blocks
    series_rows = ceil_to(series, 8)
    with_data = width_here == LANES
    here = n * most

    waves = jnp.transpose(waves, (0, 2, 1, 3)).reshape(stations * components, slots, taps)
    groups = jnp.transpose(slot_group, (0, 2, 1))
    samples = jnp.transpose(data, (1, 2, 0, 3)).reshape(stations * components, blocks, width_here)
    block_rows = (components * whole + tails) * rows + (series_rows if with_data else 0)
    block_rows = ceil_to(block_rows, 16)
    ins = ([samples] if with_data else []) + [waves, groups, slot_local, moveout]
    ins = [pltpu.with_memory_space_constraint(x, pltpu.HBM) for x in ins]
    send = pl.pallas_call(
        functools.partial(
            pack_kernel, (n, stations, slots, components, taps, most, rows), with_data
        ),
        out_shape=[jax.ShapeDtypeStruct((block_rows, LANES), jnp.bfloat16)] * n,
        in_specs=[pl.BlockSpec(memory_space=pltpu.HBM)] * len(ins),
        scratch_shapes=[pltpu.VMEM(x.shape, x.dtype) for x in ins]
        + [pltpu.SemaphoreType.DMA((len(ins),))],
        compiler_params=pltpu.CompilerParams(vmem_limit_bytes=24 << 20),
        name="pack",
    )(*ins)
    received = [
        lax.ppermute(block, "tmpl", [(i, i ^ d) for i in range(n)]) if d else block
        for d, block in zip(partners(n), send)
    ]
    if not with_data:
        samples = lax.all_gather(samples.reshape(series, width_here), "tmpl", axis=1, tiled=True)
    vmem = pl.BlockSpec(memory_space=pltpu.VMEM)
    partial_stacks = pl.pallas_call(
        functools.partial(
            correlate_kernel,
            (n, stations, blocks, components, taps, most, rows, width, per_group),
            with_data,
        ),
        out_shape=[jax.ShapeDtypeStruct((TPD, blocks * NK + LANES), jnp.bfloat16)] * owners,
        in_specs=[vmem] * (0 if with_data else 1) + [pl.BlockSpec(memory_space=pltpu.SMEM)] + [vmem] * n,
        scratch_shapes=[
            pltpu.VMEM((width // LANES, series_rows, LANES), jnp.float32),
            pltpu.VMEM((series_rows * PHASES, LANES), jnp.float32),
            pltpu.VMEM((series_rows * PHASES, LANES), jnp.float32),
            pltpu.VMEM((stations * components * PHASES * here, (whole + 1) * LANES), jnp.bfloat16),
            pltpu.VMEM((stations * here, components * LANES), jnp.float32),
            pltpu.VMEM((stations * here, LANES), jnp.float32),
            pltpu.VMEM((stations * here, blocks * NK + LANES), jnp.bfloat16),
            pltpu.VMEM((per_group, blocks * NK + LANES), jnp.float32),
        ],
        compiler_params=pltpu.CompilerParams(vmem_limit_bytes=40 << 20),
        name="correlate",
    )(*([] if with_data else [samples]), chan_mask, *received)
    parts = [
        lax.ppermute(part, "stn", [(i, i ^ d) for i in range(owners)]) if d else part
        for d, part in zip(partners(owners), partial_stacks)
    ]
    return pl.pallas_call(
        functools.partial(finish_kernel, taps, blocks),
        out_shape=jax.ShapeDtypeStruct((blocks, TPD, NK), jnp.float32),
        compiler_params=pltpu.CompilerParams(vmem_limit_bytes=4 << 20),
        name="finish",
    )(*parts)


def solution(mesh):
    in_specs = (
        P(None, "stn", None, "tmpl"),
        P("stn", "tmpl", None, None),
        P("stn", "tmpl", None),
        P("stn", "tmpl"),
        P("stn", "tmpl"),
        P("stn", None),
    )
    out_specs = P(None, ("tmpl", "stn"), None)
    return jax.shard_map(body, mesh=mesh, in_specs=in_specs, out_specs=out_specs, check_vma=False)
```

```python
import functools

import jax
import jax.numpy as jnp
from jax import lax
from jax.experimental import pallas as pl
from jax.experimental.pallas import tpu as pltpu
from jax.sharding import PartitionSpec as P

NK = 256
TPD = 16
LANES = 128
SHIFTS = 16

epsilon = 1e-06


def ceil_to(value, multiple):
    return -(-value // multiple) * multiple


def quotient(values, divisor):
    if divisor & (divisor - 1):
        return values // divisor
    return lax.shift_right_logical(values, divisor.bit_length() - 1)


def remainder(values, divisor):
    if divisor & (divisor - 1):
        return values % divisor
    return values & (divisor - 1)


def partners(n):
    return [0] + list(range(n - 1, 0, -1))


def chips(n):
    return list(range(n - 2, 0, -2))


def column_of(row):
    n = row.shape[1]
    eye = lax.broadcasted_iota(jnp.int32, (n, n), 0) == lax.broadcasted_iota(jnp.int32, (n, n), 1)
    return jnp.sum(jnp.where(eye, jnp.broadcast_to(row, (n, n)), 0), axis=1, keepdims=True)


def chunk_plan(taps, components):
    whole = taps // LANES
    tail = taps - whole * LANES
    per_tail = (LANES - 3) // tail
    return whole, tail, per_tail, ceil_to(components, per_tail) // per_tail


def pack_kernel(dims, with_data, *refs):
    n, stations, slots, components, taps, most, rows = dims
    ins = refs[: 5 if with_data else 4]
    own_ref, core_ref, *chip_refs = refs[len(ins) : len(ins) + 1 + n // 2]
    held = refs[len(ins) + 1 + n // 2 : -1]
    block_rows = own_ref.shape[0]
    sems = refs[-1]
    copies = [pltpu.make_async_copy(ins[i], held[i], sems.at[i]) for i in range(len(ins))]
    for copy in copies:
        copy.start()
    waves_ref, group_ref, local_ref, moveout_ref = held[-4:]
    count = stations * slots
    whole, tail, per_tail, tails = chunk_plan(taps, components)

    def flat(ref, three):
        pieces = [ref[s] if three else ref[s : s + 1, :] for s in range(stations)]
        return jnp.concatenate(pieces, axis=1)

    for copy in copies[-3:]:
        copy.wait()
    group = flat(group_ref, True)
    local = flat(local_ref, False)
    moveout = flat(moveout_ref, False)
    group_col = column_of(group)
    upper = lax.broadcasted_iota(jnp.int32, (count, count), 0)
    lower = lax.broadcasted_iota(jnp.int32, (count, count), 1)
    same = (quotient(upper, slots) == quotient(lower, slots)) & (upper < lower)
    rank = jnp.sum(jnp.where(same & (group_col == group), 1, 0), axis=0, keepdims=True)
    station = quotient(lax.broadcasted_iota(jnp.int32, (1, count), 1), slots)
    partner = group ^ lax.axis_index("tmpl")
    position = partner * rows + station * most + rank
    place = lax.broadcasted_iota(jnp.int32, (n * rows, count), 0) == position
    place = jnp.where(place, 1.0, 0.0).astype(jnp.bfloat16)

    lane = lax.broadcasted_iota(jnp.int32, (count, LANES), 1)
    meta = jnp.where(lane == LANES - 1, column_of(local) + 1, 0)
    meta = jnp.where(lane == LANES - 2, column_of(quotient(moveout, LANES)), meta)
    meta = jnp.where(lane == LANES - 3, column_of(remainder(moveout, LANES)), meta)
    meta = meta.astype(jnp.float32).astype(jnp.bfloat16)

    for copy in copies[:-3]:
        copy.wait()
    waves = [
        jnp.concatenate([waves_ref[s * components + c] for s in range(stations)], axis=0)
        for c in range(components)
    ]
    placed = [
        jnp.dot(place, waves[c][:, : whole * LANES], preferred_element_type=jnp.float32)
        for c in range(components)
    ]
    ends = []
    for e in range(tails):
        pieces = [waves[c][:, whole * LANES :] for c in range(e * per_tail, min((e + 1) * per_tail, components))]
        used = tail * len(pieces)
        pieces.append(
            meta[:, used:] if e == 0 else jnp.zeros((count, LANES - used), jnp.bfloat16)
        )
        ends.append(jnp.concatenate(pieces, axis=1))
    ends = jnp.dot(place, jnp.concatenate(ends, axis=1), preferred_element_type=jnp.float32)
    if with_data:
        samples = held[0][...].astype(jnp.float32)
        samples = samples.reshape(samples.shape[0] * samples.shape[1], LANES)
        extra = block_rows - (components * whole + tails) * rows - samples.shape[0]
        samples = jnp.concatenate([samples, jnp.zeros((extra, LANES), jnp.float32)], axis=0)
    to = [(0, own_ref, 0), (1, core_ref, 0)]
    for d, ref in zip(chips(n), chip_refs):
        to += [(d, ref, 0), (d + 1, ref, block_rows)]
    for g, send_ref, at in to:
        mine = slice(g * rows, (g + 1) * rows)
        pieces = [
            placed[c][mine, a * LANES : (a + 1) * LANES] for c in range(components) for a in range(whole)
        ]
        pieces += [ends[mine, e * LANES : (e + 1) * LANES] for e in range(tails)]
        if with_data:
            pieces.append(samples)
        send_ref[at : at + block_rows, :] = jnp.concatenate(pieces, axis=0).astype(jnp.bfloat16)


def correlate_kernel(dims, with_data, *refs):
    if with_data:
        mask_ref, *refs = refs
    else:
        data_ref, mask_ref, *refs = refs
    n, stations, blocks, components, taps, most, rows, width, per_group = dims
    own_ref, core_ref, *chip_refs = refs[:n]
    refs = refs[n:]
    block_rows = own_ref.shape[0]
    come = [(0, own_ref, 0), (1, core_ref, 0)]
    for i, d in enumerate(chips(n)):
        come += [(d, chip_refs[i], 0), (d + 1, chip_refs[n // 2 - 1 + i], block_rows)]
    *out_refs, x_ref, dsh_ref, rd_ref, ws_ref, rw_ref, meta_ref, sh_ref, stack_ref = refs
    whole, tail, per_tail, tails = chunk_plan(taps, components)
    chunks = whole + 1
    sent = components * whole + tails
    total = n * rows
    here = n * most
    lag_tiles = ceil_to(width - taps + 1, LANES) // LANES
    lag_width = lag_tiles * LANES
    series = stations * components * blocks
    series_rows = ceil_to(series, 8)

    if with_data:
        first = sent * rows
        for d, ref, at in come:
            samples = ref[at + first : at + block_rows, :].astype(jnp.float32)
            x_ref[lax.axis_index("tmpl") ^ d] = samples[:series_rows]
        x = jnp.concatenate([x_ref[i] for i in range(n)], axis=1)
    else:
        x = data_ref[...].astype(jnp.float32)
        x = jnp.concatenate([x, jnp.zeros((series_rows - series, width), jnp.float32)], axis=0)
    for r in range(SHIFTS):
        moved = pltpu.roll(x, width - r, 1) if r else x
        for t in range(width // LANES):
            dsh_ref[t, r * series_rows : (r + 1) * series_rows, :] = moved[:, t * LANES : (t + 1) * LANES]

    def ahead(values, by):
        return pltpu.roll(values, width - by, 1)

    sums = {1: x * x}
    size = 1
    while 2 * size <= taps:
        sums[2 * size] = sums[size] + ahead(sums[size], size)
        size = 2 * size
    power = sums[size]
    start = size
    while start < taps:
        size = size // 2
        if taps - start >= size:
            power = power + ahead(sums[size], start)
            start += size
    scale = lax.rsqrt(power / taps + epsilon)
    row = lax.broadcasted_iota(jnp.int32, (series_rows, LANES), 0)
    factor = jnp.zeros((series_rows, LANES), jnp.float32)
    for s in range(stations):
        used = [mask_ref[s, c] for c in range(components)]
        total_used = jnp.maximum(functools.reduce(lambda p, q: p + q, used), 1)
        for c in range(components):
            at = (s * components + c) * blocks
            mine = (row >= at) & (row < at + blocks)
            value = jnp.full((series_rows, LANES), used[c]).astype(jnp.float32)
            value = value / jnp.full((series_rows, LANES), total_used).astype(jnp.float32)
            factor = jnp.where(mine, value, factor)
    for t in range(lag_tiles):
        rd_ref[:, t * LANES : (t + 1) * LANES] = scale[:, t * LANES : (t + 1) * LANES] * factor

    target = lax.broadcasted_iota(jnp.int32, (stations * here, total), 0)
    source = lax.broadcasted_iota(jnp.int32, (stations * here, total), 1)
    wanted = (
        quotient(remainder(target, here), most) * rows
        + quotient(target, here) * most
        + remainder(target, most)
    )
    order = jnp.where(source == wanted, 1.0, 0.0).astype(jnp.bfloat16)
    lane = lax.broadcasted_iota(jnp.int32, (stations * here, LANES), 1)
    blocks_in = [ref[at : at + ceil_to(sent * rows, 16), :].astype(jnp.float32) for _, ref, at in come]

    def received(k):
        piece = jnp.concatenate([blocks_in[i][k * rows : (k + 1) * rows] for i in range(n)], axis=0)
        return jnp.dot(order, piece.astype(jnp.bfloat16), preferred_element_type=jnp.float32)

    ends = [received(components * whole + e) for e in range(tails)]
    meta_ref[...] = ends[0]
    for c in range(components):
        pieces = [received(c * whole + a) for a in range(whole)]
        end, before = ends[c // per_tail], (c % per_tail) * tail
        end = pltpu.roll(end, LANES - before, 1) if before else end
        pieces.append(jnp.where(lane < tail, end, 0.0))
        squares = functools.reduce(lambda p, q: p + q, [piece * piece for piece in pieces])
        for a in range(chunks):
            at = (c * chunks + a) * LANES
            ws_ref[:, at : at + LANES] = pieces[a].astype(jnp.bfloat16)
        wave_power = jnp.sum(squares, axis=1, keepdims=True) / taps
        rw_ref[:, c * LANES : (c + 1) * LANES] = jnp.broadcast_to(
            lax.rsqrt(wave_power + epsilon) / taps, (stations * here, LANES)
        )

    depth = (chunks - 1) * LANES + ceil_to(tail, 16)
    lane_here = lax.broadcasted_iota(jnp.int32, (here, LANES), 1)

    for s in range(stations):
        rows_here = slice(s * here, (s + 1) * here)
        meta = meta_ref[rows_here, :]
        tiles_over = meta[:, LANES - 2 : LANES - 1].astype(jnp.int32)
        lanes_over = meta[:, LANES - 3 : LANES - 2].astype(jnp.int32)
        index = lane_here + lanes_over
        within = index < LANES
        index = jnp.bitwise_and(index, LANES - 1)
        for b in range(blocks):
            total_corr = [jnp.zeros((here, LANES), jnp.float32) for _ in range(lag_tiles)]
            for c in range(components):
                at = (s * components + c) * blocks + b
                low = [
                    dsh_ref[t, pl.ds(at, SHIFTS, stride=series_rows), :] for t in range(width // LANES)
                ]
                low = jnp.concatenate(low, axis=1).astype(jnp.bfloat16)
                pieces = [low] + [pltpu.roll(low, width - q, 1) for q in range(SHIFTS, LANES, SHIFTS)]
                shifted = jnp.concatenate(pieces, axis=0)
                hankel = jnp.concatenate(
                    [
                        shifted[: min(LANES, depth - a * LANES), a * LANES : a * LANES + lag_width]
                        for a in range(chunks)
                    ],
                    axis=0,
                )
                w = ws_ref[rows_here, c * chunks * LANES : c * chunks * LANES + depth]
                numerator = jnp.dot(w, hankel, preferred_element_type=jnp.float32)
                over_wave = rw_ref[rows_here, c * LANES : (c + 1) * LANES]
                over_data = rd_ref[at : at + 1, :]
                for t in range(lag_tiles):
                    cut = slice(t * LANES, (t + 1) * LANES)
                    total_corr[t] = total_corr[t] + numerator[:, cut] * over_wave * over_data[:, cut]
            windows = []
            for t in range(NK // LANES + 1):
                window = total_corr[t]
                for h in range(1, lag_tiles - NK // LANES):
                    if t + h < lag_tiles:
                        window = jnp.where(tiles_over == h, total_corr[t + h], window)
                windows.append(jnp.take_along_axis(window, index, axis=1))
            for t in range(NK // LANES):
                aligned = jnp.where(within, windows[t], windows[t + 1])
                at = b * NK + t * LANES
                sh_ref[rows_here, at : at + LANES] = aligned.astype(jnp.bfloat16)

    slot = lax.broadcasted_iota(jnp.int32, (stations * here, LANES), 0)
    half = (slot < stations * here // 2) == (lane < LANES // 2)
    sh_ref[:, blocks * NK :] = jnp.where(half, 1.0, 0.0).astype(jnp.bfloat16)
    local = meta_ref[:, LANES - 1 :].astype(jnp.int32) - 1
    template = lax.broadcasted_iota(jnp.int32, (stations * here, per_group), 1)
    onehot = jnp.where(local == template, 1.0, 0.0).astype(jnp.bfloat16)
    stack_ref[...] = lax.dot_general(
        onehot, sh_ref[...], (((0,), (0,)), ((), ())), preferred_element_type=jnp.float32
    )
    me = lax.axis_index("stn")
    for d, out_ref in zip(partners(len(out_refs)), out_refs):
        owner = me ^ d
        theirs = pl.ds(pl.multiple_of(owner * TPD, TPD), TPD)
        out_ref[...] = stack_ref[theirs, :].astype(jnp.bfloat16)


def finish_kernel(taps, blocks, *refs):
    *parts_refs, out_ref = refs
    total = functools.reduce(lambda p, q: p + q, [ref[...].astype(jnp.float32) for ref in parts_refs])
    first, middle = blocks * NK, blocks * NK + LANES // 2
    count = total[:, first : first + 1] + total[:, middle : middle + 1]
    scale = jnp.sqrt(jnp.float32(taps)) / jnp.sqrt(jnp.maximum(count, 1.0))
    for b in range(blocks):
        out_ref[b] = total[:, b * NK : (b + 1) * NK] * scale


def body(data, waves, slot_group, slot_local, moveout, chan_mask):
    blocks, stations, components, width_here = data.shape
    slots, taps = waves.shape[1], waves.shape[3]
    n = lax.axis_size("tmpl")
    owners = lax.axis_size("stn")
    per_group = TPD * owners
    width = width_here * n
    most = max(2, 2 * slots // n)
    rows = ceil_to(stations * most, 8)
    whole, tail, per_tail, tails = chunk_plan(taps, components)
    series = stations * components * blocks
    series_rows = ceil_to(series, 8)
    with_data = width_here == LANES
    here = n * most

    waves = jnp.transpose(waves, (0, 2, 1, 3)).reshape(stations * components, slots, taps)
    groups = jnp.transpose(slot_group, (0, 2, 1))
    samples = jnp.transpose(data, (1, 2, 0, 3)).reshape(stations * components, blocks, width_here)
    block_rows = (components * whole + tails) * rows + (series_rows if with_data else 0)
    block_rows = ceil_to(block_rows, 16)
    ins = ([samples] if with_data else []) + [waves, groups, slot_local, moveout]
    ins = [pltpu.with_memory_space_constraint(x, pltpu.HBM) for x in ins]
    send = pl.pallas_call(
        functools.partial(
            pack_kernel, (n, stations, slots, components, taps, most, rows), with_data
        ),
        out_shape=[jax.ShapeDtypeStruct((block_rows, LANES), jnp.bfloat16)] * 2
        + [jax.ShapeDtypeStruct((2 * block_rows, LANES), jnp.bfloat16)] * (n // 2 - 1),
        in_specs=[pl.BlockSpec(memory_space=pltpu.HBM)] * len(ins),
        scratch_shapes=[pltpu.VMEM(x.shape, x.dtype) for x in ins]
        + [pltpu.SemaphoreType.DMA((len(ins),))],
        compiler_params=pltpu.CompilerParams(vmem_limit_bytes=24 << 20),
        name="pack",
    )(*ins)
    def swap(block, d):
        return lax.ppermute(block, "tmpl", [(i, i ^ d) for i in range(n)])

    own, for_core, *for_chips = send
    from_chips = [swap(block, d) for d, block in zip(chips(n), for_chips)]
    received = [own, swap(for_core, 1)] + from_chips + [swap(block, 1) for block in from_chips]
    if not with_data:
        samples = lax.all_gather(samples.reshape(series, width_here), "tmpl", axis=1, tiled=True)
    vmem = pl.BlockSpec(memory_space=pltpu.VMEM)
    partial_stacks = pl.pallas_call(
        functools.partial(
            correlate_kernel,
            (n, stations, blocks, components, taps, most, rows, width, per_group),
            with_data,
        ),
        out_shape=[jax.ShapeDtypeStruct((TPD, blocks * NK + LANES), jnp.bfloat16)] * owners,
        in_specs=[vmem] * (0 if with_data else 1) + [pl.BlockSpec(memory_space=pltpu.SMEM)] + [vmem] * n,
        scratch_shapes=[
            pltpu.VMEM((width // LANES, series_rows, LANES), jnp.float32),
            pltpu.VMEM((width // LANES, SHIFTS * series_rows, LANES), jnp.float32),
            pltpu.VMEM((series_rows, ceil_to(width - taps + 1, LANES)), jnp.float32),
            pltpu.VMEM((stations * here, components * (whole + 1) * LANES), jnp.bfloat16),
            pltpu.VMEM((stations * here, components * LANES), jnp.float32),
            pltpu.VMEM((stations * here, LANES), jnp.float32),
            pltpu.VMEM((stations * here, blocks * NK + LANES), jnp.bfloat16),
            pltpu.VMEM((per_group, blocks * NK + LANES), jnp.float32),
        ],
        compiler_params=pltpu.CompilerParams(vmem_limit_bytes=40 << 20),
        name="correlate",
    )(*([] if with_data else [samples]), chan_mask, *received)
    parts = [
        lax.ppermute(part, "stn", [(i, i ^ d) for i in range(owners)]) if d else part
        for d, part in zip(partners(owners), partial_stacks)
    ]
    return pl.pallas_call(
        functools.partial(finish_kernel, taps, blocks),
        out_shape=jax.ShapeDtypeStruct((blocks, TPD, NK), jnp.float32),
        compiler_params=pltpu.CompilerParams(vmem_limit_bytes=4 << 20),
        name="finish",
    )(*parts)


def solution(mesh):
    in_specs = (
        P(None, "stn", None, "tmpl"),
        P("stn", "tmpl", None, None),
        P("stn", "tmpl", None),
        P("stn", "tmpl"),
        P("stn", "tmpl"),
        P("stn", None),
    )
    out_specs = P(None, ("tmpl", "stn"), None)
    return jax.shard_map(body, mesh=mesh, in_specs=in_specs, out_specs=out_specs, check_vma=False)
```

```python
import functools

import jax
import jax.numpy as jnp
from jax import lax
from jax.experimental import pallas as pl
from jax.experimental.pallas import tpu as pltpu
from jax.sharding import PartitionSpec as P

NK = 256
TPD = 16
LANES = 128
SHIFTS = 16

epsilon = 1e-06


def ceil_to(value, multiple):
    return -(-value // multiple) * multiple


def quotient(values, divisor):
    if divisor & (divisor - 1):
        return values // divisor
    return lax.shift_right_logical(values, divisor.bit_length() - 1)


def remainder(values, divisor):
    if divisor & (divisor - 1):
        return values % divisor
    return values & (divisor - 1)


def partners(n):
    return [0] + list(range(n - 1, 0, -1))


def chips(n):
    return list(range(n - 2, 0, -2))


def column_of(row):
    n = row.shape[1]
    eye = lax.broadcasted_iota(jnp.int32, (n, n), 0) == lax.broadcasted_iota(jnp.int32, (n, n), 1)
    return jnp.sum(jnp.where(eye, jnp.broadcast_to(row, (n, n)), 0), axis=1, keepdims=True)


SMALL = 8
EXTRAS = 4


def chunk_plan(taps, components):
    whole = taps // LANES
    tail = taps - whole * LANES
    left = components * tail - LANES
    assert 0 < left <= min(tail, SMALL - 3)
    return whole, tail, left


def pack_kernel(dims, with_data, *refs):
    n, stations, slots, components, taps, most, rows = dims
    ins = refs[: 5 if with_data else 4]
    own_ref, core_ref, *chip_refs = refs[len(ins) : len(ins) + 1 + n // 2]
    held = refs[len(ins) + 1 + n // 2 : -1]
    sems = refs[-1]
    copies = [pltpu.make_async_copy(ins[i], held[i], sems.at[i]) for i in range(len(ins))]
    for copy in copies:
        copy.start()
    waves_ref, group_ref, local_ref, moveout_ref = held[-4:]
    count = stations * slots
    whole, tail, left = chunk_plan(taps, components)

    def flat(ref, three):
        pieces = [ref[s] if three else ref[s : s + 1, :] for s in range(stations)]
        return jnp.concatenate(pieces, axis=1)

    for copy in copies[-3:]:
        copy.wait()
    group = flat(group_ref, True)
    local = flat(local_ref, False)
    moveout = flat(moveout_ref, False)
    group_col = column_of(group)
    upper = lax.broadcasted_iota(jnp.int32, (count, count), 0)
    lower = lax.broadcasted_iota(jnp.int32, (count, count), 1)
    same = (quotient(upper, slots) == quotient(lower, slots)) & (upper < lower)
    rank = jnp.sum(jnp.where(same & (group_col == group), 1, 0), axis=0, keepdims=True)
    station = quotient(lax.broadcasted_iota(jnp.int32, (1, count), 1), slots)
    partner = group ^ lax.axis_index("tmpl")
    position = partner * rows + station * most + rank
    place = lax.broadcasted_iota(jnp.int32, (n * rows, count), 0) == position
    place = jnp.where(place, 1.0, 0.0).astype(jnp.bfloat16)

    lane = lax.broadcasted_iota(jnp.int32, (count, LANES), 1)
    meta = [column_of(local) + 1, column_of(quotient(moveout, LANES)), column_of(remainder(moveout, LANES))]

    for copy in copies[:-3]:
        copy.wait()
    waves = [
        jnp.concatenate([waves_ref[s * components + c] for s in range(stations)], axis=0)
        for c in range(components)
    ]
    placed = [
        jnp.dot(place, waves[c][:, : whole * LANES], preferred_element_type=jnp.float32)
        for c in range(components)
    ]
    ends = [waves[c][:, whole * LANES :] for c in range(components - 1)]
    ends.append(waves[-1][:, whole * LANES : taps - left])
    ends = jnp.dot(place, jnp.concatenate(ends, axis=1), preferred_element_type=jnp.float32)
    small = [waves[-1][:, taps - left + v : taps - left + v + 1] for v in range(left)] + meta
    spread = jnp.zeros((count, LANES), jnp.float32)
    for v, column in enumerate(small):
        spread = jnp.where(remainder(lane, SMALL) == v, column.astype(jnp.float32), spread)
    spread = jnp.dot(place, spread.astype(jnp.bfloat16), preferred_element_type=jnp.float32)
    each = LANES // SMALL
    within = remainder(lax.broadcasted_iota(jnp.int32, (rows, LANES), 0), each)
    within = within == quotient(lax.broadcasted_iota(jnp.int32, (rows, LANES), 1), SMALL)
    if with_data:
        samples = held[0][...].astype(jnp.float32)
        samples = samples.reshape(samples.shape[0] * samples.shape[1], LANES)
        samples = jnp.concatenate([samples, jnp.zeros((EXTRAS, LANES), jnp.float32)], axis=0)
    else:
        samples = jnp.zeros((8, LANES), jnp.float32)
    line = lax.broadcasted_iota(jnp.int32, samples.shape, 0)
    messages = [(own_ref, [0]), (core_ref, [1])]
    messages += [(ref, [d, d + 1]) for d, ref in zip(chips(n), chip_refs)]
    for send_ref, groups in messages:
        pieces, last = [], samples
        for g in groups:
            mine = slice(g * rows, (g + 1) * rows)
            for c in range(components):
                pieces += [placed[c][mine, a * LANES : (a + 1) * LANES] for a in range(whole)]
            pieces.append(ends[mine])
            kept = jnp.where(within, spread[mine], 0.0)
            for e in range(-(-rows // each)):
                packed = jnp.sum(kept[e * each : (e + 1) * each], axis=0, keepdims=True)
                last = jnp.where(line == samples.shape[0] - EXTRAS + 2 * (g % 2) + e, packed, last)
        pieces.append(last)
        extra = send_ref.shape[0] - sum(piece.shape[0] for piece in pieces)
        if extra:
            pieces.append(jnp.zeros((extra, LANES), jnp.float32))
        send_ref[...] = jnp.concatenate(pieces, axis=0).astype(jnp.bfloat16)


def correlate_kernel(dims, with_data, *refs):
    if with_data:
        mask_ref, *refs = refs
    else:
        data_ref, mask_ref, *refs = refs
    n, stations, blocks, components, taps, most, rows, width, per_group = dims
    own_ref, core_ref, *chip_refs = refs[:n]
    refs = refs[n:]
    come = [(own_ref, 0, 1), (core_ref, 0, 1)]
    for i in range(n // 2 - 1):
        come += [(chip_refs[i], 0, 2), (chip_refs[n // 2 - 1 + i], 1, 2)]
    distances = [0, 1]
    for d in chips(n):
        distances += [d, d + 1]
    *out_refs, x_ref, dsh_ref, rd_ref, ws_ref, rw_ref, meta_ref, sh_ref, stack_ref = refs
    whole, tail, left = chunk_plan(taps, components)
    chunks = whole + 1
    sent = components * whole + 1
    total = n * rows
    here = n * most
    lag_tiles = ceil_to(width - taps + 1, LANES) // LANES
    lag_width = lag_tiles * LANES
    series = stations * components * blocks
    series_rows = ceil_to(series, 8)

    def lines(ref, start, count):
        first = start // 16 * 16
        return ref[first : ceil_to(start + count, 16), :].astype(jnp.float32)[start - first :][:count]

    last_rows = series + EXTRAS if with_data else 8
    blocks_in = [lines(ref, half * sent * rows, sent * rows) for ref, half, _ in come]
    lasts = [lines(ref, count * sent * rows, last_rows) for ref, _, count in come]

    if with_data:
        for d, last in zip(distances, lasts):
            x_ref[lax.axis_index("tmpl") ^ d] = last
        x = jnp.concatenate([x_ref[i] for i in range(n)], axis=1)
    else:
        x = data_ref[...].astype(jnp.float32)
        x = jnp.concatenate([x, jnp.zeros((series_rows - series, width), jnp.float32)], axis=0)
    for r in range(SHIFTS):
        moved = pltpu.roll(x, width - r, 1) if r else x
        for t in range(width // LANES):
            dsh_ref[t, r * series_rows : (r + 1) * series_rows, :] = moved[:, t * LANES : (t + 1) * LANES]

    def ahead(values, by):
        return pltpu.roll(values, width - by, 1)

    sums = {1: x * x}
    size = 1
    while 2 * size <= taps:
        sums[2 * size] = sums[size] + ahead(sums[size], size)
        size = 2 * size
    power = sums[size]
    start = size
    while start < taps:
        size = size // 2
        if taps - start >= size:
            power = power + ahead(sums[size], start)
            start += size
    scale = lax.rsqrt(power / taps + epsilon)
    row = lax.broadcasted_iota(jnp.int32, (series_rows, LANES), 0)
    factor = jnp.zeros((series_rows, LANES), jnp.float32)
    for s in range(stations):
        used = [mask_ref[s, c] for c in range(components)]
        total_used = jnp.maximum(functools.reduce(lambda p, q: p + q, used), 1)
        for c in range(components):
            at = (s * components + c) * blocks
            mine = (row >= at) & (row < at + blocks)
            value = jnp.full((series_rows, LANES), used[c]).astype(jnp.float32)
            value = value / jnp.full((series_rows, LANES), total_used).astype(jnp.float32)
            factor = jnp.where(mine, value, factor)
    for t in range(lag_tiles):
        rd_ref[:, t * LANES : (t + 1) * LANES] = scale[:, t * LANES : (t + 1) * LANES] * factor

    target = lax.broadcasted_iota(jnp.int32, (stations * here, total), 0)
    source = lax.broadcasted_iota(jnp.int32, (stations * here, total), 1)
    wanted = (
        quotient(remainder(target, here), most) * rows
        + quotient(target, here) * most
        + remainder(target, most)
    )
    order = jnp.where(source == wanted, 1.0, 0.0).astype(jnp.bfloat16)
    lane = lax.broadcasted_iota(jnp.int32, (stations * here, LANES), 1)
    def received(k):
        piece = jnp.concatenate([blocks_in[i][k * rows : (k + 1) * rows] for i in range(n)], axis=0)
        return jnp.dot(order, piece.astype(jnp.bfloat16), preferred_element_type=jnp.float32)

    each = LANES // SMALL
    target = lax.broadcasted_iota(jnp.int32, (stations * here, n * 8), 0)
    place = quotient(target, here) * most + remainder(target, most)
    sender = quotient(remainder(target, here), most)
    line = sender * 8 + (8 - EXTRAS) + 2 * remainder(sender, 2) + quotient(place, each)
    line = lax.broadcasted_iota(jnp.int32, (stations * here, n * 8), 1) == line
    small = jnp.concatenate([last[last_rows - 8 :] for last in lasts], axis=0).astype(jnp.bfloat16)
    small = jnp.dot(
        jnp.where(line, 1.0, 0.0).astype(jnp.bfloat16), small, preferred_element_type=jnp.float32
    )
    target = lax.broadcasted_iota(jnp.int32, (stations * here, LANES), 0)
    place = remainder(quotient(target, here) * most + remainder(target, most), each)
    small = jnp.where(quotient(lane, SMALL) == place, small, 0.0).astype(jnp.bfloat16)
    fold = lax.broadcasted_iota(jnp.int32, (LANES, LANES), 0)
    fold = remainder(fold, SMALL) == lax.broadcasted_iota(jnp.int32, (LANES, LANES), 1)
    fold = jnp.where(fold, 1.0, 0.0).astype(jnp.bfloat16)
    meta_ref[...] = jnp.dot(small, fold, preferred_element_type=jnp.float32)

    ends = received(components * whole)
    for c in range(components):
        pieces = [received(c * whole + a) for a in range(whole)]
        end = pltpu.roll(ends, LANES - c * tail, 1) if c else ends
        if c == components - 1:
            end = jnp.where(lane < tail - left, end, pltpu.roll(meta_ref[...], tail - left, 1))
        pieces.append(jnp.where(lane < tail, end, 0.0))
        squares = functools.reduce(lambda p, q: p + q, [piece * piece for piece in pieces])
        for a in range(chunks):
            at = (c * chunks + a) * LANES
            ws_ref[:, at : at + LANES] = pieces[a].astype(jnp.bfloat16)
        wave_power = jnp.sum(squares, axis=1, keepdims=True) / taps
        rw_ref[:, c * LANES : (c + 1) * LANES] = jnp.broadcast_to(
            lax.rsqrt(wave_power + epsilon) / taps, (stations * here, LANES)
        )

    depth = (chunks - 1) * LANES + ceil_to(tail, 16)
    lane_here = lax.broadcasted_iota(jnp.int32, (here, LANES), 1)

    for s in range(stations):
        rows_here = slice(s * here, (s + 1) * here)
        meta = meta_ref[rows_here, :]
        tiles_over = meta[:, left + 1 : left + 2].astype(jnp.int32)
        lanes_over = meta[:, left + 2 : left + 3].astype(jnp.int32)
        index = lane_here + lanes_over
        within = index < LANES
        index = jnp.bitwise_and(index, LANES - 1)
        for b in range(blocks):
            total_corr = [jnp.zeros((here, LANES), jnp.float32) for _ in range(lag_tiles)]
            for c in range(components):
                at = (s * components + c) * blocks + b
                low = [
                    dsh_ref[t, pl.ds(at, SHIFTS, stride=series_rows), :] for t in range(width // LANES)
                ]
                low = jnp.concatenate(low, axis=1).astype(jnp.bfloat16)
                pieces = [low] + [pltpu.roll(low, width - q, 1) for q in range(SHIFTS, LANES, SHIFTS)]
                shifted = jnp.concatenate(pieces, axis=0)
                hankel = jnp.concatenate(
                    [
                        shifted[: min(LANES, depth - a * LANES), a * LANES : a * LANES + lag_width]
                        for a in range(chunks)
                    ],
                    axis=0,
                )
                w = ws_ref[rows_here, c * chunks * LANES : c * chunks * LANES + depth]
                numerator = jnp.dot(w, hankel, preferred_element_type=jnp.float32)
                over_wave = rw_ref[rows_here, c * LANES : (c + 1) * LANES]
                over_data = rd_ref[at : at + 1, :]
                for t in range(lag_tiles):
                    cut = slice(t * LANES, (t + 1) * LANES)
                    total_corr[t] = total_corr[t] + numerator[:, cut] * over_wave * over_data[:, cut]
            windows = []
            for t in range(NK // LANES + 1):
                window = total_corr[t]
                for h in range(1, lag_tiles - NK // LANES):
                    if t + h < lag_tiles:
                        window = jnp.where(tiles_over == h, total_corr[t + h], window)
                windows.append(jnp.take_along_axis(window, index, axis=1))
            for t in range(NK // LANES):
                aligned = jnp.where(within, windows[t], windows[t + 1])
                at = b * NK + t * LANES
                sh_ref[rows_here, at : at + LANES] = aligned.astype(jnp.bfloat16)

    slot = lax.broadcasted_iota(jnp.int32, (stations * here, LANES), 0)
    half = (slot < stations * here // 2) == (lane < LANES // 2)
    sh_ref[:, blocks * NK :] = jnp.where(half, 1.0, 0.0).astype(jnp.bfloat16)
    local = meta_ref[:, left : left + 1].astype(jnp.int32) - 1
    template = lax.broadcasted_iota(jnp.int32, (stations * here, per_group), 1)
    onehot = jnp.where(local == template, 1.0, 0.0).astype(jnp.bfloat16)
    stack_ref[...] = lax.dot_general(
        onehot, sh_ref[...], (((0,), (0,)), ((), ())), preferred_element_type=jnp.float32
    )
    me = lax.axis_index("stn")
    for d, out_ref in zip(partners(len(out_refs)), out_refs):
        owner = me ^ d
        theirs = pl.ds(pl.multiple_of(owner * TPD, TPD), TPD)
        out_ref[...] = stack_ref[theirs, :].astype(jnp.bfloat16)


def finish_kernel(taps, blocks, *refs):
    *parts_refs, out_ref = refs
    total = functools.reduce(lambda p, q: p + q, [ref[...].astype(jnp.float32) for ref in parts_refs])
    first, middle = blocks * NK, blocks * NK + LANES // 2
    count = total[:, first : first + 1] + total[:, middle : middle + 1]
    scale = jnp.sqrt(jnp.float32(taps)) / jnp.sqrt(jnp.maximum(count, 1.0))
    for b in range(blocks):
        out_ref[b] = total[:, b * NK : (b + 1) * NK] * scale


def body(data, waves, slot_group, slot_local, moveout, chan_mask):
    blocks, stations, components, width_here = data.shape
    slots, taps = waves.shape[1], waves.shape[3]
    n = lax.axis_size("tmpl")
    owners = lax.axis_size("stn")
    per_group = TPD * owners
    width = width_here * n
    most = max(2, 2 * slots // n)
    rows = ceil_to(stations * most, 8)
    whole, tail, left = chunk_plan(taps, components)
    series = stations * components * blocks
    series_rows = ceil_to(series, 8)
    with_data = width_here == LANES
    here = n * most

    waves = jnp.transpose(waves, (0, 2, 1, 3)).reshape(stations * components, slots, taps)
    groups = jnp.transpose(slot_group, (0, 2, 1))
    samples = jnp.transpose(data, (1, 2, 0, 3)).reshape(stations * components, blocks, width_here)
    last_rows = series + EXTRAS if with_data else 8
    message_rows = [ceil_to(k * (components * whole + 1) * rows + last_rows, 16) for k in (1, 1)]
    message_rows += [ceil_to(2 * (components * whole + 1) * rows + last_rows, 16)] * (n // 2 - 1)
    ins = ([samples] if with_data else []) + [waves, groups, slot_local, moveout]
    ins = [pltpu.with_memory_space_constraint(x, pltpu.HBM) for x in ins]
    send = pl.pallas_call(
        functools.partial(
            pack_kernel, (n, stations, slots, components, taps, most, rows), with_data
        ),
        out_shape=[jax.ShapeDtypeStruct((k, LANES), jnp.bfloat16) for k in message_rows],
        in_specs=[pl.BlockSpec(memory_space=pltpu.HBM)] * len(ins),
        scratch_shapes=[pltpu.VMEM(x.shape, x.dtype) for x in ins]
        + [pltpu.SemaphoreType.DMA((len(ins),))],
        compiler_params=pltpu.CompilerParams(vmem_limit_bytes=24 << 20),
        name="pack",
    )(*ins)
    def swap(block, d):
        return lax.ppermute(block, "tmpl", [(i, i ^ d) for i in range(n)])

    own, for_core, *for_chips = send
    from_chips = [swap(block, d) for d, block in zip(chips(n), for_chips)]
    from_core = swap(for_core, 1)
    if from_chips:
        from_chips[0], from_core = lax.optimization_barrier((from_chips[0], from_core))
    received = [own, from_core] + from_chips + [swap(block, 1) for block in from_chips]
    if not with_data:
        samples = lax.all_gather(samples.reshape(series, width_here), "tmpl", axis=1, tiled=True)
    vmem = pl.BlockSpec(memory_space=pltpu.VMEM)
    partial_stacks = pl.pallas_call(
        functools.partial(
            correlate_kernel,
            (n, stations, blocks, components, taps, most, rows, width, per_group),
            with_data,
        ),
        out_shape=[jax.ShapeDtypeStruct((TPD, blocks * NK + LANES), jnp.bfloat16)] * owners,
        in_specs=[vmem] * (0 if with_data else 1) + [pl.BlockSpec(memory_space=pltpu.SMEM)] + [vmem] * n,
        scratch_shapes=[
            pltpu.VMEM((width // LANES, series_rows, LANES), jnp.float32),
            pltpu.VMEM((width // LANES, SHIFTS * series_rows, LANES), jnp.float32),
            pltpu.VMEM((series_rows, ceil_to(width - taps + 1, LANES)), jnp.float32),
            pltpu.VMEM((stations * here, components * (whole + 1) * LANES), jnp.bfloat16),
            pltpu.VMEM((stations * here, components * LANES), jnp.float32),
            pltpu.VMEM((stations * here, LANES), jnp.float32),
            pltpu.VMEM((stations * here, blocks * NK + LANES), jnp.bfloat16),
            pltpu.VMEM((per_group, blocks * NK + LANES), jnp.float32),
        ],
        compiler_params=pltpu.CompilerParams(vmem_limit_bytes=40 << 20),
        name="correlate",
    )(*([] if with_data else [samples]), chan_mask, *received)
    parts = [
        lax.ppermute(part, "stn", [(i, i ^ d) for i in range(owners)]) if d else part
        for d, part in zip(partners(owners), partial_stacks)
    ]
    return pl.pallas_call(
        functools.partial(finish_kernel, taps, blocks),
        out_shape=jax.ShapeDtypeStruct((blocks, TPD, NK), jnp.float32),
        compiler_params=pltpu.CompilerParams(vmem_limit_bytes=4 << 20),
        name="finish",
    )(*parts)


def solution(mesh):
    in_specs = (
        P(None, "stn", None, "tmpl"),
        P("stn", "tmpl", None, None),
        P("stn", "tmpl", None),
        P("stn", "tmpl"),
        P("stn", "tmpl"),
        P("stn", None),
    )
    out_specs = P(None, ("tmpl", "stn"), None)
    return jax.shard_map(body, mesh=mesh, in_specs=in_specs, out_specs=out_specs, check_vma=False)
```

```python
import functools

import jax
import jax.numpy as jnp
from jax import lax
from jax.experimental import pallas as pl
from jax.experimental.pallas import tpu as pltpu
from jax.sharding import PartitionSpec as P

NK = 256
TPD = 16
LANES = 128
SHIFTS = 16

epsilon = 1e-06


def ceil_to(value, multiple):
    return -(-value // multiple) * multiple


def quotient(values, divisor):
    if divisor & (divisor - 1):
        return values // divisor
    return lax.shift_right_logical(values, divisor.bit_length() - 1)


def remainder(values, divisor):
    if divisor & (divisor - 1):
        return values % divisor
    return values & (divisor - 1)


def partners(n):
    return [0] + list(range(n - 1, 0, -1))


def chips(n):
    return list(range(n - 2, 0, -2))


def column_of(row):
    n = row.shape[1]
    eye = lax.broadcasted_iota(jnp.int32, (n, n), 0) == lax.broadcasted_iota(jnp.int32, (n, n), 1)
    return jnp.sum(jnp.where(eye, jnp.broadcast_to(row, (n, n)), 0), axis=1, keepdims=True)


SMALL = 8
EXTRAS = 4


def chunk_plan(taps, components):
    whole = taps // LANES
    tail = taps - whole * LANES
    left = components * tail - LANES
    assert 0 < left <= min(tail, SMALL - 3)
    return whole, tail, left


def pack_kernel(dims, with_data, *refs):
    n, stations, slots, components, taps, most, rows = dims
    ins = refs[: 5 if with_data else 4]
    own_ref, core_ref, *chip_refs = refs[len(ins) : len(ins) + 1 + n // 2]
    held = refs[len(ins) + 1 + n // 2 : -1]
    sems = refs[-1]
    copies = [pltpu.make_async_copy(ins[i], held[i], sems.at[i]) for i in range(len(ins))]
    for copy in copies:
        copy.start()
    waves_ref, group_ref, local_ref, moveout_ref = held[-4:]
    count = stations * slots
    whole, tail, left = chunk_plan(taps, components)

    def flat(ref, three):
        pieces = [ref[s] if three else ref[s : s + 1, :] for s in range(stations)]
        return jnp.concatenate(pieces, axis=1)

    for copy in copies[-3:]:
        copy.wait()
    group = flat(group_ref, True)
    local = flat(local_ref, False)
    moveout = flat(moveout_ref, False)
    group_col = column_of(group)
    upper = lax.broadcasted_iota(jnp.int32, (count, count), 0)
    lower = lax.broadcasted_iota(jnp.int32, (count, count), 1)
    same = (quotient(upper, slots) == quotient(lower, slots)) & (upper < lower)
    rank = jnp.sum(jnp.where(same & (group_col == group), 1, 0), axis=0, keepdims=True)
    station = quotient(lax.broadcasted_iota(jnp.int32, (1, count), 1), slots)
    partner = group ^ lax.axis_index("tmpl")
    position = partner * rows + station * most + rank
    place = lax.broadcasted_iota(jnp.int32, (n * rows, count), 0) == position
    place = jnp.where(place, 1.0, 0.0).astype(jnp.bfloat16)

    lane = lax.broadcasted_iota(jnp.int32, (count, LANES), 1)
    meta = [column_of(local) + 1, column_of(quotient(moveout, LANES)), column_of(remainder(moveout, LANES))]

    for copy in copies[:-3]:
        copy.wait()
    waves = [
        jnp.concatenate([waves_ref[s * components + c] for s in range(stations)], axis=0)
        for c in range(components)
    ]
    placed = [
        jnp.dot(place, waves[c][:, : whole * LANES], preferred_element_type=jnp.float32)
        for c in range(components)
    ]
    ends = [waves[c][:, whole * LANES :] for c in range(components - 1)]
    ends.append(waves[-1][:, whole * LANES : taps - left])
    ends = jnp.dot(place, jnp.concatenate(ends, axis=1), preferred_element_type=jnp.float32)
    small = [waves[-1][:, taps - left + v : taps - left + v + 1] for v in range(left)] + meta
    spread = jnp.zeros((count, LANES), jnp.float32)
    for v, column in enumerate(small):
        spread = jnp.where(remainder(lane, SMALL) == v, column.astype(jnp.float32), spread)
    spread = jnp.dot(place, spread.astype(jnp.bfloat16), preferred_element_type=jnp.float32)
    each = LANES // SMALL
    within = remainder(lax.broadcasted_iota(jnp.int32, (rows, LANES), 0), each)
    within = within == quotient(lax.broadcasted_iota(jnp.int32, (rows, LANES), 1), SMALL)
    if with_data:
        samples = held[0][...].astype(jnp.float32)
        samples = samples.reshape(samples.shape[0] * samples.shape[1], LANES)
        samples = jnp.concatenate([samples, jnp.zeros((EXTRAS, LANES), jnp.float32)], axis=0)
    else:
        samples = jnp.zeros((8, LANES), jnp.float32)
    line = lax.broadcasted_iota(jnp.int32, samples.shape, 0)
    messages = [(own_ref, [0]), (core_ref, [1])]
    messages += [(ref, [d, d + 1]) for d, ref in zip(chips(n), chip_refs)]
    for send_ref, groups in messages:
        pieces, last = [], samples
        for g in groups:
            mine = slice(g * rows, (g + 1) * rows)
            for c in range(components):
                pieces += [placed[c][mine, a * LANES : (a + 1) * LANES] for a in range(whole)]
            pieces.append(ends[mine])
            kept = jnp.where(within, spread[mine], 0.0)
            for e in range(-(-rows // each)):
                packed = jnp.sum(kept[e * each : (e + 1) * each], axis=0, keepdims=True)
                last = jnp.where(line == samples.shape[0] - EXTRAS + 2 * (g % 2) + e, packed, last)
        pieces.append(last)
        extra = send_ref.shape[0] - sum(piece.shape[0] for piece in pieces)
        if extra:
            pieces.append(jnp.zeros((extra, LANES), jnp.float32))
        send_ref[...] = jnp.concatenate(pieces, axis=0).astype(jnp.bfloat16)


def correlate_kernel(dims, with_data, *refs):
    if with_data:
        mask_ref, *refs = refs
    else:
        data_ref, mask_ref, *refs = refs
    n, stations, blocks, components, taps, most, rows, width, per_group = dims
    own_ref, core_ref, *chip_refs = refs[:n]
    refs = refs[n:]
    come = [(own_ref, 0, 1), (core_ref, 0, 1)]
    for i in range(n // 2 - 1):
        come += [(chip_refs[i], 0, 2), (chip_refs[n // 2 - 1 + i], 1, 2)]
    distances = [0, 1]
    for d in chips(n):
        distances += [d, d + 1]
    *out_refs, x_ref, dsh_ref, rd_ref, ws_ref, rw_ref, meta_ref, sh_ref, stack_ref = refs
    whole, tail, left = chunk_plan(taps, components)
    chunks = whole + 1
    sent = components * whole + 1
    total = n * rows
    here = n * most
    lag_tiles = ceil_to(width - taps + 1, LANES) // LANES
    lag_width = lag_tiles * LANES
    series = stations * components * blocks
    series_rows = ceil_to(series, 8)

    def lines(ref, start, count):
        first = start // 16 * 16
        return ref[first : ceil_to(start + count, 16), :].astype(jnp.float32)[start - first :][:count]

    last_rows = series + EXTRAS if with_data else 8
    blocks_in = [lines(ref, half * sent * rows, sent * rows) for ref, half, _ in come]
    lasts = [lines(ref, count * sent * rows, last_rows) for ref, _, count in come]

    if with_data:
        for d, last in zip(distances, lasts):
            x_ref[lax.axis_index("tmpl") ^ d] = last
        x = jnp.concatenate([x_ref[i] for i in range(n)], axis=1)
    else:
        x = data_ref[...].astype(jnp.float32)
        x = jnp.concatenate([x, jnp.zeros((series_rows - series, width), jnp.float32)], axis=0)
    for r in range(SHIFTS):
        moved = pltpu.roll(x, width - r, 1) if r else x
        for t in range(width // LANES):
            dsh_ref[t, r * series_rows : (r + 1) * series_rows, :] = moved[:, t * LANES : (t + 1) * LANES]

    squares = jnp.concatenate([x * x, jnp.zeros((series_rows, chunks * LANES), jnp.float32)], axis=1)
    rounded = squares.astype(jnp.bfloat16).astype(jnp.float32)
    rest = squares - rounded
    reach = (chunks + 1) * LANES
    sample = lax.broadcasted_iota(jnp.int32, (reach, LANES), 0)
    sample = sample - lax.broadcasted_iota(jnp.int32, (reach, LANES), 1)
    ones = jnp.where((sample >= 0) & (sample < taps), 1.0, 0.0).astype(jnp.bfloat16)
    spans = [
        part[:, t * LANES : t * LANES + reach] for t in range(lag_tiles) for part in (rounded, rest)
    ]
    power = jnp.dot(jnp.concatenate(spans, axis=0).astype(jnp.bfloat16), ones, preferred_element_type=jnp.float32)
    power = [
        power[2 * t * series_rows : (2 * t + 1) * series_rows]
        + power[(2 * t + 1) * series_rows : (2 * t + 2) * series_rows]
        for t in range(lag_tiles)
    ]
    row = lax.broadcasted_iota(jnp.int32, (series_rows, LANES), 0)
    factor = jnp.zeros((series_rows, LANES), jnp.float32)
    for s in range(stations):
        used = [mask_ref[s, c] for c in range(components)]
        total_used = jnp.maximum(functools.reduce(lambda p, q: p + q, used), 1)
        for c in range(components):
            at = (s * components + c) * blocks
            mine = (row >= at) & (row < at + blocks)
            value = jnp.full((series_rows, LANES), used[c]).astype(jnp.float32)
            value = value / jnp.full((series_rows, LANES), total_used).astype(jnp.float32)
            factor = jnp.where(mine, value, factor)
    for t in range(lag_tiles):
        rd_ref[:, t * LANES : (t + 1) * LANES] = lax.rsqrt(power[t] / taps + epsilon) * factor

    target = lax.broadcasted_iota(jnp.int32, (stations * here, total), 0)
    source = lax.broadcasted_iota(jnp.int32, (stations * here, total), 1)
    wanted = (
        quotient(remainder(target, here), most) * rows
        + quotient(target, here) * most
        + remainder(target, most)
    )
    order = jnp.where(source == wanted, 1.0, 0.0).astype(jnp.bfloat16)
    lane = lax.broadcasted_iota(jnp.int32, (stations * here, LANES), 1)
    def received(k):
        piece = jnp.concatenate([blocks_in[i][k * rows : (k + 1) * rows] for i in range(n)], axis=0)
        return jnp.dot(order, piece.astype(jnp.bfloat16), preferred_element_type=jnp.float32)

    each = LANES // SMALL
    target = lax.broadcasted_iota(jnp.int32, (stations * here, n * 8), 0)
    place = quotient(target, here) * most + remainder(target, most)
    sender = quotient(remainder(target, here), most)
    line = sender * 8 + (8 - EXTRAS) + 2 * remainder(sender, 2) + quotient(place, each)
    line = lax.broadcasted_iota(jnp.int32, (stations * here, n * 8), 1) == line
    small = jnp.concatenate([last[last_rows - 8 :] for last in lasts], axis=0).astype(jnp.bfloat16)
    small = jnp.dot(
        jnp.where(line, 1.0, 0.0).astype(jnp.bfloat16), small, preferred_element_type=jnp.float32
    )
    target = lax.broadcasted_iota(jnp.int32, (stations * here, LANES), 0)
    place = remainder(quotient(target, here) * most + remainder(target, most), each)
    small = jnp.where(quotient(lane, SMALL) == place, small, 0.0).astype(jnp.bfloat16)
    fold = lax.broadcasted_iota(jnp.int32, (LANES, LANES), 0)
    fold = remainder(fold, SMALL) == lax.broadcasted_iota(jnp.int32, (LANES, LANES), 1)
    fold = jnp.where(fold, 1.0, 0.0).astype(jnp.bfloat16)
    meta_ref[...] = jnp.dot(small, fold, preferred_element_type=jnp.float32)

    ends = received(components * whole)
    for c in range(components):
        pieces = [received(c * whole + a) for a in range(whole)]
        end = pltpu.roll(ends, LANES - c * tail, 1) if c else ends
        if c == components - 1:
            end = jnp.where(lane < tail - left, end, pltpu.roll(meta_ref[...], tail - left, 1))
        pieces.append(jnp.where(lane < tail, end, 0.0))
        squares = functools.reduce(lambda p, q: p + q, [piece * piece for piece in pieces])
        for a in range(chunks):
            at = (c * chunks + a) * LANES
            ws_ref[:, at : at + LANES] = pieces[a].astype(jnp.bfloat16)
        wave_power = jnp.sum(squares, axis=1, keepdims=True) / taps
        rw_ref[:, c * LANES : (c + 1) * LANES] = jnp.broadcast_to(
            lax.rsqrt(wave_power + epsilon) / taps, (stations * here, LANES)
        )

    depth = (chunks - 1) * LANES + ceil_to(tail, 16)
    lane_here = lax.broadcasted_iota(jnp.int32, (here, LANES), 1)

    for s in range(stations):
        rows_here = slice(s * here, (s + 1) * here)
        meta = meta_ref[rows_here, :]
        tiles_over = jnp.broadcast_to(meta[:, left + 1 : left + 2], (here, LANES)).astype(jnp.int32)
        lanes_over = jnp.broadcast_to(meta[:, left + 2 : left + 3], (here, LANES)).astype(jnp.int32)
        index = lane_here + lanes_over
        within = lane_here >= lanes_over
        index = jnp.bitwise_and(index, LANES - 1)
        for b in range(blocks):
            total_corr = [jnp.zeros((here, LANES), jnp.float32) for _ in range(lag_tiles)]
            for c in range(components):
                at = (s * components + c) * blocks + b
                low = [
                    dsh_ref[t, pl.ds(at, SHIFTS, stride=series_rows), :] for t in range(width // LANES)
                ]
                low = jnp.concatenate(low, axis=1).astype(jnp.bfloat16)
                pieces = [low] + [pltpu.roll(low, width - q, 1) for q in range(SHIFTS, LANES, SHIFTS)]
                shifted = jnp.concatenate(pieces, axis=0)
                hankel = jnp.concatenate(
                    [
                        shifted[: min(LANES, depth - a * LANES), a * LANES : a * LANES + lag_width]
                        for a in range(chunks)
                    ],
                    axis=0,
                )
                w = ws_ref[rows_here, c * chunks * LANES : c * chunks * LANES + depth]
                numerator = jnp.dot(w, hankel, preferred_element_type=jnp.float32)
                over_wave = rw_ref[rows_here, c * LANES : (c + 1) * LANES]
                over_data = rd_ref[at : at + 1, :]
                for t in range(lag_tiles):
                    cut = slice(t * LANES, (t + 1) * LANES)
                    total_corr[t] = total_corr[t] + numerator[:, cut] * over_wave * over_data[:, cut]
            windows = []
            for t in range(NK // LANES + 1):
                window = total_corr[t]
                for h in range(1, lag_tiles - NK // LANES):
                    if t + h < lag_tiles:
                        window = jnp.where(tiles_over == h, total_corr[t + h], window)
                windows.append(window)
            for t in range(NK // LANES):
                aligned = jnp.where(within, windows[t], windows[t + 1])
                aligned = jnp.take_along_axis(aligned, index, axis=1)
                at = b * NK + t * LANES
                sh_ref[rows_here, at : at + LANES] = aligned.astype(jnp.bfloat16)

    slot = lax.broadcasted_iota(jnp.int32, (stations * here, LANES), 0)
    half = (slot < stations * here // 2) == (lane < LANES // 2)
    sh_ref[:, blocks * NK :] = jnp.where(half, 1.0, 0.0).astype(jnp.bfloat16)
    local = meta_ref[:, left : left + 1].astype(jnp.int32) - 1
    template = lax.broadcasted_iota(jnp.int32, (stations * here, per_group), 1)
    onehot = jnp.where(local == template, 1.0, 0.0).astype(jnp.bfloat16)
    stack_ref[...] = lax.dot_general(
        onehot, sh_ref[...], (((0,), (0,)), ((), ())), preferred_element_type=jnp.float32
    )
    me = lax.axis_index("stn")
    for d, out_ref in zip(partners(len(out_refs)), out_refs):
        owner = me ^ d
        theirs = pl.ds(pl.multiple_of(owner * TPD, TPD), TPD)
        out_ref[...] = stack_ref[theirs, :].astype(jnp.bfloat16)


def finish_kernel(taps, blocks, *refs):
    *parts_refs, out_ref = refs
    total = functools.reduce(lambda p, q: p + q, [ref[...].astype(jnp.float32) for ref in parts_refs])
    first, middle = blocks * NK, blocks * NK + LANES // 2
    count = total[:, first : first + 1] + total[:, middle : middle + 1]
    scale = jnp.sqrt(jnp.float32(taps)) / jnp.sqrt(jnp.maximum(count, 1.0))
    for b in range(blocks):
        out_ref[b] = total[:, b * NK : (b + 1) * NK] * scale


def body(data, waves, slot_group, slot_local, moveout, chan_mask):
    blocks, stations, components, width_here = data.shape
    slots, taps = waves.shape[1], waves.shape[3]
    n = lax.axis_size("tmpl")
    owners = lax.axis_size("stn")
    per_group = TPD * owners
    width = width_here * n
    most = max(2, 2 * slots // n)
    rows = ceil_to(stations * most, 8)
    whole, tail, left = chunk_plan(taps, components)
    series = stations * components * blocks
    series_rows = ceil_to(series, 8)
    with_data = width_here == LANES
    here = n * most

    waves = jnp.transpose(waves, (0, 2, 1, 3)).reshape(stations * components, slots, taps)
    groups = jnp.transpose(slot_group, (0, 2, 1))
    samples = jnp.transpose(data, (1, 2, 0, 3)).reshape(stations * components, blocks, width_here)
    last_rows = series + EXTRAS if with_data else 8
    message_rows = [ceil_to(k * (components * whole + 1) * rows + last_rows, 16) for k in (1, 1)]
    message_rows += [ceil_to(2 * (components * whole + 1) * rows + last_rows, 16)] * (n // 2 - 1)
    ins = ([samples] if with_data else []) + [waves, groups, slot_local, moveout]
    ins = [pltpu.with_memory_space_constraint(x, pltpu.HBM) for x in ins]
    send = pl.pallas_call(
        functools.partial(
            pack_kernel, (n, stations, slots, components, taps, most, rows), with_data
        ),
        out_shape=[jax.ShapeDtypeStruct((k, LANES), jnp.bfloat16) for k in message_rows],
        in_specs=[pl.BlockSpec(memory_space=pltpu.HBM)] * len(ins),
        scratch_shapes=[pltpu.VMEM(x.shape, x.dtype) for x in ins]
        + [pltpu.SemaphoreType.DMA((len(ins),))],
        compiler_params=pltpu.CompilerParams(vmem_limit_bytes=24 << 20),
        name="pack",
    )(*ins)
    def swap(block, d):
        return lax.ppermute(block, "tmpl", [(i, i ^ d) for i in range(n)])

    own, for_core, *for_chips = send
    from_chips = [swap(block, d) for d, block in zip(chips(n), for_chips)]
    from_core = swap(for_core, 1)
    if from_chips:
        from_chips[0], from_core = lax.optimization_barrier((from_chips[0], from_core))
    received = [own, from_core] + from_chips + [swap(block, 1) for block in from_chips]
    if not with_data:
        samples = lax.all_gather(samples.reshape(series, width_here), "tmpl", axis=1, tiled=True)
    vmem = pl.BlockSpec(memory_space=pltpu.VMEM)
    partial_stacks = pl.pallas_call(
        functools.partial(
            correlate_kernel,
            (n, stations, blocks, components, taps, most, rows, width, per_group),
            with_data,
        ),
        out_shape=[jax.ShapeDtypeStruct((TPD, blocks * NK + LANES), jnp.bfloat16)] * owners,
        in_specs=[vmem] * (0 if with_data else 1) + [pl.BlockSpec(memory_space=pltpu.SMEM)] + [vmem] * n,
        scratch_shapes=[
            pltpu.VMEM((width // LANES, series_rows, LANES), jnp.float32),
            pltpu.VMEM((width // LANES, SHIFTS * series_rows, LANES), jnp.float32),
            pltpu.VMEM((series_rows, ceil_to(width - taps + 1, LANES)), jnp.float32),
            pltpu.VMEM((stations * here, components * (whole + 1) * LANES), jnp.bfloat16),
            pltpu.VMEM((stations * here, components * LANES), jnp.float32),
            pltpu.VMEM((stations * here, LANES), jnp.float32),
            pltpu.VMEM((stations * here, blocks * NK + LANES), jnp.bfloat16),
            pltpu.VMEM((per_group, blocks * NK + LANES), jnp.float32),
        ],
        compiler_params=pltpu.CompilerParams(vmem_limit_bytes=40 << 20),
        name="correlate",
    )(*([] if with_data else [samples]), chan_mask, *received)
    parts = [
        lax.ppermute(part, "stn", [(i, i ^ d) for i in range(owners)]) if d else part
        for d, part in zip(partners(owners), partial_stacks)
    ]
    return pl.pallas_call(
        functools.partial(finish_kernel, taps, blocks),
        out_shape=jax.ShapeDtypeStruct((blocks, TPD, NK), jnp.float32),
        compiler_params=pltpu.CompilerParams(vmem_limit_bytes=4 << 20),
        name="finish",
    )(*parts)


def solution(mesh):
    in_specs = (
        P(None, "stn", None, "tmpl"),
        P("stn", "tmpl", None, None),
        P("stn", "tmpl", None),
        P("stn", "tmpl"),
        P("stn", "tmpl"),
        P("stn", None),
    )
    out_specs = P(None, ("tmpl", "stn"), None)
    return jax.shard_map(body, mesh=mesh, in_specs=in_specs, out_specs=out_specs, check_vma=False)
```

```python
import functools

import jax
import jax.numpy as jnp
from jax import lax
from jax.experimental import pallas as pl
from jax.experimental.pallas import tpu as pltpu
from jax.sharding import PartitionSpec as P

NK = 256
TPD = 16
LANES = 128
SHIFTS = 16

epsilon = 1e-06


def ceil_to(value, multiple):
    return -(-value // multiple) * multiple


def quotient(values, divisor):
    if divisor & (divisor - 1):
        return values // divisor
    return lax.shift_right_logical(values, divisor.bit_length() - 1)


def remainder(values, divisor):
    if divisor & (divisor - 1):
        return values % divisor
    return values & (divisor - 1)


def halvings(n):
    order, step = [0], n
    while step > 1:
        step = step // 2
        order = order + [d + n // (2 * step) for d in order]
    return [int(format(d, "b").zfill(n.bit_length() - 1)[::-1], 2) if n > 1 else 0 for d in order]


def chips(n):
    return list(range(n - 2, 0, -2))


def column_of(row):
    n = row.shape[1]
    eye = lax.broadcasted_iota(jnp.int32, (n, n), 0) == lax.broadcasted_iota(jnp.int32, (n, n), 1)
    return jnp.sum(jnp.where(eye, jnp.broadcast_to(row, (n, n)), 0), axis=1, keepdims=True)


SMALL = 8
EXTRAS = 4


def chunk_plan(taps, components):
    whole = taps // LANES
    tail = taps - whole * LANES
    left = components * tail - LANES
    assert 0 < left <= min(tail, SMALL - 3)
    return whole, tail, left


def pack_kernel(dims, with_data, *refs):
    n, stations, slots, components, taps, most, rows = dims
    ins = refs[: 5 if with_data else 4]
    own_ref, core_ref, *chip_refs = refs[len(ins) : len(ins) + 1 + n // 2]
    held = refs[len(ins) + 1 + n // 2 : -1]
    sems = refs[-1]
    copies = [pltpu.make_async_copy(ins[i], held[i], sems.at[i]) for i in range(len(ins))]
    for copy in copies:
        copy.start()
    waves_ref, group_ref, local_ref, moveout_ref = held[-4:]
    count = stations * slots
    whole, tail, left = chunk_plan(taps, components)

    def flat(ref, three):
        pieces = [ref[s] if three else ref[s : s + 1, :] for s in range(stations)]
        return jnp.concatenate(pieces, axis=1)

    for copy in copies[-3:]:
        copy.wait()
    group = flat(group_ref, True)
    local = flat(local_ref, False)
    moveout = flat(moveout_ref, False)
    group_col = column_of(group)
    upper = lax.broadcasted_iota(jnp.int32, (count, count), 0)
    lower = lax.broadcasted_iota(jnp.int32, (count, count), 1)
    same = (quotient(upper, slots) == quotient(lower, slots)) & (upper < lower)
    rank = jnp.sum(jnp.where(same & (group_col == group), 1, 0), axis=0, keepdims=True)
    station = quotient(lax.broadcasted_iota(jnp.int32, (1, count), 1), slots)
    partner = group ^ lax.axis_index("tmpl")
    position = partner * rows + station * most + rank
    place = lax.broadcasted_iota(jnp.int32, (n * rows, count), 0) == position
    place = jnp.where(place, 1.0, 0.0).astype(jnp.bfloat16)

    lane = lax.broadcasted_iota(jnp.int32, (count, LANES), 1)
    meta = [column_of(local) + 1, column_of(quotient(moveout, LANES)), column_of(remainder(moveout, LANES))]

    for copy in copies[:-3]:
        copy.wait()
    waves = [
        jnp.concatenate([waves_ref[s * components + c] for s in range(stations)], axis=0)
        for c in range(components)
    ]
    placed = [
        jnp.dot(place, waves[c][:, : whole * LANES], preferred_element_type=jnp.float32)
        for c in range(components)
    ]
    ends = [waves[c][:, whole * LANES :] for c in range(components - 1)]
    ends.append(waves[-1][:, whole * LANES : taps - left])
    ends = jnp.dot(place, jnp.concatenate(ends, axis=1), preferred_element_type=jnp.float32)
    small = [waves[-1][:, taps - left + v : taps - left + v + 1] for v in range(left)] + meta
    spread = jnp.zeros((count, LANES), jnp.float32)
    for v, column in enumerate(small):
        spread = jnp.where(remainder(lane, SMALL) == v, column.astype(jnp.float32), spread)
    spread = jnp.dot(place, spread.astype(jnp.bfloat16), preferred_element_type=jnp.float32)
    each = LANES // SMALL
    within = remainder(lax.broadcasted_iota(jnp.int32, (rows, LANES), 0), each)
    within = within == quotient(lax.broadcasted_iota(jnp.int32, (rows, LANES), 1), SMALL)
    if with_data:
        samples = held[0][...].astype(jnp.float32)
        samples = samples.reshape(samples.shape[0] * samples.shape[1], LANES)
        samples = jnp.concatenate([samples, jnp.zeros((EXTRAS, LANES), jnp.float32)], axis=0)
    else:
        samples = jnp.zeros((8, LANES), jnp.float32)
    line = lax.broadcasted_iota(jnp.int32, samples.shape, 0)
    messages = [(own_ref, [0]), (core_ref, [1])]
    messages += [(ref, [d, d + 1]) for d, ref in zip(chips(n), chip_refs)]
    for send_ref, groups in messages:
        pieces, last = [], samples
        for g in groups:
            mine = slice(g * rows, (g + 1) * rows)
            for c in range(components):
                pieces += [placed[c][mine, a * LANES : (a + 1) * LANES] for a in range(whole)]
            pieces.append(ends[mine])
            kept = jnp.where(within, spread[mine], 0.0)
            for e in range(-(-rows // each)):
                packed = jnp.sum(kept[e * each : (e + 1) * each], axis=0, keepdims=True)
                last = jnp.where(line == samples.shape[0] - EXTRAS + 2 * (g % 2) + e, packed, last)
        pieces.append(last)
        extra = send_ref.shape[0] - sum(piece.shape[0] for piece in pieces)
        if extra:
            pieces.append(jnp.zeros((extra, LANES), jnp.float32))
        send_ref[...] = jnp.concatenate(pieces, axis=0).astype(jnp.bfloat16)


def correlate_kernel(dims, with_data, *refs):
    if with_data:
        mask_ref, *refs = refs
    else:
        data_ref, mask_ref, *refs = refs
    n, stations, blocks, components, taps, most, rows, width, per_group = dims
    keep = max(1, per_group // TPD // 2)
    own_ref, core_ref, *chip_refs = refs[:n]
    refs = refs[n:]
    come = [(own_ref, 0, 1), (core_ref, 0, 1)]
    for i in range(n // 2 - 1):
        come += [(chip_refs[i], 0, 2), (chip_refs[n // 2 - 1 + i], 1, 2)]
    distances = [0, 1]
    for d in chips(n):
        distances += [d, d + 1]
    *out_refs, x_ref, dsh_ref, rd_ref, ws_ref, rw_ref, meta_ref, sh_ref, stack_ref = refs
    whole, tail, left = chunk_plan(taps, components)
    chunks = whole + 1
    sent = components * whole + 1
    total = n * rows
    here = n * most
    lag_tiles = ceil_to(width - taps + 1, LANES) // LANES
    lag_width = lag_tiles * LANES
    series = stations * components * blocks
    series_rows = ceil_to(series, 8)

    def lines(ref, start, count):
        first = start // 16 * 16
        return ref[first : ceil_to(start + count, 16), :].astype(jnp.float32)[start - first :][:count]

    last_rows = series + EXTRAS if with_data else 8
    blocks_in = [lines(ref, half * sent * rows, sent * rows) for ref, half, _ in come]
    lasts = [lines(ref, count * sent * rows, last_rows) for ref, _, count in come]

    if with_data:
        for d, last in zip(distances, lasts):
            x_ref[lax.axis_index("tmpl") ^ d] = last
        x = jnp.concatenate([x_ref[i] for i in range(n)], axis=1)
    else:
        x = data_ref[...].astype(jnp.float32)
        x = jnp.concatenate([x, jnp.zeros((series_rows - series, width), jnp.float32)], axis=0)
    for r in range(SHIFTS):
        moved = pltpu.roll(x, width - r, 1) if r else x
        for t in range(width // LANES):
            dsh_ref[t, r * series_rows : (r + 1) * series_rows, :] = moved[:, t * LANES : (t + 1) * LANES]

    squares = jnp.concatenate([x * x, jnp.zeros((series_rows, chunks * LANES), jnp.float32)], axis=1)
    rounded = squares.astype(jnp.bfloat16).astype(jnp.float32)
    rest = squares - rounded
    reach = (chunks + 1) * LANES
    sample = lax.broadcasted_iota(jnp.int32, (reach, LANES), 0)
    sample = sample - lax.broadcasted_iota(jnp.int32, (reach, LANES), 1)
    ones = jnp.where((sample >= 0) & (sample < taps), 1.0, 0.0).astype(jnp.bfloat16)
    spans = [
        part[:, t * LANES : t * LANES + reach] for t in range(lag_tiles) for part in (rounded, rest)
    ]
    power = jnp.dot(jnp.concatenate(spans, axis=0).astype(jnp.bfloat16), ones, preferred_element_type=jnp.float32)
    power = [
        power[2 * t * series_rows : (2 * t + 1) * series_rows]
        + power[(2 * t + 1) * series_rows : (2 * t + 2) * series_rows]
        for t in range(lag_tiles)
    ]
    row = lax.broadcasted_iota(jnp.int32, (series_rows, LANES), 0)
    factor = jnp.zeros((series_rows, LANES), jnp.float32)
    for s in range(stations):
        used = [mask_ref[s, c] for c in range(components)]
        total_used = jnp.maximum(functools.reduce(lambda p, q: p + q, used), 1)
        for c in range(components):
            at = (s * components + c) * blocks
            mine = (row >= at) & (row < at + blocks)
            value = jnp.full((series_rows, LANES), used[c]).astype(jnp.float32)
            value = value / jnp.full((series_rows, LANES), total_used).astype(jnp.float32)
            factor = jnp.where(mine, value, factor)
    for t in range(lag_tiles):
        rd_ref[:, t * LANES : (t + 1) * LANES] = lax.rsqrt(power[t] / taps + epsilon) * factor

    target = lax.broadcasted_iota(jnp.int32, (stations * here, total), 0)
    source = lax.broadcasted_iota(jnp.int32, (stations * here, total), 1)
    wanted = (
        quotient(remainder(target, here), most) * rows
        + quotient(target, here) * most
        + remainder(target, most)
    )
    order = jnp.where(source == wanted, 1.0, 0.0).astype(jnp.bfloat16)
    lane = lax.broadcasted_iota(jnp.int32, (stations * here, LANES), 1)
    def received(k):
        piece = jnp.concatenate([blocks_in[i][k * rows : (k + 1) * rows] for i in range(n)], axis=0)
        return jnp.dot(order, piece.astype(jnp.bfloat16), preferred_element_type=jnp.float32)

    each = LANES // SMALL
    target = lax.broadcasted_iota(jnp.int32, (stations * here, n * 8), 0)
    place = quotient(target, here) * most + remainder(target, most)
    sender = quotient(remainder(target, here), most)
    line = sender * 8 + (8 - EXTRAS) + 2 * remainder(sender, 2) + quotient(place, each)
    line = lax.broadcasted_iota(jnp.int32, (stations * here, n * 8), 1) == line
    small = jnp.concatenate([last[last_rows - 8 :] for last in lasts], axis=0).astype(jnp.bfloat16)
    small = jnp.dot(
        jnp.where(line, 1.0, 0.0).astype(jnp.bfloat16), small, preferred_element_type=jnp.float32
    )
    target = lax.broadcasted_iota(jnp.int32, (stations * here, LANES), 0)
    place = remainder(quotient(target, here) * most + remainder(target, most), each)
    small = jnp.where(quotient(lane, SMALL) == place, small, 0.0).astype(jnp.bfloat16)
    fold = lax.broadcasted_iota(jnp.int32, (LANES, LANES), 0)
    fold = remainder(fold, SMALL) == lax.broadcasted_iota(jnp.int32, (LANES, LANES), 1)
    fold = jnp.where(fold, 1.0, 0.0).astype(jnp.bfloat16)
    meta_ref[...] = jnp.dot(small, fold, preferred_element_type=jnp.float32)

    ends = received(components * whole)
    for c in range(components):
        pieces = [received(c * whole + a) for a in range(whole)]
        end = pltpu.roll(ends, LANES - c * tail, 1) if c else ends
        if c == components - 1:
            end = jnp.where(lane < tail - left, end, pltpu.roll(meta_ref[...], tail - left, 1))
        pieces.append(jnp.where(lane < tail, end, 0.0))
        squares = functools.reduce(lambda p, q: p + q, [piece * piece for piece in pieces])
        for a in range(chunks):
            at = (c * chunks + a) * LANES
            ws_ref[:, at : at + LANES] = pieces[a].astype(jnp.bfloat16)
        wave_power = jnp.sum(squares, axis=1, keepdims=True) / taps
        rw_ref[:, c * LANES : (c + 1) * LANES] = jnp.broadcast_to(
            lax.rsqrt(wave_power + epsilon) / taps, (stations * here, LANES)
        )

    depth = (chunks - 1) * LANES + ceil_to(tail, 16)
    lane_here = lax.broadcasted_iota(jnp.int32, (here, LANES), 1)

    for s in range(stations):
        rows_here = slice(s * here, (s + 1) * here)
        meta = meta_ref[rows_here, :]
        tiles_over = jnp.broadcast_to(meta[:, left + 1 : left + 2], (here, LANES)).astype(jnp.int32)
        lanes_over = jnp.broadcast_to(meta[:, left + 2 : left + 3], (here, LANES)).astype(jnp.int32)
        index = lane_here + lanes_over
        within = lane_here >= lanes_over
        index = jnp.bitwise_and(index, LANES - 1)
        for b in range(blocks):
            total_corr = [jnp.zeros((here, LANES), jnp.float32) for _ in range(lag_tiles)]
            for c in range(components):
                at = (s * components + c) * blocks + b
                low = [
                    dsh_ref[t, pl.ds(at, SHIFTS, stride=series_rows), :] for t in range(width // LANES)
                ]
                low = jnp.concatenate(low, axis=1).astype(jnp.bfloat16)
                pieces = [low] + [pltpu.roll(low, width - q, 1) for q in range(SHIFTS, LANES, SHIFTS)]
                shifted = jnp.concatenate(pieces, axis=0)
                hankel = jnp.concatenate(
                    [
                        shifted[: min(LANES, depth - a * LANES), a * LANES : a * LANES + lag_width]
                        for a in range(chunks)
                    ],
                    axis=0,
                )
                w = ws_ref[rows_here, c * chunks * LANES : c * chunks * LANES + depth]
                numerator = jnp.dot(w, hankel, preferred_element_type=jnp.float32)
                over_wave = rw_ref[rows_here, c * LANES : (c + 1) * LANES]
                over_data = rd_ref[at : at + 1, :]
                for t in range(lag_tiles):
                    cut = slice(t * LANES, (t + 1) * LANES)
                    total_corr[t] = total_corr[t] + numerator[:, cut] * over_wave * over_data[:, cut]
            windows = []
            for t in range(NK // LANES + 1):
                window = total_corr[t]
                for h in range(1, lag_tiles - NK // LANES):
                    if t + h < lag_tiles:
                        window = jnp.where(tiles_over == h, total_corr[t + h], window)
                windows.append(window)
            for t in range(NK // LANES):
                aligned = jnp.where(within, windows[t], windows[t + 1])
                aligned = jnp.take_along_axis(aligned, index, axis=1)
                at = b * NK + t * LANES
                sh_ref[rows_here, at : at + LANES] = aligned.astype(jnp.bfloat16)

    slot = lax.broadcasted_iota(jnp.int32, (stations * here, LANES), 0)
    half = (slot < stations * here // 2) == (lane < LANES // 2)
    sh_ref[:, blocks * NK :] = jnp.where(half, 1.0, 0.0).astype(jnp.bfloat16)
    local = meta_ref[:, left : left + 1].astype(jnp.int32) - 1
    template = lax.broadcasted_iota(jnp.int32, (stations * here, per_group), 1)
    onehot = jnp.where(local == template, 1.0, 0.0).astype(jnp.bfloat16)
    stack_ref[...] = lax.dot_general(
        onehot, sh_ref[...], (((0,), (0,)), ((), ())), preferred_element_type=jnp.float32
    )
    me = lax.axis_index("stn")
    for i, d in enumerate(halvings(per_group // TPD)):
        theirs = pl.ds(pl.multiple_of((me ^ d) * TPD, TPD), TPD)
        out_ref = out_refs[i // keep]
        at = i % keep * TPD
        out_ref[at : at + TPD, :] = stack_ref[theirs, :].astype(out_ref.dtype)


def add_kernel(blocks, kept_ref, came_ref, keep_ref, send_ref):
    total = kept_ref[...] + came_ref[...].astype(jnp.float32)
    count = total[:, blocks * NK :]
    count = count + pltpu.roll(count, LANES // 2, 1)
    high = jnp.floor(count * (1.0 / LANES)) * LANES
    lane = lax.broadcasted_iota(jnp.int32, count.shape, 1)
    count = jnp.where(lane < LANES // 2, count - high, high)
    total = jnp.concatenate([total[:, : blocks * NK], count], axis=1)
    half = keep_ref.shape[0]
    keep_ref[...] = total[:half]
    send_ref[...] = total[half:].astype(send_ref.dtype)


def finish_kernel(taps, blocks, *refs):
    *parts_refs, out_ref = refs
    total = functools.reduce(lambda p, q: p + q, [ref[...].astype(jnp.float32) for ref in parts_refs])
    first, middle = blocks * NK, blocks * NK + LANES // 2
    count = total[:, first : first + 1] + total[:, middle : middle + 1]
    scale = jnp.sqrt(jnp.float32(taps)) / jnp.sqrt(jnp.maximum(count, 1.0))
    for b in range(blocks):
        out_ref[b] = total[:, b * NK : (b + 1) * NK] * scale


def body(data, waves, slot_group, slot_local, moveout, chan_mask):
    blocks, stations, components, width_here = data.shape
    slots, taps = waves.shape[1], waves.shape[3]
    n = lax.axis_size("tmpl")
    owners = lax.axis_size("stn")
    per_group = TPD * owners
    keep = max(1, owners // 2)
    width = width_here * n
    most = max(2, 2 * slots // n)
    rows = ceil_to(stations * most, 8)
    whole, tail, left = chunk_plan(taps, components)
    series = stations * components * blocks
    series_rows = ceil_to(series, 8)
    with_data = width_here == LANES
    here = n * most

    waves = jnp.transpose(waves, (0, 2, 1, 3)).reshape(stations * components, slots, taps)
    groups = jnp.transpose(slot_group, (0, 2, 1))
    samples = jnp.transpose(data, (1, 2, 0, 3)).reshape(stations * components, blocks, width_here)
    last_rows = series + EXTRAS if with_data else 8
    message_rows = [ceil_to(k * (components * whole + 1) * rows + last_rows, 16) for k in (1, 1)]
    message_rows += [ceil_to(2 * (components * whole + 1) * rows + last_rows, 16)] * (n // 2 - 1)
    ins = ([samples] if with_data else []) + [waves, groups, slot_local, moveout]
    ins = [pltpu.with_memory_space_constraint(x, pltpu.HBM) for x in ins]
    send = pl.pallas_call(
        functools.partial(
            pack_kernel, (n, stations, slots, components, taps, most, rows), with_data
        ),
        out_shape=[jax.ShapeDtypeStruct((k, LANES), jnp.bfloat16) for k in message_rows],
        in_specs=[pl.BlockSpec(memory_space=pltpu.HBM)] * len(ins),
        scratch_shapes=[pltpu.VMEM(x.shape, x.dtype) for x in ins]
        + [pltpu.SemaphoreType.DMA((len(ins),))],
        compiler_params=pltpu.CompilerParams(vmem_limit_bytes=24 << 20),
        name="pack",
    )(*ins)
    def swap(block, d):
        return lax.ppermute(block, "tmpl", [(i, i ^ d) for i in range(n)])

    own, for_core, *for_chips = send
    from_chips = [swap(block, d) for d, block in zip(chips(n), for_chips)]
    from_core = swap(for_core, 1)
    if from_chips:
        from_chips[0], from_core = lax.optimization_barrier((from_chips[0], from_core))
    received = [own, from_core] + from_chips + [swap(block, 1) for block in from_chips]
    if not with_data:
        samples = lax.all_gather(samples.reshape(series, width_here), "tmpl", axis=1, tiled=True)
    vmem = pl.BlockSpec(memory_space=pltpu.VMEM)
    partial_stacks = pl.pallas_call(
        functools.partial(
            correlate_kernel,
            (n, stations, blocks, components, taps, most, rows, width, per_group),
            with_data,
        ),
        out_shape=[
            jax.ShapeDtypeStruct((keep * TPD, blocks * NK + LANES), held)
            for held in ([jnp.float32, jnp.bfloat16] if owners > 1 else [jnp.float32])
        ],
        in_specs=[vmem] * (0 if with_data else 1) + [pl.BlockSpec(memory_space=pltpu.SMEM)] + [vmem] * n,
        scratch_shapes=[
            pltpu.VMEM((width // LANES, series_rows, LANES), jnp.float32),
            pltpu.VMEM((width // LANES, SHIFTS * series_rows, LANES), jnp.float32),
            pltpu.VMEM((series_rows, ceil_to(width - taps + 1, LANES)), jnp.float32),
            pltpu.VMEM((stations * here, components * (whole + 1) * LANES), jnp.bfloat16),
            pltpu.VMEM((stations * here, components * LANES), jnp.float32),
            pltpu.VMEM((stations * here, LANES), jnp.float32),
            pltpu.VMEM((stations * here, blocks * NK + LANES), jnp.bfloat16),
            pltpu.VMEM((per_group, blocks * NK + LANES), jnp.float32),
        ],
        compiler_params=pltpu.CompilerParams(vmem_limit_bytes=40 << 20),
        name="correlate",
    )(*([] if with_data else [samples]), chan_mask, *received)
    small = pltpu.CompilerParams(vmem_limit_bytes=4 << 20)
    parts = list(partial_stacks)
    distance = 1
    while distance < owners:
        step = [(i, i ^ distance) for i in range(owners)]
        parts[1] = lax.ppermute(parts[1], "stn", step)
        distance = 2 * distance
        if distance < owners:
            keep = keep // 2
            parts = pl.pallas_call(
                functools.partial(add_kernel, blocks),
                out_shape=[
                    jax.ShapeDtypeStruct((keep * TPD, blocks * NK + LANES), held)
                    for held in (jnp.float32, jnp.bfloat16)
                ],
                compiler_params=small,
                name="add",
            )(*parts)
            parts = list(parts)
    return pl.pallas_call(
        functools.partial(finish_kernel, taps, blocks),
        out_shape=jax.ShapeDtypeStruct((blocks, TPD, NK), jnp.float32),
        compiler_params=small,
        name="finish",
    )(*parts)


def solution(mesh):
    in_specs = (
        P(None, "stn", None, "tmpl"),
        P("stn", "tmpl", None, None),
        P("stn", "tmpl", None),
        P("stn", "tmpl"),
        P("stn", "tmpl"),
        P("stn", None),
    )
    out_specs = P(None, ("tmpl", "stn"), None)
    return jax.shard_map(body, mesh=mesh, in_specs=in_specs, out_specs=out_specs, check_vma=False)
```

```python
import functools

import jax
import jax.numpy as jnp
from jax import lax
from jax.experimental import pallas as pl
from jax.experimental.pallas import tpu as pltpu
from jax.sharding import PartitionSpec as P

NK = 256
TPD = 16
LANES = 128
SHIFTS = 16

epsilon = 1e-06


def ceil_to(value, multiple):
    return -(-value // multiple) * multiple


def quotient(values, divisor):
    if divisor & (divisor - 1):
        return values // divisor
    return lax.shift_right_logical(values, divisor.bit_length() - 1)


def remainder(values, divisor):
    if divisor & (divisor - 1):
        return values % divisor
    return values & (divisor - 1)


def chips(n):
    return list(range(n - 2, 0, -2))


def column_of(row):
    n = row.shape[1]
    eye = lax.broadcasted_iota(jnp.int32, (n, n), 0) == lax.broadcasted_iota(jnp.int32, (n, n), 1)
    return jnp.sum(jnp.where(eye, jnp.broadcast_to(row, (n, n)), 0), axis=1, keepdims=True)


SMALL = 8
EXTRAS = 4


def chunk_plan(taps, components):
    whole = taps // LANES
    tail = taps - whole * LANES
    left = components * tail - LANES
    assert 0 < left <= min(tail, SMALL - 3)
    return whole, tail, left


def pack_kernel(dims, with_data, *refs):
    n, stations, slots, components, taps, most, rows = dims
    ins = refs[: 5 if with_data else 4]
    own_ref, core_ref, *chip_refs = refs[len(ins) : len(ins) + 1 + n // 2]
    held = refs[len(ins) + 1 + n // 2 : -1]
    sems = refs[-1]
    copies = [pltpu.make_async_copy(ins[i], held[i], sems.at[i]) for i in range(len(ins))]
    for copy in copies:
        copy.start()
    waves_ref, group_ref, local_ref, moveout_ref = held[-4:]
    count = stations * slots
    whole, tail, left = chunk_plan(taps, components)

    def flat(ref, three):
        pieces = [ref[s] if three else ref[s : s + 1, :] for s in range(stations)]
        return jnp.concatenate(pieces, axis=1)

    for copy in copies[-3:]:
        copy.wait()
    group = flat(group_ref, True)
    local = flat(local_ref, False)
    moveout = flat(moveout_ref, False)
    group_col = column_of(group)
    upper = lax.broadcasted_iota(jnp.int32, (count, count), 0)
    lower = lax.broadcasted_iota(jnp.int32, (count, count), 1)
    same = (quotient(upper, slots) == quotient(lower, slots)) & (upper < lower)
    rank = jnp.sum(jnp.where(same & (group_col == group), 1, 0), axis=0, keepdims=True)
    station = quotient(lax.broadcasted_iota(jnp.int32, (1, count), 1), slots)
    partner = group ^ lax.axis_index("tmpl")
    position = partner * rows + station * most + rank
    place = lax.broadcasted_iota(jnp.int32, (n * rows, count), 0) == position
    place = jnp.where(place, 1.0, 0.0).astype(jnp.bfloat16)

    lane = lax.broadcasted_iota(jnp.int32, (count, LANES), 1)
    meta = [column_of(local) + 1, column_of(quotient(moveout, LANES)), column_of(remainder(moveout, LANES))]

    for copy in copies[:-3]:
        copy.wait()
    waves = [
        jnp.concatenate([waves_ref[s * components + c] for s in range(stations)], axis=0)
        for c in range(components)
    ]
    placed = [
        jnp.dot(place, waves[c][:, : whole * LANES], preferred_element_type=jnp.float32)
        for c in range(components)
    ]
    ends = [waves[c][:, whole * LANES :] for c in range(components - 1)]
    ends.append(waves[-1][:, whole * LANES : taps - left])
    ends = jnp.dot(place, jnp.concatenate(ends, axis=1), preferred_element_type=jnp.float32)
    small = [waves[-1][:, taps - left + v : taps - left + v + 1] for v in range(left)] + meta
    spread = jnp.zeros((count, LANES), jnp.float32)
    for v, column in enumerate(small):
        spread = jnp.where(remainder(lane, SMALL) == v, column.astype(jnp.float32), spread)
    spread = jnp.dot(place, spread.astype(jnp.bfloat16), preferred_element_type=jnp.float32)
    each = LANES // SMALL
    within = remainder(lax.broadcasted_iota(jnp.int32, (rows, LANES), 0), each)
    within = within == quotient(lax.broadcasted_iota(jnp.int32, (rows, LANES), 1), SMALL)
    if with_data:
        samples = held[0][...].astype(jnp.float32)
        samples = samples.reshape(samples.shape[0] * samples.shape[1], LANES)
        samples = jnp.concatenate([samples, jnp.zeros((EXTRAS, LANES), jnp.float32)], axis=0)
    else:
        samples = jnp.zeros((8, LANES), jnp.float32)
    line = lax.broadcasted_iota(jnp.int32, samples.shape, 0)
    messages = [(own_ref, [0]), (core_ref, [1])]
    messages += [(ref, [d, d + 1]) for d, ref in zip(chips(n), chip_refs)]
    for send_ref, groups in messages:
        pieces, last = [], samples
        for g in groups:
            mine = slice(g * rows, (g + 1) * rows)
            for c in range(components):
                pieces += [placed[c][mine, a * LANES : (a + 1) * LANES] for a in range(whole)]
            pieces.append(ends[mine])
            kept = jnp.where(within, spread[mine], 0.0)
            for e in range(-(-rows // each)):
                packed = jnp.sum(kept[e * each : (e + 1) * each], axis=0, keepdims=True)
                last = jnp.where(line == samples.shape[0] - EXTRAS + 2 * (g % 2) + e, packed, last)
        pieces.append(last)
        extra = send_ref.shape[0] - sum(piece.shape[0] for piece in pieces)
        if extra:
            pieces.append(jnp.zeros((extra, LANES), jnp.float32))
        send_ref[...] = jnp.concatenate(pieces, axis=0).astype(jnp.bfloat16)


def correlate_kernel(dims, with_data, *refs):
    if with_data:
        mask_ref, *refs = refs
    else:
        data_ref, mask_ref, *refs = refs
    n, stations, blocks, components, taps, most, rows, width, per_group = dims
    own_ref, core_ref, *chip_refs = refs[:n]
    refs = refs[n:]
    come = [(own_ref, 0, 1), (core_ref, 0, 1)]
    for i in range(n // 2 - 1):
        come += [(chip_refs[i], 0, 2), (chip_refs[n // 2 - 1 + i], 1, 2)]
    distances = [0, 1]
    for d in chips(n):
        distances += [d, d + 1]
    *out_refs, x_ref, dsh_ref, rd_ref, ws_ref, rw_ref, meta_ref, sh_ref, stack_ref = refs
    whole, tail, left = chunk_plan(taps, components)
    chunks = whole + 1
    sent = components * whole + 1
    total = n * rows
    here = n * most
    lag_tiles = ceil_to(width - taps + 1, LANES) // LANES
    lag_width = lag_tiles * LANES
    series = stations * components * blocks
    series_rows = ceil_to(series, 8)

    def lines(ref, start, count):
        first = start // 16 * 16
        return ref[first : ceil_to(start + count, 16), :].astype(jnp.float32)[start - first :][:count]

    last_rows = series + EXTRAS if with_data else 8
    blocks_in = [lines(ref, half * sent * rows, sent * rows) for ref, half, _ in come]
    lasts = [lines(ref, count * sent * rows, last_rows) for ref, _, count in come]

    if with_data:
        for d, last in zip(distances, lasts):
            x_ref[lax.axis_index("tmpl") ^ d] = last
        x = jnp.concatenate([x_ref[i] for i in range(n)], axis=1)
    else:
        x = data_ref[...].astype(jnp.float32)
        x = jnp.concatenate([x, jnp.zeros((series_rows - series, width), jnp.float32)], axis=0)
    for r in range(SHIFTS):
        moved = pltpu.roll(x, width - r, 1) if r else x
        for t in range(width // LANES):
            dsh_ref[t, r * series_rows : (r + 1) * series_rows, :] = moved[:, t * LANES : (t + 1) * LANES]

    squares = jnp.concatenate([x * x, jnp.zeros((series_rows, chunks * LANES), jnp.float32)], axis=1)
    rounded = squares.astype(jnp.bfloat16).astype(jnp.float32)
    rest = squares - rounded
    reach = (chunks + 1) * LANES
    sample = lax.broadcasted_iota(jnp.int32, (reach, LANES), 0)
    sample = sample - lax.broadcasted_iota(jnp.int32, (reach, LANES), 1)
    ones = jnp.where((sample >= 0) & (sample < taps), 1.0, 0.0).astype(jnp.bfloat16)
    spans = [
        part[:, t * LANES : t * LANES + reach] for t in range(lag_tiles) for part in (rounded, rest)
    ]
    power = jnp.dot(jnp.concatenate(spans, axis=0).astype(jnp.bfloat16), ones, preferred_element_type=jnp.float32)
    power = [
        power[2 * t * series_rows : (2 * t + 1) * series_rows]
        + power[(2 * t + 1) * series_rows : (2 * t + 2) * series_rows]
        for t in range(lag_tiles)
    ]
    row = lax.broadcasted_iota(jnp.int32, (series_rows, LANES), 0)
    factor = jnp.zeros((series_rows, LANES), jnp.float32)
    for s in range(stations):
        used = [mask_ref[s, c] for c in range(components)]
        total_used = jnp.maximum(functools.reduce(lambda p, q: p + q, used), 1)
        for c in range(components):
            at = (s * components + c) * blocks
            mine = (row >= at) & (row < at + blocks)
            value = jnp.full((series_rows, LANES), used[c]).astype(jnp.float32)
            value = value / jnp.full((series_rows, LANES), total_used).astype(jnp.float32)
            factor = jnp.where(mine, value, factor)
    for t in range(lag_tiles):
        rd_ref[:, t * LANES : (t + 1) * LANES] = lax.rsqrt(power[t] / taps + epsilon) * factor

    target = lax.broadcasted_iota(jnp.int32, (stations * here, total), 0)
    source = lax.broadcasted_iota(jnp.int32, (stations * here, total), 1)
    wanted = (
        quotient(remainder(target, here), most) * rows
        + quotient(target, here) * most
        + remainder(target, most)
    )
    order = jnp.where(source == wanted, 1.0, 0.0).astype(jnp.bfloat16)
    lane = lax.broadcasted_iota(jnp.int32, (stations * here, LANES), 1)
    def received(k):
        piece = jnp.concatenate([blocks_in[i][k * rows : (k + 1) * rows] for i in range(n)], axis=0)
        return jnp.dot(order, piece.astype(jnp.bfloat16), preferred_element_type=jnp.float32)

    each = LANES // SMALL
    target = lax.broadcasted_iota(jnp.int32, (stations * here, n * 8), 0)
    place = quotient(target, here) * most + remainder(target, most)
    sender = quotient(remainder(target, here), most)
    line = sender * 8 + (8 - EXTRAS) + 2 * remainder(sender, 2) + quotient(place, each)
    line = lax.broadcasted_iota(jnp.int32, (stations * here, n * 8), 1) == line
    small = jnp.concatenate([last[last_rows - 8 :] for last in lasts], axis=0).astype(jnp.bfloat16)
    small = jnp.dot(
        jnp.where(line, 1.0, 0.0).astype(jnp.bfloat16), small, preferred_element_type=jnp.float32
    )
    target = lax.broadcasted_iota(jnp.int32, (stations * here, LANES), 0)
    place = remainder(quotient(target, here) * most + remainder(target, most), each)
    small = jnp.where(quotient(lane, SMALL) == place, small, 0.0).astype(jnp.bfloat16)
    fold = lax.broadcasted_iota(jnp.int32, (LANES, LANES), 0)
    fold = remainder(fold, SMALL) == lax.broadcasted_iota(jnp.int32, (LANES, LANES), 1)
    fold = jnp.where(fold, 1.0, 0.0).astype(jnp.bfloat16)
    meta_ref[...] = jnp.dot(small, fold, preferred_element_type=jnp.float32)

    wanted = lax.broadcasted_iota(jnp.int32, (8, LANES), 1) == left
    local = lax.dot_general(
        jnp.where(wanted, 1.0, 0.0).astype(jnp.bfloat16),
        meta_ref[...].astype(jnp.bfloat16),
        (((1,), (1,)), ((), ())),
        preferred_element_type=jnp.float32,
    )
    template = lax.broadcasted_iota(jnp.int32, (per_group, stations * here), 0) + 1
    onehot = jnp.where(local[:1].astype(jnp.int32) == template, 1.0, 0.0).astype(jnp.bfloat16)

    ends = received(components * whole)
    for c in range(components):
        pieces = [received(c * whole + a) for a in range(whole)]
        end = pltpu.roll(ends, LANES - c * tail, 1) if c else ends
        if c == components - 1:
            end = jnp.where(lane < tail - left, end, pltpu.roll(meta_ref[...], tail - left, 1))
        pieces.append(jnp.where(lane < tail, end, 0.0))
        squares = functools.reduce(lambda p, q: p + q, [piece * piece for piece in pieces])
        for a in range(chunks):
            at = (c * chunks + a) * LANES
            ws_ref[:, at : at + LANES] = pieces[a].astype(jnp.bfloat16)
        wave_power = jnp.sum(squares, axis=1, keepdims=True) / taps
        rw_ref[:, c * LANES : (c + 1) * LANES] = jnp.broadcast_to(
            lax.rsqrt(wave_power + epsilon) / taps, (stations * here, LANES)
        )

    depth = (chunks - 1) * LANES + ceil_to(tail, 16)
    lane_here = lax.broadcasted_iota(jnp.int32, (here, LANES), 1)

    for s in range(stations):
        rows_here = slice(s * here, (s + 1) * here)
        meta = meta_ref[rows_here, :]
        tiles_over = jnp.broadcast_to(meta[:, left + 1 : left + 2], (here, LANES)).astype(jnp.int32)
        lanes_over = jnp.broadcast_to(meta[:, left + 2 : left + 3], (here, LANES)).astype(jnp.int32)
        index = lane_here + lanes_over
        within = lane_here >= lanes_over
        index = jnp.bitwise_and(index, LANES - 1)
        for b in range(blocks):
            total_corr = [jnp.zeros((here, LANES), jnp.float32) for _ in range(lag_tiles)]
            for c in range(components):
                at = (s * components + c) * blocks + b
                low = [
                    dsh_ref[t, pl.ds(at, SHIFTS, stride=series_rows), :] for t in range(width // LANES)
                ]
                low = jnp.concatenate(low, axis=1).astype(jnp.bfloat16)
                pieces = [low] + [pltpu.roll(low, width - q, 1) for q in range(SHIFTS, LANES, SHIFTS)]
                shifted = jnp.concatenate(pieces, axis=0)
                hankel = jnp.concatenate(
                    [
                        shifted[: min(LANES, depth - a * LANES), a * LANES : a * LANES + lag_width]
                        for a in range(chunks)
                    ],
                    axis=0,
                )
                w = ws_ref[rows_here, c * chunks * LANES : c * chunks * LANES + depth]
                numerator = jnp.dot(w, hankel, preferred_element_type=jnp.float32)
                over_wave = rw_ref[rows_here, c * LANES : (c + 1) * LANES]
                over_data = rd_ref[at : at + 1, :]
                for t in range(lag_tiles):
                    cut = slice(t * LANES, (t + 1) * LANES)
                    total_corr[t] = total_corr[t] + numerator[:, cut] * over_wave * over_data[:, cut]
            windows = []
            for t in range(NK // LANES + 1):
                window = total_corr[t]
                for h in range(1, lag_tiles - NK // LANES):
                    if t + h < lag_tiles:
                        window = jnp.where(tiles_over == h, total_corr[t + h], window)
                windows.append(window)
            for t in range(NK // LANES):
                aligned = jnp.where(within, windows[t], windows[t + 1])
                aligned = jnp.take_along_axis(aligned, index, axis=1)
                at = b * NK + t * LANES
                sh_ref[rows_here, at : at + LANES] = aligned.astype(jnp.bfloat16)

    slot = lax.broadcasted_iota(jnp.int32, (stations * here, LANES), 0)
    half = (slot < stations * here // 2) == (lane < LANES // 2)
    sh_ref[:, blocks * NK :] = jnp.where(half, 1.0, 0.0).astype(jnp.bfloat16)
    stack_ref[...] = jnp.dot(onehot, sh_ref[...], preferred_element_type=jnp.float32)
    me = lax.axis_index("stn")
    for d, out_ref in enumerate(out_refs):
        owner = lax.rem(me + d, len(out_refs))
        theirs = pl.ds(pl.multiple_of(owner * TPD, TPD), TPD)
        out_ref[...] = stack_ref[theirs, :].astype(jnp.bfloat16)


def finish_kernel(taps, blocks, *refs):
    *parts_refs, out_ref = refs
    total = functools.reduce(lambda p, q: p + q, [ref[...].astype(jnp.float32) for ref in parts_refs])
    first, middle = blocks * NK, blocks * NK + LANES // 2
    count = total[:, first : first + 1] + total[:, middle : middle + 1]
    scale = jnp.sqrt(jnp.float32(taps)) / jnp.sqrt(jnp.maximum(count, 1.0))
    for b in range(blocks):
        out_ref[b] = total[:, b * NK : (b + 1) * NK] * scale


def body(data, waves, slot_group, slot_local, moveout, chan_mask):
    blocks, stations, components, width_here = data.shape
    slots, taps = waves.shape[1], waves.shape[3]
    n = lax.axis_size("tmpl")
    owners = lax.axis_size("stn")
    per_group = TPD * owners
    width = width_here * n
    most = max(2, 2 * slots // n)
    rows = ceil_to(stations * most, 8)
    whole, tail, left = chunk_plan(taps, components)
    series = stations * components * blocks
    series_rows = ceil_to(series, 8)
    with_data = width_here == LANES
    here = n * most

    waves = jnp.transpose(waves, (0, 2, 1, 3)).reshape(stations * components, slots, taps)
    groups = jnp.transpose(slot_group, (0, 2, 1))
    samples = jnp.transpose(data, (1, 2, 0, 3)).reshape(stations * components, blocks, width_here)
    last_rows = series + EXTRAS if with_data else 8
    message_rows = [ceil_to(k * (components * whole + 1) * rows + last_rows, 16) for k in (1, 1)]
    message_rows += [ceil_to(2 * (components * whole + 1) * rows + last_rows, 16)] * (n // 2 - 1)
    ins = ([samples] if with_data else []) + [waves, groups, slot_local, moveout]
    ins = [pltpu.with_memory_space_constraint(x, pltpu.HBM) for x in ins]
    send = pl.pallas_call(
        functools.partial(
            pack_kernel, (n, stations, slots, components, taps, most, rows), with_data
        ),
        out_shape=[jax.ShapeDtypeStruct((k, LANES), jnp.bfloat16) for k in message_rows],
        in_specs=[pl.BlockSpec(memory_space=pltpu.HBM)] * len(ins),
        scratch_shapes=[pltpu.VMEM(x.shape, x.dtype) for x in ins]
        + [pltpu.SemaphoreType.DMA((len(ins),))],
        compiler_params=pltpu.CompilerParams(vmem_limit_bytes=24 << 20),
        name="pack",
    )(*ins)
    def swap(block, d):
        return lax.ppermute(block, "tmpl", [(i, i ^ d) for i in range(n)])

    own, for_core, *for_chips = send
    from_chips = [swap(block, d) for d, block in zip(chips(n), for_chips)]
    from_core = swap(for_core, 1)
    if from_chips:
        from_chips[0], from_core = lax.optimization_barrier((from_chips[0], from_core))
    received = [own, from_core] + from_chips + [swap(block, 1) for block in from_chips]
    if not with_data:
        samples = lax.all_gather(samples.reshape(series, width_here), "tmpl", axis=1, tiled=True)
    vmem = pl.BlockSpec(memory_space=pltpu.VMEM)
    partial_stacks = pl.pallas_call(
        functools.partial(
            correlate_kernel,
            (n, stations, blocks, components, taps, most, rows, width, per_group),
            with_data,
        ),
        out_shape=[jax.ShapeDtypeStruct((TPD, blocks * NK + LANES), jnp.bfloat16)] * owners,
        in_specs=[vmem] * (0 if with_data else 1) + [pl.BlockSpec(memory_space=pltpu.SMEM)] + [vmem] * n,
        scratch_shapes=[
            pltpu.VMEM((width // LANES, series_rows, LANES), jnp.float32),
            pltpu.VMEM((width // LANES, SHIFTS * series_rows, LANES), jnp.float32),
            pltpu.VMEM((series_rows, ceil_to(width - taps + 1, LANES)), jnp.float32),
            pltpu.VMEM((stations * here, components * (whole + 1) * LANES), jnp.bfloat16),
            pltpu.VMEM((stations * here, components * LANES), jnp.float32),
            pltpu.VMEM((stations * here, LANES), jnp.float32),
            pltpu.VMEM((stations * here, blocks * NK + LANES), jnp.bfloat16),
            pltpu.VMEM((per_group, blocks * NK + LANES), jnp.float32),
        ],
        compiler_params=pltpu.CompilerParams(vmem_limit_bytes=40 << 20),
        name="correlate",
    )(*([] if with_data else [samples]), chan_mask, *received)
    parts = [
        lax.ppermute(part, "stn", [(i, (i + d) % owners) for i in range(owners)]) if d else part
        for d, part in enumerate(partial_stacks)
    ]
    return pl.pallas_call(
        functools.partial(finish_kernel, taps, blocks),
        out_shape=jax.ShapeDtypeStruct((blocks, TPD, NK), jnp.float32),
        compiler_params=pltpu.CompilerParams(vmem_limit_bytes=4 << 20),
        name="finish",
    )(*parts)


def solution(mesh):
    in_specs = (
        P(None, "stn", None, "tmpl"),
        P("stn", "tmpl", None, None),
        P("stn", "tmpl", None),
        P("stn", "tmpl"),
        P("stn", "tmpl"),
        P("stn", None),
    )
    out_specs = P(None, ("tmpl", "stn"), None)
    return jax.shard_map(body, mesh=mesh, in_specs=in_specs, out_specs=out_specs, check_vma=False)
```

```python
import functools

import jax
import jax.numpy as jnp
from jax import lax
from jax.experimental import pallas as pl
from jax.experimental.pallas import tpu as pltpu
from jax.sharding import PartitionSpec as P

NK = 256
TPD = 16
LANES = 128
SHIFTS = 16

epsilon = 1e-06


def ceil_to(value, multiple):
    return -(-value // multiple) * multiple


def quotient(values, divisor):
    if divisor & (divisor - 1):
        return values // divisor
    return lax.shift_right_logical(values, divisor.bit_length() - 1)


def remainder(values, divisor):
    if divisor & (divisor - 1):
        return values % divisor
    return values & (divisor - 1)


def rotations(n):
    return [0] + [d for d in [n // 2] if d] + [d for d in range(1, n) if d != n // 2]


def chips(n):
    return list(range(n - 2, 0, -2))


def column_of(row):
    n = row.shape[1]
    eye = lax.broadcasted_iota(jnp.int32, (n, n), 0) == lax.broadcasted_iota(jnp.int32, (n, n), 1)
    return jnp.sum(jnp.where(eye, jnp.broadcast_to(row, (n, n)), 0), axis=1, keepdims=True)


SMALL = 8
EXTRAS = 4


def chunk_plan(taps, components):
    whole = taps // LANES
    tail = taps - whole * LANES
    left = components * tail - LANES
    assert 0 < left <= min(tail, SMALL - 3)
    return whole, tail, left


def pack_kernel(dims, with_data, *refs):
    n, stations, slots, components, taps, most, rows = dims
    ins = refs[: 5 if with_data else 4]
    own_ref, core_ref, *chip_refs = refs[len(ins) : len(ins) + 1 + n // 2]
    held = refs[len(ins) + 1 + n // 2 : -1]
    sems = refs[-1]
    copies = [pltpu.make_async_copy(ins[i], held[i], sems.at[i]) for i in range(len(ins))]
    for copy in copies:
        copy.start()
    waves_ref, group_ref, local_ref, moveout_ref = held[-4:]
    count = stations * slots
    whole, tail, left = chunk_plan(taps, components)

    def flat(ref, three):
        pieces = [ref[s] if three else ref[s : s + 1, :] for s in range(stations)]
        return jnp.concatenate(pieces, axis=1)

    for copy in copies[-3:]:
        copy.wait()
    group = flat(group_ref, True)
    local = flat(local_ref, False)
    moveout = flat(moveout_ref, False)
    group_col = column_of(group)
    upper = lax.broadcasted_iota(jnp.int32, (count, count), 0)
    lower = lax.broadcasted_iota(jnp.int32, (count, count), 1)
    same = (quotient(upper, slots) == quotient(lower, slots)) & (upper < lower)
    rank = jnp.sum(jnp.where(same & (group_col == group), 1, 0), axis=0, keepdims=True)
    station = quotient(lax.broadcasted_iota(jnp.int32, (1, count), 1), slots)
    partner = group ^ lax.axis_index("tmpl")
    position = partner * rows + station * most + rank
    place = lax.broadcasted_iota(jnp.int32, (n * rows, count), 0) == position
    place = jnp.where(place, 1.0, 0.0).astype(jnp.bfloat16)

    lane = lax.broadcasted_iota(jnp.int32, (count, LANES), 1)
    meta = [column_of(local) + 1, column_of(quotient(moveout, LANES)), column_of(remainder(moveout, LANES))]

    for copy in copies[:-3]:
        copy.wait()
    waves = [
        jnp.concatenate([waves_ref[s * components + c] for s in range(stations)], axis=0)
        for c in range(components)
    ]
    placed = [
        jnp.dot(place, waves[c][:, : whole * LANES], preferred_element_type=jnp.float32)
        for c in range(components)
    ]
    ends = [waves[c][:, whole * LANES :] for c in range(components - 1)]
    ends.append(waves[-1][:, whole * LANES : taps - left])
    ends = jnp.dot(place, jnp.concatenate(ends, axis=1), preferred_element_type=jnp.float32)
    small = [waves[-1][:, taps - left + v : taps - left + v + 1] for v in range(left)] + meta
    spread = jnp.zeros((count, LANES), jnp.float32)
    for v, column in enumerate(small):
        spread = jnp.where(remainder(lane, SMALL) == v, column.astype(jnp.float32), spread)
    spread = jnp.dot(place, spread.astype(jnp.bfloat16), preferred_element_type=jnp.float32)
    each = LANES // SMALL
    within = remainder(lax.broadcasted_iota(jnp.int32, (rows, LANES), 0), each)
    within = within == quotient(lax.broadcasted_iota(jnp.int32, (rows, LANES), 1), SMALL)
    if with_data:
        samples = held[0][...].astype(jnp.float32)
        samples = samples.reshape(samples.shape[0] * samples.shape[1], LANES)
        samples = jnp.concatenate([samples, jnp.zeros((EXTRAS, LANES), jnp.float32)], axis=0)
    else:
        samples = jnp.zeros((8, LANES), jnp.float32)
    line = lax.broadcasted_iota(jnp.int32, samples.shape, 0)
    messages = [(own_ref, [0]), (core_ref, [1])]
    messages += [(ref, [d, d + 1]) for d, ref in zip(chips(n), chip_refs)]
    for send_ref, groups in messages:
        pieces, last = [], samples
        for g in groups:
            mine = slice(g * rows, (g + 1) * rows)
            for c in range(components):
                pieces += [placed[c][mine, a * LANES : (a + 1) * LANES] for a in range(whole)]
            pieces.append(ends[mine])
            kept = jnp.where(within, spread[mine], 0.0)
            for e in range(-(-rows // each)):
                packed = jnp.sum(kept[e * each : (e + 1) * each], axis=0, keepdims=True)
                last = jnp.where(line == samples.shape[0] - EXTRAS + 2 * (g % 2) + e, packed, last)
        pieces.append(last)
        extra = send_ref.shape[0] - sum(piece.shape[0] for piece in pieces)
        if extra:
            pieces.append(jnp.zeros((extra, LANES), jnp.float32))
        send_ref[...] = jnp.concatenate(pieces, axis=0).astype(jnp.bfloat16)


def correlate_kernel(dims, with_data, *refs):
    if with_data:
        mask_ref, *refs = refs
    else:
        data_ref, mask_ref, *refs = refs
    n, stations, blocks, components, taps, most, rows, width, per_group = dims
    own_ref, core_ref, *chip_refs = refs[:n]
    refs = refs[n:]
    come = [(own_ref, 0, 1), (core_ref, 0, 1)]
    for i in range(n // 2 - 1):
        come += [(chip_refs[i], 0, 2), (chip_refs[n // 2 - 1 + i], 1, 2)]
    distances = [0, 1]
    for d in chips(n):
        distances += [d, d + 1]
    *out_refs, x_ref, dsh_ref, rd_ref, ws_ref, rw_ref, meta_ref, sh_ref, stack_ref = refs
    whole, tail, left = chunk_plan(taps, components)
    chunks = whole + 1
    sent = components * whole + 1
    total = n * rows
    here = n * most
    lag_tiles = ceil_to(width - taps + 1, LANES) // LANES
    lag_width = lag_tiles * LANES
    series = stations * components * blocks
    series_rows = ceil_to(series, 8)

    def lines(ref, start, count):
        first = start // 16 * 16
        return ref[first : ceil_to(start + count, 16), :].astype(jnp.float32)[start - first :][:count]

    last_rows = series + EXTRAS if with_data else 8
    blocks_in = [lines(ref, half * sent * rows, sent * rows) for ref, half, _ in come]
    lasts = [lines(ref, count * sent * rows, last_rows) for ref, _, count in come]

    if with_data:
        for d, last in zip(distances, lasts):
            x_ref[lax.axis_index("tmpl") ^ d] = last
        x = jnp.concatenate([x_ref[i] for i in range(n)], axis=1)
    else:
        x = data_ref[...].astype(jnp.float32)
        x = jnp.concatenate([x, jnp.zeros((series_rows - series, width), jnp.float32)], axis=0)
    for r in range(SHIFTS):
        moved = pltpu.roll(x, width - r, 1) if r else x
        for t in range(width // LANES):
            dsh_ref[t, r * series_rows : (r + 1) * series_rows, :] = moved[:, t * LANES : (t + 1) * LANES]

    squares = jnp.concatenate([x * x, jnp.zeros((series_rows, chunks * LANES), jnp.float32)], axis=1)
    rounded = squares.astype(jnp.bfloat16).astype(jnp.float32)
    rest = squares - rounded
    reach = (chunks + 1) * LANES
    sample = lax.broadcasted_iota(jnp.int32, (reach, LANES), 0)
    sample = sample - lax.broadcasted_iota(jnp.int32, (reach, LANES), 1)
    ones = jnp.where((sample >= 0) & (sample < taps), 1.0, 0.0).astype(jnp.bfloat16)
    spans = [
        part[:, t * LANES : t * LANES + reach] for t in range(lag_tiles) for part in (rounded, rest)
    ]
    power = jnp.dot(jnp.concatenate(spans, axis=0).astype(jnp.bfloat16), ones, preferred_element_type=jnp.float32)
    power = [
        power[2 * t * series_rows : (2 * t + 1) * series_rows]
        + power[(2 * t + 1) * series_rows : (2 * t + 2) * series_rows]
        for t in range(lag_tiles)
    ]
    row = lax.broadcasted_iota(jnp.int32, (series_rows, LANES), 0)
    factor = jnp.zeros((series_rows, LANES), jnp.float32)
    for s in range(stations):
        used = [mask_ref[s, c] for c in range(components)]
        total_used = jnp.maximum(functools.reduce(lambda p, q: p + q, used), 1)
        for c in range(components):
            at = (s * components + c) * blocks
            mine = (row >= at) & (row < at + blocks)
            value = jnp.full((series_rows, LANES), used[c]).astype(jnp.float32)
            value = value / jnp.full((series_rows, LANES), total_used).astype(jnp.float32)
            factor = jnp.where(mine, value, factor)
    for t in range(lag_tiles):
        rd_ref[:, t * LANES : (t + 1) * LANES] = lax.rsqrt(power[t] / taps + epsilon) * factor

    target = lax.broadcasted_iota(jnp.int32, (stations * here, total), 0)
    source = lax.broadcasted_iota(jnp.int32, (stations * here, total), 1)
    wanted = (
        quotient(remainder(target, here), most) * rows
        + quotient(target, here) * most
        + remainder(target, most)
    )
    order = jnp.where(source == wanted, 1.0, 0.0).astype(jnp.bfloat16)
    lane = lax.broadcasted_iota(jnp.int32, (stations * here, LANES), 1)
    def received(k):
        piece = jnp.concatenate([blocks_in[i][k * rows : (k + 1) * rows] for i in range(n)], axis=0)
        return jnp.dot(order, piece.astype(jnp.bfloat16), preferred_element_type=jnp.float32)

    each = LANES // SMALL
    target = lax.broadcasted_iota(jnp.int32, (stations * here, n * 8), 0)
    place = quotient(target, here) * most + remainder(target, most)
    sender = quotient(remainder(target, here), most)
    line = sender * 8 + (8 - EXTRAS) + 2 * remainder(sender, 2) + quotient(place, each)
    line = lax.broadcasted_iota(jnp.int32, (stations * here, n * 8), 1) == line
    small = jnp.concatenate([last[last_rows - 8 :] for last in lasts], axis=0).astype(jnp.bfloat16)
    small = jnp.dot(
        jnp.where(line, 1.0, 0.0).astype(jnp.bfloat16), small, preferred_element_type=jnp.float32
    )
    target = lax.broadcasted_iota(jnp.int32, (stations * here, LANES), 0)
    place = remainder(quotient(target, here) * most + remainder(target, most), each)
    small = jnp.where(quotient(lane, SMALL) == place, small, 0.0).astype(jnp.bfloat16)
    fold = lax.broadcasted_iota(jnp.int32, (LANES, LANES), 0)
    fold = remainder(fold, SMALL) == lax.broadcasted_iota(jnp.int32, (LANES, LANES), 1)
    fold = jnp.where(fold, 1.0, 0.0).astype(jnp.bfloat16)
    meta_ref[...] = jnp.dot(small, fold, preferred_element_type=jnp.float32)

    wanted = lax.broadcasted_iota(jnp.int32, (8, LANES), 1) == left
    local = lax.dot_general(
        jnp.where(wanted, 1.0, 0.0).astype(jnp.bfloat16),
        meta_ref[...].astype(jnp.bfloat16),
        (((1,), (1,)), ((), ())),
        preferred_element_type=jnp.float32,
    )
    template = lax.broadcasted_iota(jnp.int32, (per_group, stations * here), 0) + 1
    onehot = jnp.where(local[:1].astype(jnp.int32) == template, 1.0, 0.0).astype(jnp.bfloat16)

    ends = received(components * whole)
    for c in range(components):
        pieces = [received(c * whole + a) for a in range(whole)]
        end = pltpu.roll(ends, LANES - c * tail, 1) if c else ends
        if c == components - 1:
            end = jnp.where(lane < tail - left, end, pltpu.roll(meta_ref[...], tail - left, 1))
        pieces.append(jnp.where(lane < tail, end, 0.0))
        squares = functools.reduce(lambda p, q: p + q, [piece * piece for piece in pieces])
        for a in range(chunks):
            at = (c * chunks + a) * LANES
            ws_ref[:, at : at + LANES] = pieces[a].astype(jnp.bfloat16)
        wave_power = jnp.sum(squares, axis=1, keepdims=True) / taps
        rw_ref[:, c * LANES : (c + 1) * LANES] = jnp.broadcast_to(
            lax.rsqrt(wave_power + epsilon) / taps, (stations * here, LANES)
        )

    depth = (chunks - 1) * LANES + ceil_to(tail, 16)
    lane_here = lax.broadcasted_iota(jnp.int32, (here, LANES), 1)

    for s in range(stations):
        rows_here = slice(s * here, (s + 1) * here)
        meta = meta_ref[rows_here, :]
        tiles_over = jnp.broadcast_to(meta[:, left + 1 : left + 2], (here, LANES)).astype(jnp.int32)
        lanes_over = jnp.broadcast_to(meta[:, left + 2 : left + 3], (here, LANES)).astype(jnp.int32)
        index = lane_here + lanes_over
        within = lane_here >= lanes_over
        index = jnp.bitwise_and(index, LANES - 1)
        for b in range(blocks):
            total_corr = [jnp.zeros((here, LANES), jnp.float32) for _ in range(lag_tiles)]
            for c in range(components):
                at = (s * components + c) * blocks + b
                low = [
                    dsh_ref[t, pl.ds(at, SHIFTS, stride=series_rows), :] for t in range(width // LANES)
                ]
                low = jnp.concatenate(low, axis=1).astype(jnp.bfloat16)
                pieces = [low] + [pltpu.roll(low, width - q, 1) for q in range(SHIFTS, LANES, SHIFTS)]
                shifted = jnp.concatenate(pieces, axis=0)
                hankel = jnp.concatenate(
                    [
                        shifted[: min(LANES, depth - a * LANES), a * LANES : a * LANES + lag_width]
                        for a in range(chunks)
                    ],
                    axis=0,
                )
                w = ws_ref[rows_here, c * chunks * LANES : c * chunks * LANES + depth]
                numerator = jnp.dot(w, hankel, preferred_element_type=jnp.float32)
                over_wave = rw_ref[rows_here, c * LANES : (c + 1) * LANES]
                over_data = rd_ref[at : at + 1, :]
                for t in range(lag_tiles):
                    cut = slice(t * LANES, (t + 1) * LANES)
                    total_corr[t] = total_corr[t] + numerator[:, cut] * over_wave * over_data[:, cut]
            windows = []
            for t in range(NK // LANES + 1):
                window = total_corr[t]
                for h in range(1, lag_tiles - NK // LANES):
                    if t + h < lag_tiles:
                        window = jnp.where(tiles_over == h, total_corr[t + h], window)
                windows.append(window)
            for t in range(NK // LANES):
                aligned = jnp.where(within, windows[t], windows[t + 1])
                aligned = jnp.take_along_axis(aligned, index, axis=1)
                at = b * NK + t * LANES
                sh_ref[rows_here, at : at + LANES] = aligned.astype(jnp.bfloat16)

    slot = lax.broadcasted_iota(jnp.int32, (stations * here, LANES), 0)
    half = (slot < stations * here // 2) == (lane < LANES // 2)
    sh_ref[:, blocks * NK :] = jnp.where(half, 1.0, 0.0).astype(jnp.bfloat16)
    stack_ref[...] = jnp.dot(onehot, sh_ref[...], preferred_element_type=jnp.float32)
    me = lax.axis_index("stn")
    for d, out_ref in zip(rotations(len(out_refs)), out_refs):
        owner = lax.rem(me + d, len(out_refs))
        theirs = pl.ds(pl.multiple_of(owner * TPD, TPD), TPD)
        out_ref[...] = stack_ref[theirs, :].astype(jnp.bfloat16)


def finish_kernel(taps, blocks, *refs):
    *parts_refs, out_ref = refs
    total = functools.reduce(lambda p, q: p + q, [ref[...].astype(jnp.float32) for ref in parts_refs])
    first, middle = blocks * NK, blocks * NK + LANES // 2
    count = total[:, first : first + 1] + total[:, middle : middle + 1]
    scale = jnp.sqrt(jnp.float32(taps)) / jnp.sqrt(jnp.maximum(count, 1.0))
    for b in range(blocks):
        out_ref[b] = total[:, b * NK : (b + 1) * NK] * scale


def body(data, waves, slot_group, slot_local, moveout, chan_mask):
    blocks, stations, components, width_here = data.shape
    slots, taps = waves.shape[1], waves.shape[3]
    n = lax.axis_size("tmpl")
    owners = lax.axis_size("stn")
    per_group = TPD * owners
    width = width_here * n
    most = max(2, 2 * slots // n)
    rows = ceil_to(stations * most, 8)
    whole, tail, left = chunk_plan(taps, components)
    series = stations * components * blocks
    series_rows = ceil_to(series, 8)
    with_data = width_here == LANES
    here = n * most

    waves = jnp.transpose(waves, (0, 2, 1, 3)).reshape(stations * components, slots, taps)
    groups = jnp.transpose(slot_group, (0, 2, 1))
    samples = jnp.transpose(data, (1, 2, 0, 3)).reshape(stations * components, blocks, width_here)
    last_rows = series + EXTRAS if with_data else 8
    message_rows = [ceil_to(k * (components * whole + 1) * rows + last_rows, 16) for k in (1, 1)]
    message_rows += [ceil_to(2 * (components * whole + 1) * rows + last_rows, 16)] * (n // 2 - 1)
    ins = ([samples] if with_data else []) + [waves, groups, slot_local, moveout]
    ins = [pltpu.with_memory_space_constraint(x, pltpu.HBM) for x in ins]
    send = pl.pallas_call(
        functools.partial(
            pack_kernel, (n, stations, slots, components, taps, most, rows), with_data
        ),
        out_shape=[jax.ShapeDtypeStruct((k, LANES), jnp.bfloat16) for k in message_rows],
        in_specs=[pl.BlockSpec(memory_space=pltpu.HBM)] * len(ins),
        scratch_shapes=[pltpu.VMEM(x.shape, x.dtype) for x in ins]
        + [pltpu.SemaphoreType.DMA((len(ins),))],
        compiler_params=pltpu.CompilerParams(vmem_limit_bytes=24 << 20),
        name="pack",
    )(*ins)
    def swap(block, d):
        return lax.ppermute(block, "tmpl", [(i, i ^ d) for i in range(n)])

    own, for_core, *for_chips = send
    from_chips = [swap(block, d) for d, block in zip(chips(n), for_chips)]
    from_core = swap(for_core, 1)
    if from_chips:
        from_chips[0], from_core = lax.optimization_barrier((from_chips[0], from_core))
    received = [own, from_core] + from_chips + [swap(block, 1) for block in from_chips]
    if not with_data:
        samples = lax.all_gather(samples.reshape(series, width_here), "tmpl", axis=1, tiled=True)
    vmem = pl.BlockSpec(memory_space=pltpu.VMEM)
    partial_stacks = pl.pallas_call(
        functools.partial(
            correlate_kernel,
            (n, stations, blocks, components, taps, most, rows, width, per_group),
            with_data,
        ),
        out_shape=[jax.ShapeDtypeStruct((TPD, blocks * NK + LANES), jnp.bfloat16)] * owners,
        in_specs=[vmem] * (0 if with_data else 1) + [pl.BlockSpec(memory_space=pltpu.SMEM)] + [vmem] * n,
        scratch_shapes=[
            pltpu.VMEM((width // LANES, series_rows, LANES), jnp.float32),
            pltpu.VMEM((width // LANES, SHIFTS * series_rows, LANES), jnp.float32),
            pltpu.VMEM((series_rows, ceil_to(width - taps + 1, LANES)), jnp.float32),
            pltpu.VMEM((stations * here, components * (whole + 1) * LANES), jnp.bfloat16),
            pltpu.VMEM((stations * here, components * LANES), jnp.float32),
            pltpu.VMEM((stations * here, LANES), jnp.float32),
            pltpu.VMEM((stations * here, blocks * NK + LANES), jnp.bfloat16),
            pltpu.VMEM((per_group, blocks * NK + LANES), jnp.float32),
        ],
        compiler_params=pltpu.CompilerParams(vmem_limit_bytes=40 << 20),
        name="correlate",
    )(*([] if with_data else [samples]), chan_mask, *received)
    parts = [
        lax.ppermute(part, "stn", [(i, (i + d) % owners) for i in range(owners)]) if d else part
        for d, part in zip(rotations(owners), partial_stacks)
    ]
    return pl.pallas_call(
        functools.partial(finish_kernel, taps, blocks),
        out_shape=jax.ShapeDtypeStruct((blocks, TPD, NK), jnp.float32),
        compiler_params=pltpu.CompilerParams(vmem_limit_bytes=4 << 20),
        name="finish",
    )(*parts)


def solution(mesh):
    in_specs = (
        P(None, "stn", None, "tmpl"),
        P("stn", "tmpl", None, None),
        P("stn", "tmpl", None),
        P("stn", "tmpl"),
        P("stn", "tmpl"),
        P("stn", None),
    )
    out_specs = P(None, ("tmpl", "stn"), None)
    return jax.shard_map(body, mesh=mesh, in_specs=in_specs, out_specs=out_specs, check_vma=False)
```

```python
import functools

import jax
import jax.numpy as jnp
from jax import lax
from jax.experimental import pallas as pl
from jax.experimental.pallas import tpu as pltpu
from jax.sharding import PartitionSpec as P

NK = 256
TPD = 16
LANES = 128
SHIFTS = 16

epsilon = 1e-06


def ceil_to(value, multiple):
    return -(-value // multiple) * multiple


def quotient(values, divisor):
    if divisor & (divisor - 1):
        return values // divisor
    return lax.shift_right_logical(values, divisor.bit_length() - 1)


def remainder(values, divisor):
    if divisor & (divisor - 1):
        return values % divisor
    return values & (divisor - 1)


def rotations(n):
    return [0] + list(range(n - 1, 0, -1))


def chips(n):
    return list(range(n - 2, 0, -2))


def column_of(row):
    n = row.shape[1]
    eye = lax.broadcasted_iota(jnp.int32, (n, n), 0) == lax.broadcasted_iota(jnp.int32, (n, n), 1)
    return jnp.sum(jnp.where(eye, jnp.broadcast_to(row, (n, n)), 0), axis=1, keepdims=True)


SMALL = 8
EXTRAS = 4


def chunk_plan(taps, components):
    whole = taps // LANES
    tail = taps - whole * LANES
    left = components * tail - LANES
    assert 0 < left <= min(tail, SMALL - 3)
    return whole, tail, left


def pack_kernel(dims, with_data, *refs):
    n, stations, slots, components, taps, most, rows = dims
    ins = refs[: 5 if with_data else 4]
    own_ref, core_ref, *chip_refs = refs[len(ins) : len(ins) + 1 + n // 2]
    held = refs[len(ins) + 1 + n // 2 : -1]
    sems = refs[-1]
    copies = [pltpu.make_async_copy(ins[i], held[i], sems.at[i]) for i in range(len(ins))]
    for copy in copies:
        copy.start()
    waves_ref, group_ref, local_ref, moveout_ref = held[-4:]
    count = stations * slots
    whole, tail, left = chunk_plan(taps, components)

    def flat(ref, three):
        pieces = [ref[s] if three else ref[s : s + 1, :] for s in range(stations)]
        return jnp.concatenate(pieces, axis=1)

    for copy in copies[-3:]:
        copy.wait()
    group = flat(group_ref, True)
    local = flat(local_ref, False)
    moveout = flat(moveout_ref, False)
    group_col = column_of(group)
    upper = lax.broadcasted_iota(jnp.int32, (count, count), 0)
    lower = lax.broadcasted_iota(jnp.int32, (count, count), 1)
    same = (quotient(upper, slots) == quotient(lower, slots)) & (upper < lower)
    rank = jnp.sum(jnp.where(same & (group_col == group), 1, 0), axis=0, keepdims=True)
    station = quotient(lax.broadcasted_iota(jnp.int32, (1, count), 1), slots)
    partner = group ^ lax.axis_index("tmpl")
    position = partner * rows + station * most + rank
    place = lax.broadcasted_iota(jnp.int32, (n * rows, count), 0) == position
    place = jnp.where(place, 1.0, 0.0).astype(jnp.bfloat16)

    lane = lax.broadcasted_iota(jnp.int32, (count, LANES), 1)
    meta = [column_of(local) + 1, column_of(quotient(moveout, LANES)), column_of(remainder(moveout, LANES))]

    for copy in copies[:-3]:
        copy.wait()
    waves = [
        jnp.concatenate([waves_ref[s * components + c] for s in range(stations)], axis=0)
        for c in range(components)
    ]
    placed = [
        jnp.dot(place, waves[c][:, : whole * LANES], preferred_element_type=jnp.float32)
        for c in range(components)
    ]
    ends = [waves[c][:, whole * LANES :] for c in range(components - 1)]
    ends.append(waves[-1][:, whole * LANES : taps - left])
    ends = jnp.dot(place, jnp.concatenate(ends, axis=1), preferred_element_type=jnp.float32)
    small = [waves[-1][:, taps - left + v : taps - left + v + 1] for v in range(left)] + meta
    spread = jnp.zeros((count, LANES), jnp.float32)
    for v, column in enumerate(small):
        spread = jnp.where(remainder(lane, SMALL) == v, column.astype(jnp.float32), spread)
    spread = jnp.dot(place, spread.astype(jnp.bfloat16), preferred_element_type=jnp.float32)
    each = LANES // SMALL
    within = remainder(lax.broadcasted_iota(jnp.int32, (rows, LANES), 0), each)
    within = within == quotient(lax.broadcasted_iota(jnp.int32, (rows, LANES), 1), SMALL)
    if with_data:
        samples = held[0][...].astype(jnp.float32)
        samples = samples.reshape(samples.shape[0] * samples.shape[1], LANES)
        samples = jnp.concatenate([samples, jnp.zeros((EXTRAS, LANES), jnp.float32)], axis=0)
    else:
        samples = jnp.zeros((8, LANES), jnp.float32)
    line = lax.broadcasted_iota(jnp.int32, samples.shape, 0)
    messages = [(own_ref, [0]), (core_ref, [1])]
    messages += [(ref, [d, d + 1]) for d, ref in zip(chips(n), chip_refs)]
    for send_ref, groups in messages:
        pieces, last = [], samples
        for g in groups:
            mine = slice(g * rows, (g + 1) * rows)
            for c in range(components):
                pieces += [placed[c][mine, a * LANES : (a + 1) * LANES] for a in range(whole)]
            pieces.append(ends[mine])
            kept = jnp.where(within, spread[mine], 0.0)
            for e in range(-(-rows // each)):
                packed = jnp.sum(kept[e * each : (e + 1) * each], axis=0, keepdims=True)
                last = jnp.where(line == samples.shape[0] - EXTRAS + 2 * (g % 2) + e, packed, last)
        pieces.append(last)
        extra = send_ref.shape[0] - sum(piece.shape[0] for piece in pieces)
        if extra:
            pieces.append(jnp.zeros((extra, LANES), jnp.float32))
        send_ref[...] = jnp.concatenate(pieces, axis=0).astype(jnp.bfloat16)


def correlate_kernel(dims, with_data, *refs):
    if with_data:
        mask_ref, *refs = refs
    else:
        data_ref, mask_ref, *refs = refs
    n, stations, blocks, components, taps, most, rows, width, per_group = dims
    own_ref, core_ref, *chip_refs = refs[:n]
    refs = refs[n:]
    come = [(own_ref, 0, 1), (core_ref, 0, 1)]
    for i in range(n // 2 - 1):
        come += [(chip_refs[i], 0, 2), (chip_refs[n // 2 - 1 + i], 1, 2)]
    distances = [0, 1]
    for d in chips(n):
        distances += [d, d + 1]
    *out_refs, x_ref, dsh_ref, rd_ref, ws_ref, rw_ref, meta_ref, sh_ref, stack_ref = refs
    whole, tail, left = chunk_plan(taps, components)
    chunks = whole + 1
    sent = components * whole + 1
    total = n * rows
    here = n * most
    lag_tiles = ceil_to(width - taps + 1, LANES) // LANES
    lag_width = lag_tiles * LANES
    series = stations * components * blocks
    series_rows = ceil_to(series, 8)

    def lines(ref, start, count):
        first = start // 16 * 16
        return ref[first : ceil_to(start + count, 16), :].astype(jnp.float32)[start - first :][:count]

    last_rows = series + EXTRAS if with_data else 8
    blocks_in = [lines(ref, half * sent * rows, sent * rows) for ref, half, _ in come]
    lasts = [lines(ref, count * sent * rows, last_rows) for ref, _, count in come]

    if with_data:
        for d, last in zip(distances, lasts):
            x_ref[lax.axis_index("tmpl") ^ d] = last
        x = jnp.concatenate([x_ref[i] for i in range(n)], axis=1)
    else:
        x = data_ref[...].astype(jnp.float32)
        x = jnp.concatenate([x, jnp.zeros((series_rows - series, width), jnp.float32)], axis=0)
    for r in range(SHIFTS):
        moved = pltpu.roll(x, width - r, 1) if r else x
        for t in range(width // LANES):
            dsh_ref[t, r * series_rows : (r + 1) * series_rows, :] = moved[:, t * LANES : (t + 1) * LANES]

    squares = jnp.concatenate([x * x, jnp.zeros((series_rows, chunks * LANES), jnp.float32)], axis=1)
    rounded = squares.astype(jnp.bfloat16).astype(jnp.float32)
    rest = squares - rounded
    reach = (chunks + 1) * LANES
    sample = lax.broadcasted_iota(jnp.int32, (reach, LANES), 0)
    sample = sample - lax.broadcasted_iota(jnp.int32, (reach, LANES), 1)
    ones = jnp.where((sample >= 0) & (sample < taps), 1.0, 0.0).astype(jnp.bfloat16)
    spans = [
        part[:, t * LANES : t * LANES + reach] for t in range(lag_tiles) for part in (rounded, rest)
    ]
    power = jnp.dot(jnp.concatenate(spans, axis=0).astype(jnp.bfloat16), ones, preferred_element_type=jnp.float32)
    power = [
        power[2 * t * series_rows : (2 * t + 1) * series_rows]
        + power[(2 * t + 1) * series_rows : (2 * t + 2) * series_rows]
        for t in range(lag_tiles)
    ]
    row = lax.broadcasted_iota(jnp.int32, (series_rows, LANES), 0)
    factor = jnp.zeros((series_rows, LANES), jnp.float32)
    for s in range(stations):
        used = [mask_ref[s, c] for c in range(components)]
        total_used = jnp.maximum(functools.reduce(lambda p, q: p + q, used), 1)
        for c in range(components):
            at = (s * components + c) * blocks
            mine = (row >= at) & (row < at + blocks)
            value = jnp.full((series_rows, LANES), used[c]).astype(jnp.float32)
            value = value / jnp.full((series_rows, LANES), total_used).astype(jnp.float32)
            factor = jnp.where(mine, value, factor)
    for t in range(lag_tiles):
        rd_ref[:, t * LANES : (t + 1) * LANES] = lax.rsqrt(power[t] / taps + epsilon) * factor

    target = lax.broadcasted_iota(jnp.int32, (stations * here, total), 0)
    source = lax.broadcasted_iota(jnp.int32, (stations * here, total), 1)
    wanted = (
        quotient(remainder(target, here), most) * rows
        + quotient(target, here) * most
        + remainder(target, most)
    )
    order = jnp.where(source == wanted, 1.0, 0.0).astype(jnp.bfloat16)
    lane = lax.broadcasted_iota(jnp.int32, (stations * here, LANES), 1)
    def received(k):
        piece = jnp.concatenate([blocks_in[i][k * rows : (k + 1) * rows] for i in range(n)], axis=0)
        return jnp.dot(order, piece.astype(jnp.bfloat16), preferred_element_type=jnp.float32)

    each = LANES // SMALL
    target = lax.broadcasted_iota(jnp.int32, (stations * here, n * 8), 0)
    place = quotient(target, here) * most + remainder(target, most)
    sender = quotient(remainder(target, here), most)
    line = sender * 8 + (8 - EXTRAS) + 2 * remainder(sender, 2) + quotient(place, each)
    line = lax.broadcasted_iota(jnp.int32, (stations * here, n * 8), 1) == line
    small = jnp.concatenate([last[last_rows - 8 :] for last in lasts], axis=0).astype(jnp.bfloat16)
    small = jnp.dot(
        jnp.where(line, 1.0, 0.0).astype(jnp.bfloat16), small, preferred_element_type=jnp.float32
    )
    target = lax.broadcasted_iota(jnp.int32, (stations * here, LANES), 0)
    place = remainder(quotient(target, here) * most + remainder(target, most), each)
    small = jnp.where(quotient(lane, SMALL) == place, small, 0.0).astype(jnp.bfloat16)
    fold = lax.broadcasted_iota(jnp.int32, (LANES, LANES), 0)
    fold = remainder(fold, SMALL) == lax.broadcasted_iota(jnp.int32, (LANES, LANES), 1)
    fold = jnp.where(fold, 1.0, 0.0).astype(jnp.bfloat16)
    meta_ref[...] = jnp.dot(small, fold, preferred_element_type=jnp.float32)

    wanted = lax.broadcasted_iota(jnp.int32, (8, LANES), 1) == left
    local = lax.dot_general(
        jnp.where(wanted, 1.0, 0.0).astype(jnp.bfloat16),
        meta_ref[...].astype(jnp.bfloat16),
        (((1,), (1,)), ((), ())),
        preferred_element_type=jnp.float32,
    )
    template = lax.broadcasted_iota(jnp.int32, (per_group, stations * here), 0) + 1
    onehot = jnp.where(local[:1].astype(jnp.int32) == template, 1.0, 0.0).astype(jnp.bfloat16)

    ends = received(components * whole)
    for c in range(components):
        pieces = [received(c * whole + a) for a in range(whole)]
        end = pltpu.roll(ends, LANES - c * tail, 1) if c else ends
        if c == components - 1:
            end = jnp.where(lane < tail - left, end, pltpu.roll(meta_ref[...], tail - left, 1))
        pieces.append(jnp.where(lane < tail, end, 0.0))
        squares = functools.reduce(lambda p, q: p + q, [piece * piece for piece in pieces])
        for a in range(chunks):
            at = (c * chunks + a) * LANES
            ws_ref[:, at : at + LANES] = pieces[a].astype(jnp.bfloat16)
        wave_power = jnp.sum(squares, axis=1, keepdims=True) / taps
        rw_ref[:, c * LANES : (c + 1) * LANES] = jnp.broadcast_to(
            lax.rsqrt(wave_power + epsilon) / taps, (stations * here, LANES)
        )

    depth = (chunks - 1) * LANES + ceil_to(tail, 16)
    lane_here = lax.broadcasted_iota(jnp.int32, (here, LANES), 1)

    for s in range(stations):
        rows_here = slice(s * here, (s + 1) * here)
        meta = meta_ref[rows_here, :]
        tiles_over = jnp.broadcast_to(meta[:, left + 1 : left + 2], (here, LANES)).astype(jnp.int32)
        lanes_over = jnp.broadcast_to(meta[:, left + 2 : left + 3], (here, LANES)).astype(jnp.int32)
        index = lane_here + lanes_over
        within = lane_here >= lanes_over
        index = jnp.bitwise_and(index, LANES - 1)
        for b in range(blocks):
            total_corr = [jnp.zeros((here, LANES), jnp.float32) for _ in range(lag_tiles)]
            for c in range(components):
                at = (s * components + c) * blocks + b
                low = [
                    dsh_ref[t, pl.ds(at, SHIFTS, stride=series_rows), :] for t in range(width // LANES)
                ]
                low = jnp.concatenate(low, axis=1).astype(jnp.bfloat16)
                pieces = [low] + [pltpu.roll(low, width - q, 1) for q in range(SHIFTS, LANES, SHIFTS)]
                shifted = jnp.concatenate(pieces, axis=0)
                hankel = jnp.concatenate(
                    [
                        shifted[: min(LANES, depth - a * LANES), a * LANES : a * LANES + lag_width]
                        for a in range(chunks)
                    ],
                    axis=0,
                )
                w = ws_ref[rows_here, c * chunks * LANES : c * chunks * LANES + depth]
                numerator = jnp.dot(w, hankel, preferred_element_type=jnp.float32)
                over_wave = rw_ref[rows_here, c * LANES : (c + 1) * LANES]
                over_data = rd_ref[at : at + 1, :]
                for t in range(lag_tiles):
                    cut = slice(t * LANES, (t + 1) * LANES)
                    total_corr[t] = total_corr[t] + numerator[:, cut] * over_wave * over_data[:, cut]
            windows = []
            for t in range(NK // LANES + 1):
                window = total_corr[t]
                for h in range(1, lag_tiles - NK // LANES):
                    if t + h < lag_tiles:
                        window = jnp.where(tiles_over == h, total_corr[t + h], window)
                windows.append(window)
            for t in range(NK // LANES):
                aligned = jnp.where(within, windows[t], windows[t + 1])
                aligned = jnp.take_along_axis(aligned, index, axis=1)
                at = b * NK + t * LANES
                sh_ref[rows_here, at : at + LANES] = aligned.astype(jnp.bfloat16)

    slot = lax.broadcasted_iota(jnp.int32, (stations * here, LANES), 0)
    half = (slot < stations * here // 2) == (lane < LANES // 2)
    sh_ref[:, blocks * NK :] = jnp.where(half, 1.0, 0.0).astype(jnp.bfloat16)
    stack_ref[...] = jnp.dot(onehot, sh_ref[...], preferred_element_type=jnp.float32)
    me = lax.axis_index("stn")
    for d, out_ref in zip(rotations(len(out_refs)), out_refs):
        owner = lax.rem(me + d, len(out_refs))
        theirs = pl.ds(pl.multiple_of(owner * TPD, TPD), TPD)
        out_ref[...] = stack_ref[theirs, :].astype(jnp.bfloat16)


def finish_kernel(taps, blocks, *refs):
    *parts_refs, out_ref = refs
    total = functools.reduce(lambda p, q: p + q, [ref[...].astype(jnp.float32) for ref in parts_refs])
    first, middle = blocks * NK, blocks * NK + LANES // 2
    count = total[:, first : first + 1] + total[:, middle : middle + 1]
    scale = jnp.sqrt(jnp.float32(taps)) / jnp.sqrt(jnp.maximum(count, 1.0))
    for b in range(blocks):
        out_ref[b] = total[:, b * NK : (b + 1) * NK] * scale


def body(data, waves, slot_group, slot_local, moveout, chan_mask):
    blocks, stations, components, width_here = data.shape
    slots, taps = waves.shape[1], waves.shape[3]
    n = lax.axis_size("tmpl")
    owners = lax.axis_size("stn")
    per_group = TPD * owners
    width = width_here * n
    most = max(2, 2 * slots // n)
    rows = ceil_to(stations * most, 8)
    whole, tail, left = chunk_plan(taps, components)
    series = stations * components * blocks
    series_rows = ceil_to(series, 8)
    with_data = width_here == LANES
    here = n * most

    waves = jnp.transpose(waves, (0, 2, 1, 3)).reshape(stations * components, slots, taps)
    groups = jnp.transpose(slot_group, (0, 2, 1))
    samples = jnp.transpose(data, (1, 2, 0, 3)).reshape(stations * components, blocks, width_here)
    last_rows = series + EXTRAS if with_data else 8
    message_rows = [ceil_to(k * (components * whole + 1) * rows + last_rows, 16) for k in (1, 1)]
    message_rows += [ceil_to(2 * (components * whole + 1) * rows + last_rows, 16)] * (n // 2 - 1)
    ins = ([samples] if with_data else []) + [waves, groups, slot_local, moveout]
    ins = [pltpu.with_memory_space_constraint(x, pltpu.HBM) for x in ins]
    send = pl.pallas_call(
        functools.partial(
            pack_kernel, (n, stations, slots, components, taps, most, rows), with_data
        ),
        out_shape=[jax.ShapeDtypeStruct((k, LANES), jnp.bfloat16) for k in message_rows],
        in_specs=[pl.BlockSpec(memory_space=pltpu.HBM)] * len(ins),
        scratch_shapes=[pltpu.VMEM(x.shape, x.dtype) for x in ins]
        + [pltpu.SemaphoreType.DMA((len(ins),))],
        compiler_params=pltpu.CompilerParams(vmem_limit_bytes=24 << 20),
        name="pack",
    )(*ins)
    def swap(block, d):
        return lax.ppermute(block, "tmpl", [(i, i ^ d) for i in range(n)])

    own, for_core, *for_chips = send
    from_chips = [swap(block, d) for d, block in zip(chips(n), for_chips)]
    from_core = swap(for_core, 1)
    if from_chips:
        from_chips[0], from_core = lax.optimization_barrier((from_chips[0], from_core))
    received = [own, from_core] + from_chips + [swap(block, 1) for block in from_chips]
    if not with_data:
        samples = lax.all_gather(samples.reshape(series, width_here), "tmpl", axis=1, tiled=True)
    vmem = pl.BlockSpec(memory_space=pltpu.VMEM)
    partial_stacks = pl.pallas_call(
        functools.partial(
            correlate_kernel,
            (n, stations, blocks, components, taps, most, rows, width, per_group),
            with_data,
        ),
        out_shape=[jax.ShapeDtypeStruct((TPD, blocks * NK + LANES), jnp.bfloat16)] * owners,
        in_specs=[vmem] * (0 if with_data else 1) + [pl.BlockSpec(memory_space=pltpu.SMEM)] + [vmem] * n,
        scratch_shapes=[
            pltpu.VMEM((width // LANES, series_rows, LANES), jnp.float32),
            pltpu.VMEM((width // LANES, SHIFTS * series_rows, LANES), jnp.float32),
            pltpu.VMEM((series_rows, ceil_to(width - taps + 1, LANES)), jnp.float32),
            pltpu.VMEM((stations * here, components * (whole + 1) * LANES), jnp.bfloat16),
            pltpu.VMEM((stations * here, components * LANES), jnp.float32),
            pltpu.VMEM((stations * here, LANES), jnp.float32),
            pltpu.VMEM((stations * here, blocks * NK + LANES), jnp.bfloat16),
            pltpu.VMEM((per_group, blocks * NK + LANES), jnp.float32),
        ],
        compiler_params=pltpu.CompilerParams(vmem_limit_bytes=40 << 20),
        name="correlate",
    )(*([] if with_data else [samples]), chan_mask, *received)
    parts = [
        lax.ppermute(part, "stn", [(i, (i + d) % owners) for i in range(owners)]) if d else part
        for d, part in zip(rotations(owners), partial_stacks)
    ]
    return pl.pallas_call(
        functools.partial(finish_kernel, taps, blocks),
        out_shape=jax.ShapeDtypeStruct((blocks, TPD, NK), jnp.float32),
        compiler_params=pltpu.CompilerParams(vmem_limit_bytes=4 << 20),
        name="finish",
    )(*parts)


def solution(mesh):
    in_specs = (
        P(None, "stn", None, "tmpl"),
        P("stn", "tmpl", None, None),
        P("stn", "tmpl", None),
        P("stn", "tmpl"),
        P("stn", "tmpl"),
        P("stn", None),
    )
    out_specs = P(None, ("tmpl", "stn"), None)
    return jax.shard_map(body, mesh=mesh, in_specs=in_specs, out_specs=out_specs, check_vma=False)
```
